32 devices in a mesh: rows: 8 (over z, y), tp: 4 (over x, core).
Axes of the slice: x: 2, y: 2, z: 4, core: 2. Of those that a mesh axis runs over, the one named last changes fastest.
Arguments:
- datapoints: bfloat16 [16384, 1024], P('rows', 'tp'), may hold values from -6 to 6
- lengths: int32 [8, 3], P('rows'), may hold values from 1 to 1024, 2048 in all within a row
- qkv_weight: bfloat16 [3, 1024, 1024], P(None, None, 'tp'), may hold values from -0.1875 to 0.1875
- out_weight: bfloat16 [1024, 1024], P('tp'), may hold values from -3 to 3
- up_weight: bfloat16 [1024, 4096], P(None, 'tp'), may hold values from -0.1875 to 0.1875
- up_bias: float32 [4096], P('tp'), may hold values from -3 to 3
- down_weight: bfloat16 [4096, 1024], P('tp'), may hold values from -0.09375 to 0.09375
- down_bias: float32 [1024], P('tp'), may hold values from -3 to 3
- gain_one: float32 [1024], P('tp'), may hold values from 0.5 to 1.5
- shift_one: float32 [1024], P('tp'), may hold values from -2 to 2
- gain_two: float32 [1024], P('tp'), may hold values from 0.5 to 1.5
- shift_two: float32 [1024], P('tp'), may hold values from -2 to 2
- grad_out: bfloat16 [16384, 1024], P('rows', 'tp'), may hold values from -6 to 6
Outputs:
- output: bfloat16 [16384, 1024], P('rows', 'tp')
- d_input: float32 [16384, 1024], P('rows', 'tp')
- d_qkv: float32 [3, 1024, 1024], P(None, None, 'tp')
- d_out: float32 [1024, 1024], P('tp')
- d_up: float32 [1024, 4096], P(None, 'tp')
- d_up_bias: float32 [4096], P('tp')
- d_down: float32 [4096, 1024], P('tp')
- d_down_bias: float32 [1024], P('tp')
- d_gain_one: float32 [1024], P('tp')
- d_shift_one: float32 [1024], P('tp')
- d_gain_two: float32 [1024], P('tp')
- d_shift_two: float32 [1024], P('tp')
The draws below stay inside these ranges and needn't reach their ends.
Inputs may be any that keep to these rules, and one draw needn't show every extreme that they name: Each row lists 3 dataset lengths that sum to 2048; the largest in each row is 1024.
All inputs are finite; a program needn't handle non-finite values.
Results may differ from the reference program's by a relative error of at most 0.029.
Values may be sent and summed in bfloat16 or wider, within the bound.
No kernel may reach another device: no remote copies, remote signals or barrier semaphores. Data moves between devices by JAX's collectives and lax.ppermute only.
A program may use at most 192 MiB of HBM per device.

```python
import math
import jax
import jax.numpy as jnp
import numpy as np
from jax import lax

D = 1024
HEADS = 8
DH = 128
FF = 4096
TOK_DEV = 2048
DSETS = 3
BLK = 512
POINTS = 16384
N_ROWS = 8


def levels(stream_key, dims, pieces, low, top_value):
    level = 1.0
    for dim, parts in pieces:
        heights = jax.random.uniform(jax.random.fold_in(jax.random.fold_in(stream_key, 6), dim), (parts,), jnp.float32, low / len(pieces), top_value / len(pieces))
        level = level * jnp.repeat(jnp.exp(heights), dims[dim] // parts).reshape((-1,) + (1,) * (len(dims) - 1 - dim))
    return level


def length_profile(count, total, reach, lean):
    portions = [(1 << 20) // math.isqrt(rank ** lean) + 1 for rank in range(2, count + 1)]
    surplus, counts = total - reach - (count - 1), [1] * (count - 1)
    while surplus > 0:
        free = [i for i in range(count - 1) if counts[i] < reach]
        whole, remaining = sum([portions[i] for i in free]), surplus
        for i in free:
            addition = min(reach - counts[i], max(1, remaining * portions[i] // whole), surplus)
            counts[i] = counts[i] + addition
            surplus = surplus - addition
    return np.array([reach] + counts)


def ragged(own_key, count, total, most, skew):
    if count == 2:
        one = jax.random.randint(own_key, (), max(1, total - most), min(most, total - 1) + 1)
        return jnp.stack([one, total - one])
    sizes = jnp.asarray(length_profile(count, total, most, skew), jnp.int32)
    couples = (count - 1) // 2
    giver, sink = sizes[1:1 + 2 * couples:2], sizes[2:2 + 2 * couples:2]
    margin = jnp.minimum(giver - 1, most - sink)
    moved = jax.random.randint(jax.random.fold_in(own_key, 1), (couples,), 0, 1 << 20) % (margin + 1)
    sizes = sizes.at[1:1 + 2 * couples:2].set(giver - moved).at[2:2 + 2 * couples:2].set(sink + moved)
    return sizes[jax.random.permutation(jax.random.fold_in(own_key, 2), count)]


def gaussian(own_key, extent, deviation, limit, split=(), held_as=jnp.bfloat16):
    array = deviation * jax.random.normal(own_key, extent, jnp.float32)
    if split:
        array = array * levels(own_key, extent, split, -0.22, 0.18)
    return jnp.clip(array, -limit, limit).astype(held_as)


def setup_inputs(seed: int = 0) -> dict:
    splits = jax.random.split(jax.random.key(seed), 14)
    datapoints = gaussian(splits[0], (POINTS, D), 1.0, 6.0, ((0, 8), (1, 4)))
    lengths = jax.vmap(lambda own: ragged(own, DSETS, TOK_DEV, TOK_DEV // 2, 2))(jax.random.split(splits[1], N_ROWS)).reshape((N_ROWS, DSETS)).astype(jnp.int32)
    qkv_weight = gaussian(splits[2], (3, D, D), D ** -0.5, 0.1875, ((2, 4),))
    out_weight = gaussian(splits[3], (D, D), (max(D // 256, 1)) ** -0.5, 3.0, ((0, 4),))
    up_weight = gaussian(splits[4], (D, FF), D ** -0.5, 0.1875, ((1, 4),))
    up_bias = gaussian(splits[5], (FF,), 0.5, 3.0, ((0, 4),), jnp.float32)
    down_weight = gaussian(splits[6], (FF, D), FF ** -0.5, 0.09375, ((0, 4),))
    down_bias = gaussian(splits[7], (D,), 0.5, 3.0, ((0, 4),), jnp.float32)
    gain_one = jnp.clip(1.0 + 0.1 * jax.random.normal(splits[8], (D,), jnp.float32), 0.5, 1.5)
    shift_one = gaussian(splits[9], (D,), 0.3, 2.0, ((0, 4),), jnp.float32)
    gain_two = jnp.clip(1.0 + 0.1 * jax.random.normal(splits[10], (D,), jnp.float32), 0.5, 1.5)
    shift_two = gaussian(splits[11], (D,), 0.3, 2.0, ((0, 4),), jnp.float32)
    grad_out = gaussian(splits[12], (POINTS, D), 1.0, 6.0, ((0, 8), (1, 4)))
    return {"datapoints": datapoints, "lengths": lengths, "qkv_weight": qkv_weight, "out_weight": out_weight, "up_weight": up_weight, "up_bias": up_bias, "down_weight": down_weight, "down_bias": down_bias, "gain_one": gain_one, "shift_one": shift_one, "gain_two": gain_two, "shift_two": shift_two, "grad_out": grad_out}


EPS_NORM = 1e-05
NEG_FILL = -1e+30
HIGHEST = lax.Precision.HIGHEST

@jax.custom_vjp
def low(v):
    return lax.optimization_barrier(v.astype(jnp.bfloat16)).astype(jnp.float32)

@jax.custom_vjp
def low_back(v):
    return v

def low_keep(v):
    return (low(v), None)

def low_pass(kept, grad):
    return (grad,)

def back_keep(v):
    return (v, None)

def back_low(kept, grad):
    return (low(grad),)
low.defvjp(low_keep, low_pass)
low_back.defvjp(back_keep, back_low)

def dataset_ids(lengths, count):
    ends = jnp.cumsum(lengths.reshape(-1).astype(jnp.int32))
    place = lax.broadcasted_iota(jnp.int32, (count, 1), 0)
    return lax.optimization_barrier(jnp.sum((place >= ends[None, :]).astype(jnp.int32), axis=1))

def layer_norm(values, gain, shift):
    mean_row = lax.optimization_barrier(jnp.mean(values, axis=-1, keepdims=True))
    centered = values - mean_row
    spread = lax.optimization_barrier(jnp.mean(centered * centered, axis=-1, keepdims=True))
    return centered * lax.rsqrt(spread + EPS_NORM) * gain + shift

def matmul(left, right):
    return jnp.dot(left, right, precision=HIGHEST, preferred_element_type=jnp.float32)

def layer(inputs, lengths, params):
    qkv_w, out_w, up_w, up_b, down_w, down_b, gain_a, shift_a, gain_b, shift_b = params
    dataset_of = dataset_ids(lengths, TOK_DEV)
    normed_acts = low(layer_norm(inputs, gain_a, shift_a))
    queries = low(low_back(matmul(normed_acts, qkv_w[0]) * DH ** (-0.5))).reshape(TOK_DEV, HEADS, DH)
    key_rows = low(low_back(matmul(normed_acts, qkv_w[1]))).reshape(TOK_DEV, HEADS, DH)
    value_rows = low(low_back(matmul(normed_acts, qkv_w[2]))).reshape(TOK_DEV, HEADS, DH)
    n_blocks = TOK_DEV // BLK

    def attend_one(block_item):
        q_block, s_block = block_item
        scores = low_back(jnp.einsum('qhd,khd->hqk', q_block, key_rows, precision=HIGHEST))
        allowed = (s_block[:, None] == dataset_of[None, :])[None]
        softmaxed = jax.nn.softmax(jnp.where(allowed, scores, NEG_FILL), axis=-1)
        return jnp.einsum('hqk,khd->qhd', low(softmaxed), value_rows, precision=HIGHEST)
    attn_mixed = lax.map(jax.checkpoint(attend_one), (queries.reshape(n_blocks, BLK, HEADS, DH), dataset_of.reshape(n_blocks, BLK)))
    attn_mixed = low(low_back(attn_mixed.reshape(TOK_DEV, D)))
    residual = inputs + low_back(matmul(attn_mixed, out_w))
    mlp_input = low(layer_norm(residual, gain_b, shift_b))
    pre_act = low_back(matmul(mlp_input, up_w) + up_b)
    hidden = low(jax.nn.gelu(pre_act))
    return residual + matmul(hidden, down_w) + down_b

def reference(datapoints, lengths, qkv_weight, out_weight, up_weight, up_bias, down_weight, down_bias, gain_one, shift_one, gain_two, shift_two, grad_out):
    params = tuple((weight_arr.astype(jnp.float32) for weight_arr in (qkv_weight, out_weight, up_weight, up_bias, down_weight, down_bias, gain_one, shift_one, gain_two, shift_two)))
    grouped = datapoints.astype(jnp.float32).reshape(N_ROWS, TOK_DEV, D)
    step_fn = jax.checkpoint(layer)

    def forward(grouped_in, params_in):
        return lax.map(lambda pair: step_fn(pair[0], pair[1], params_in), (grouped_in, lengths))
    result, pull_back = jax.vjp(forward, grouped, params)
    d_grouped, d_params = pull_back(grad_out.astype(jnp.float32).reshape(N_ROWS, TOK_DEV, D))
    return (result.reshape(N_ROWS * TOK_DEV, D).astype(jnp.bfloat16), d_grouped.reshape(N_ROWS * TOK_DEV, D), d_params[0], d_params[1], d_params[2], d_params[3], d_params[4], d_params[5], d_params[6], d_params[7], d_params[8], d_params[9])
```

```python
import functools

import jax
import jax.numpy as jnp
from jax import lax
from jax.experimental import pallas as pl
from jax.experimental.pallas import tpu as pltpu
from jax.sharding import PartitionSpec as P

DH = 128
TILE = 256
EPS_NORM = 1e-05
NEG_FILL = -1e30
F32 = jnp.float32
BF16 = jnp.bfloat16
VMEM_LIMIT = 48 * 1024 * 1024
GELU_C = 0.7978845608028654


def dot_nn(a, b):
    return jnp.dot(a, b, preferred_element_type=F32)


def dot_nt(a, b):
    return lax.dot_general(a, b, (((1,), (1,)), ((), ())), preferred_element_type=F32)


def dot_tn(a, b):
    return lax.dot_general(a, b, (((0,), (0,)), ((), ())), preferred_element_type=F32)


def call(body, grid, in_specs, out_specs, out_shape, scalars, operands, scratch=(), flops=0):
    bytes_moved = sum(o.size * o.dtype.itemsize for o in operands)
    bytes_moved += sum(
        o.size * jnp.dtype(o.dtype).itemsize for o in jax.tree_util.tree_leaves(out_shape)
    )
    return pl.pallas_call(
        body,
        grid_spec=pltpu.PrefetchScalarGridSpec(
            num_scalar_prefetch=1,
            grid=grid,
            in_specs=in_specs,
            out_specs=out_specs,
            scratch_shapes=list(scratch),
        ),
        out_shape=out_shape,
        compiler_params=pltpu.CompilerParams(
            vmem_limit_bytes=VMEM_LIMIT,
            dimension_semantics=("arbitrary",) * len(grid),
        ),
        cost_estimate=pl.CostEstimate(
            flops=int(flops), bytes_accessed=int(bytes_moved), transcendentals=0
        ),
    )(scalars, *operands)


def full(shape):
    zeros = (0,) * len(shape)
    return pl.BlockSpec(shape, lambda *_: zeros, pipeline_mode=pl.Buffered(1))


def shape_of(shape, dtype):
    return jax.ShapeDtypeStruct(shape, dtype)


def ln_qkv_body(sc, x0, x1, x2, x3, gains, weight, qkv, acts, stats):
    t = sc[0]
    pieces = [x[...].astype(F32) for x in (x0, x1, x2, x3)]
    width = pieces[0].shape[1]
    count = width * len(pieces)
    mean = sum(jnp.sum(x, axis=1, keepdims=True) for x in pieces) / count
    centered = [x - mean for x in pieces]
    var = sum(jnp.sum(c * c, axis=1, keepdims=True) for c in centered) / count
    rstd = lax.rsqrt(var + EPS_NORM)
    total = [0.0, 0.0, 0.0]
    for k, c in enumerate(centered):
        j = jnp.bitwise_xor(t, k)
        part = (c * rstd * gains[k, 0:1, :] + gains[k, 1:2, :]).astype(BF16)
        acts[:, pl.ds(pl.multiple_of(j * width, width), width)] = part
        for s in range(3):
            total[s] = total[s] + dot_nn(part, weight[s, j])
    qkv[0] = (total[0] * (DH ** (-0.5))).astype(BF16)
    qkv[1] = total[1].astype(BF16)
    qkv[2] = total[2].astype(BF16)
    stats[:, 0:1] = mean
    stats[:, 1:2] = rstd


def ln_qkv(scalars, pieces, gains, weight4):
    rows, width = pieces[0].shape
    n = len(pieces)
    tiles = rows // TILE
    return call(
        ln_qkv_body,
        (tiles,),
        [pl.BlockSpec((TILE, width), lambda i, sc: (i, 0))] * n
        + [full(gains.shape), full(weight4.shape)],
        [
            pl.BlockSpec((3, TILE, width), lambda i, sc: (0, i, 0)),
            pl.BlockSpec((TILE, n * width), lambda i, sc: (i, 0)),
            pl.BlockSpec((TILE, 2), lambda i, sc: (i, 0)),
        ],
        [
            shape_of((3, rows, width), BF16),
            shape_of((rows, n * width), BF16),
            shape_of((rows, 2), F32),
        ],
        scalars,
        [*pieces, gains, weight4],
        flops=2 * rows * n * width * 3 * width,
    )


def attend_body(masked, sc, q, k, v, o, lse):
    i = pl.program_id(1)
    scores = dot_nt(q[0], k[0])
    rows, cols = scores.shape
    if masked:
        q_side = (i * rows + lax.broadcasted_iota(jnp.int32, (rows, 1), 0)) < sc[1]
        k_side = lax.broadcasted_iota(jnp.int32, (1, cols), 1) < sc[1]
        scores = jnp.where(jnp.logical_xor(q_side, k_side), NEG_FILL, scores)
    top = jnp.max(scores, axis=1, keepdims=True)
    weights = jnp.exp(scores - top)
    total = jnp.sum(weights, axis=1, keepdims=True)
    mixed = dot_nn(weights.astype(BF16), v[0])
    o[...] = (mixed / total).astype(BF16)
    stat = jnp.broadcast_to(top + jnp.log(total), (rows, DH))
    lse[0] = jnp.transpose(stat)[0:1, :]


def attend(scalars, qkv, masked):
    _, rows, width = qkv.shape
    heads = width // DH
    tiles = rows // TILE
    return call(
        functools.partial(attend_body, masked),
        (heads, tiles),
        [
            pl.BlockSpec((1, TILE, DH), lambda h, i, sc: (0, i, h)),
            pl.BlockSpec((1, rows, DH), lambda h, i, sc: (1, 0, h)),
            pl.BlockSpec((1, rows, DH), lambda h, i, sc: (2, 0, h)),
        ],
        [
            pl.BlockSpec((TILE, DH), lambda h, i, sc: (i, h)),
            pl.BlockSpec((1, 1, TILE), lambda h, i, sc: (h, 0, i)),
        ],
        [shape_of((rows, width), BF16), shape_of((heads, 1, rows), F32)],
        scalars,
        [qkv, qkv, qkv],
        flops=4 * rows * rows * width * 2,
    )


def feed_body(
    sc, x0, x1, x2, x3, o0, o1, o2, o3, d0, d1, d2, d3, w0, w1, w2, w3,
    gains, up, up_t, down_t, bias,
    y_out, b_out, g_out, du_out, dy_out, send, keep, bias_grad, y_acc,
):
    t = sc[0]
    i = pl.program_id(0)
    xs, os, ds, ws = (x0, x1, x2, x3), (o0, o1, o2, o3), (d0, d1, d2, d3), (w0, w1, w2, w3)
    width = x0.shape[1]
    n = len(xs)
    count = n * width

    def block(k):
        j = jnp.bitwise_xor(t, k)
        return pl.ds(pl.multiple_of(j * width, width), width)

    y_acc[...] = sum(dot_nn(o[...], w[...]) for o, w in zip(os, ws))
    for k in range(n):
        y_acc[:, block(k)] += xs[k][...].astype(F32)
        dy_out[:, block(k)] = ds[k][...]
    y = y_acc[...]
    y_out[...] = y
    mean = jnp.sum(y, axis=1, keepdims=True) / count
    centered = y - mean
    rstd = lax.rsqrt(jnp.sum(centered * centered, axis=1, keepdims=True) / count + EPS_NORM)
    b = (centered * rstd * gains[2:3, :] + gains[3:4, :]).astype(BF16)
    b_out[...] = b
    dy = dy_out[...]
    hidden = up.shape[1]
    step = 256
    total = None
    for f in range(0, hidden, step):
        cols = slice(f, f + step)
        u = dot_nn(b, up[:, cols]) + bias[:, cols]
        dh = dot_nn(dy, down_t[:, cols])
        cubic = u * u
        th = jnp.tanh(GELU_C * u * (1.0 + 0.044715 * cubic))
        half = 0.5 * (1.0 + th)
        g_out[:, cols] = (u * half).astype(BF16)
        slope = half + (0.5 * GELU_C) * u * (1.0 - th * th) * (1.0 + 0.134145 * cubic)
        du = (dh * slope).astype(BF16)
        du_out[:, cols] = du
        sums = jnp.sum(du.astype(F32), axis=0, keepdims=True)

        @pl.when(i == 0)
        def _():
            bias_grad[:, cols] = sums

        @pl.when(i > 0)
        def _():
            bias_grad[:, cols] += sums

        part = dot_nn(du, up_t[cols, :])
        total = part if total is None else total + part
    low = total.astype(BF16)

    @pl.when(i < 2)
    def _():
        send[0] = low

    @pl.when(i >= 2)
    def _():
        keep[0] = low


def relative(i):
    return jnp.where(i < 2, 2 * i + 1, 2 * i - 4)


def feed(scalars, xs, os, dys, ows, gains, up, up_t, down_t, bias):
    rows, width = xs[0].shape
    n = len(xs)
    count = n * width
    hidden = up.shape[1]
    tiles = rows // TILE

    def tile(i, sc):
        return (jnp.bitwise_xor(sc[0], relative(i)), 0)

    return call(
        feed_body,
        (tiles,),
        [pl.BlockSpec((TILE, width), tile)] * (3 * n)
        + [full(w.shape) for w in ows]
        + [full(gains.shape), full(up.shape), full(up_t.shape), full(down_t.shape), full(bias.shape)],
        [
            pl.BlockSpec((TILE, count), tile),
            pl.BlockSpec((TILE, count), tile),
            pl.BlockSpec((TILE, hidden), tile),
            pl.BlockSpec((TILE, hidden), tile),
            pl.BlockSpec((TILE, count), tile),
            pl.BlockSpec((1, TILE, count), lambda i, sc: (jnp.minimum(i, 1), 0, 0)),
            pl.BlockSpec((1, TILE, count), lambda i, sc: (jnp.maximum(i - 2, 0), 0, 0)),
            pl.BlockSpec((1, hidden), lambda i, sc: (0, 0)),
        ],
        [
            shape_of((rows, count), F32),
            shape_of((rows, count), BF16),
            shape_of((rows, hidden), BF16),
            shape_of((rows, hidden), BF16),
            shape_of((rows, count), BF16),
            shape_of((2, TILE, count), BF16),
            shape_of((2, TILE, count), BF16),
            shape_of((1, hidden), F32),
        ],
        scalars,
        [*xs, *os, *dys, *ows, gains, up, up_t, down_t, bias],
        scratch=[pltpu.VMEM((TILE, count), F32)],
        flops=2 * rows * count * (count + 3 * hidden),
    )


def norm_back_body(sc, p0, p1, p2, y, dy, gains, dz, sums):
    db = p0[0].astype(F32) + p1[0].astype(F32) + p2[...].astype(F32)
    yv = y[...]
    count = yv.shape[1]
    mean = jnp.sum(yv, axis=1, keepdims=True) / count
    centered = yv - mean
    rstd = lax.rsqrt(jnp.sum(centered * centered, axis=1, keepdims=True) / count + EPS_NORM)
    nhat = centered * rstd
    n = db * gains[2:3, :]
    first = jnp.sum(n, axis=1, keepdims=True) / count
    second = jnp.sum(n * nhat, axis=1, keepdims=True) / count
    dz[...] = (dy[...].astype(F32) + rstd * (n - first - nhat * second)).astype(BF16)
    sums[0:1, :] = jnp.sum(db * nhat, axis=0, keepdims=True)
    sums[1:2, :] = jnp.sum(db, axis=0, keepdims=True)


def norm_back(scalars, keep, got_core, got_x, y, dy, gains):
    rows, count = got_x.shape
    return call(
        norm_back_body,
        (1,),
        [
            pl.BlockSpec((1, rows, count), lambda i, sc: (0, 0, 0)),
            pl.BlockSpec((1, rows, count), lambda i, sc: (0, 0, 0)),
            pl.BlockSpec((rows, count), lambda i, sc: (0, 0)),
            pl.BlockSpec((rows, count), lambda i, sc: (sc[0], 0)),
            pl.BlockSpec((rows, count), lambda i, sc: (sc[0], 0)),
            full(gains.shape),
        ],
        [
            pl.BlockSpec((rows, count), lambda i, sc: (0, 0)),
            pl.BlockSpec((2, count), lambda i, sc: (0, 0)),
        ],
        [shape_of((rows, count), BF16), shape_of((2, count), F32)],
        scalars,
        [keep, got_core, got_x, y, dy, gains],
    )


def attend_back_body(masked, sc, z0, z1, z2, z3, out_t, q, k, v, lse, dq, dk, dv, dz_out, dk_acc, dv_acc):
    i = pl.program_id(0)
    t = sc[0]
    for j, z in enumerate((z0, z1, z2, z3)):

        @pl.when(i == j)
        def _(z=z):
            dz_out[...] = z[...]

    d_mixed = dot_nn(dz_out[...], out_t[...]).astype(BF16)
    rows = d_mixed.shape[0]
    keys = k.shape[1]
    for h in range(d_mixed.shape[1] // DH):
        cols = slice(h * DH, (h + 1) * DH)
        q_h, k_h, v_h, do_h = q[0, :, cols], k[0, :, cols], v[0, :, cols], d_mixed[:, cols]
        scores = dot_nt(k_h, q_h)
        if masked:
            base = jnp.bitwise_xor(t, i) * rows
            q_side = (base + lax.broadcasted_iota(jnp.int32, (1, rows), 1)) < sc[1]
            k_side = lax.broadcasted_iota(jnp.int32, (keys, 1), 0) < sc[1]
            scores = jnp.where(jnp.logical_xor(q_side, k_side), NEG_FILL, scores)
        p = jnp.exp(scores - lse[h])
        d_p = dot_nt(v_h, do_h)
        prod = p * d_p
        delta = jnp.sum(prod, axis=0, keepdims=True)
        d_s = (prod - p * delta).astype(BF16)
        d_v = dot_nn(p.astype(BF16), do_h)
        d_k = dot_nn(d_s, q_h)

        @pl.when(i == 0)
        def _():
            dv_acc[:, cols] = d_v
            dk_acc[:, cols] = d_k

        @pl.when(i > 0)
        def _():
            dv_acc[:, cols] += d_v
            dk_acc[:, cols] += d_k

        dq[:, cols] = dot_tn(d_s, k_h).astype(BF16)

    @pl.when(i == pl.num_programs(0) - 1)
    def _():
        dk[...] = dk_acc[...].astype(BF16)
        dv[...] = dv_acc[...].astype(BF16)


def attend_back(scalars, dzs, out_t, qkv, lse, masked):
    _, rows, width = qkv.shape
    heads = width // DH
    count = out_t.shape[0]
    tiles = rows // TILE

    def tile(i, sc):
        return (jnp.bitwise_xor(sc[0], i), 0)

    return call(
        functools.partial(attend_back_body, masked),
        (tiles,),
        [full(dz.shape) for dz in dzs]
        + [
            full(out_t.shape),
            pl.BlockSpec((1, TILE, width), lambda i, sc: (0, jnp.bitwise_xor(sc[0], i), 0)),
            pl.BlockSpec((1, rows, width), lambda i, sc: (1, 0, 0)),
            pl.BlockSpec((1, rows, width), lambda i, sc: (2, 0, 0)),
            pl.BlockSpec((heads, 1, TILE), lambda i, sc: (0, 0, jnp.bitwise_xor(sc[0], i))),
        ],
        [
            pl.BlockSpec((TILE, width), tile),
            pl.BlockSpec((rows, width), lambda i, sc: (0, 0)),
            pl.BlockSpec((rows, width), lambda i, sc: (0, 0)),
            pl.BlockSpec((TILE, count), tile),
        ],
        [
            shape_of((rows, width), BF16),
            shape_of((rows, width), BF16),
            shape_of((rows, width), BF16),
            shape_of((rows, count), BF16),
        ],
        scalars,
        [*dzs, out_t, qkv, qkv, qkv, lse],
        scratch=[pltpu.VMEM((rows, width), F32), pltpu.VMEM((rows, width), F32)],
        flops=2 * rows * count * width + 20 * rows * rows * width,
    )


def spread_body(scale, n_in, sc, *refs):
    lefts, rights, send, keep = refs[:n_in], refs[n_in : 2 * n_in], refs[-2], refs[-1]
    total = None
    for left, right in zip(lefts, rights):
        part = dot_nn(left[...], right[...])
        if total is None:
            total = part * scale if scale != 1.0 else part
        else:
            total = total + part
    low = total.astype(BF16)
    i = pl.program_id(0)

    @pl.when(i < 2)
    def _():
        send[0] = low

    @pl.when(i >= 2)
    def _():
        keep[0] = low


def spread(scalars, lefts, rights, scale=1.0):
    rows = lefts[0].shape[0]
    count = rights[0].shape[1]
    width = count // 4

    def cols(i, sc):
        return (0, jnp.bitwise_xor(sc[0], relative(i)))

    return call(
        functools.partial(spread_body, scale, len(lefts)),
        (4,),
        [full(a.shape) for a in lefts]
        + [pl.BlockSpec((b.shape[0], width), cols) for b in rights],
        [
            pl.BlockSpec((1, rows, width), lambda i, sc: (jnp.minimum(i, 1), 0, 0)),
            pl.BlockSpec((1, rows, width), lambda i, sc: (jnp.maximum(i - 2, 0), 0, 0)),
        ],
        [shape_of((2, rows, width), BF16), shape_of((2, rows, width), BF16)],
        scalars,
        [*lefts, *rights],
        flops=sum(2 * a.shape[0] * a.shape[1] * b.shape[1] for a, b in zip(lefts, rights)),
    )


def weight_grad_body(bit, n_cols, sc, a0, a1, *refs):
    rights0, rights1 = refs[:n_cols], refs[n_cols : 2 * n_cols]
    send, keep = refs[-2], refs[-1]
    i = pl.program_id(0)
    at = 0
    for r0, r1 in zip(rights0, rights1):
        width = r0.shape[1]
        low = (dot_tn(a0[...], r0[...]) + dot_tn(a1[...], r1[...])).astype(BF16)

        @pl.when(i == 0)
        def _():
            send[:, at : at + width] = low

        @pl.when(i == 1)
        def _():
            keep[:, at : at + width] = low

        at += width


def weight_grad(scalars, lefts, rights0, rights1, bit):
    rows, m = lefts[0].shape
    count = sum(b.shape[1] for b in rights0)

    def half(i, sc):
        mine = jnp.bitwise_and(jnp.right_shift(sc[2], bit), 1)
        return (0, jnp.where(i == 0, 1 - mine, mine))

    return call(
        functools.partial(weight_grad_body, bit, len(rights0)),
        (2,),
        [pl.BlockSpec((rows, m // 2), half)] * 2 + [full(b.shape) for b in (*rights0, *rights1)],
        [full((m // 2, count))] * 2,
        [shape_of((m // 2, count), BF16)] * 2,
        scalars,
        [*lefts, *rights0, *rights1],
        flops=4 * rows * m * count,
    )


def place_body(sc, first, second, out):
    i = pl.program_id(0)
    half = pl.num_programs(0) // 2

    @pl.when(i < half)
    def _():
        out[...] = first[...].astype(F32)

    @pl.when(i >= half)
    def _():
        out[...] = second[...].astype(F32)


def place(index, first, second, blocks):
    m, count = first.shape[0] * 2, first.shape[1]
    rows = m // blocks
    half = blocks // 2
    return call(
        place_body,
        (blocks,),
        [
            pl.BlockSpec((rows, count), lambda i, sc: (jnp.minimum(i, half - 1), 0)),
            pl.BlockSpec((rows, count), lambda i, sc: (jnp.maximum(i - half, 0), 0)),
        ],
        pl.BlockSpec((rows, count), lambda i, sc: (jnp.bitwise_xor(sc[0], i), 0)),
        shape_of((m, count), F32),
        index,
        [first, second],
    )


class RowSum:
    def __init__(self, r, n_rows, send, keep, bits):
        self.r, self.n_rows = r, n_rows
        self.bits = bits
        self.rest = [b for b in range(n_rows.bit_length() - 1) if b not in bits]
        self.send, self.keep = send, keep

    def flip(self, value, bit):
        return lax.ppermute(
            value, "rows", [(i, i ^ (1 << bit)) for i in range(self.n_rows)]
        )

    def bit(self, b):
        return jnp.bitwise_and(jnp.right_shift(self.r, b), 1)

    def scatter(self):
        send, keep = self.send, self.keep
        for at, b in enumerate(self.bits):
            got = self.flip(send, b)
            if at + 1 < len(self.bits):
                nxt = self.bit(self.bits[at + 1])
                half = keep.shape[0] // 2
                other, mine = (1 - nxt) * half, nxt * half

                def part(start):
                    a = lax.dynamic_slice_in_dim(keep, start, half, 0).astype(F32)
                    c = lax.dynamic_slice_in_dim(got, start, half, 0).astype(F32)
                    return a + c

                send, keep = part(other).astype(BF16), part(mine)
            else:
                total = keep.astype(F32) + got.astype(F32)
        for b in self.rest:
            low = total.astype(BF16)
            total = low.astype(F32) + self.flip(low, b).astype(F32)
        self.own = total.astype(BF16)
        return self

    def gather(self):
        buf = self.own
        index = 0
        for b in reversed(self.bits):
            got = self.flip(buf, b)
            last, buf = buf, jnp.concatenate([buf, got], 0) if b != self.bits[0] else None
        for b in self.bits:
            index = index * 2 + self.bit(b)
        blocks = 1 << len(self.bits)
        return place(jnp.stack([index, index]).astype(jnp.int32), last, got, blocks)


def local(
    n_tp, n_rows,
    datapoints, lengths, qkv_weight, out_weight, up_weight, up_bias, down_weight, down_bias,
    gain_one, shift_one, gain_two, shift_two, grad_out,
):
    tok, width = datapoints.shape
    count = n_tp * width
    half = tok // 2
    q_scale = DH ** (-0.5)
    t, r = lax.axis_index("tp"), lax.axis_index("rows")

    def core_flip(v):
        return lax.ppermute(v, "tp", [(i, i ^ 1) for i in range(n_tp)])

    def x_flip(v):
        return lax.ppermute(v, "tp", [(i, i ^ 2) for i in range(n_tp)])

    def gather(own):
        across = x_flip(own)
        return [own, core_flip(own), across, core_flip(across)]

    def row_flip(v, b):
        return lax.ppermute(v, "rows", [(i, i ^ (1 << b)) for i in range(n_rows)])

    lens = lengths.reshape(-1)
    sets = lens.shape[0]
    big = jnp.argmax(lens)
    start = jnp.sum(jnp.where(jnp.arange(sets) < big, lens, 0))
    border = lens[lax.rem(big + 1, sets)]
    scalars = jnp.stack([t, border, r]).astype(jnp.int32)

    def halves(v):
        twice = jnp.concatenate([v, v[:half]], 0)
        return [
            lax.dynamic_slice_in_dim(v, start, half, 0),
            lax.dynamic_slice_in_dim(twice, start + half, half, 0),
        ]

    def unroll(first, second):
        thrice = jnp.concatenate([second, first, second], 0)
        return lax.dynamic_slice_in_dim(thrice, half - start, tok, 0)

    x_own, dy_own = halves(datapoints), halves(grad_out)
    vectors = jnp.stack([gain_one, shift_one, gain_two, shift_two])
    gains_rel = jnp.stack(gather(vectors))
    order = jnp.bitwise_xor(t, jnp.arange(n_tp))
    gains = jnp.transpose(gains_rel[order], (1, 0, 2)).reshape(4, count)
    xs = [gather(x) for x in x_own]
    ows = gather(out_weight)
    dys = [gather(d) for d in dy_own]

    weight4 = qkv_weight.reshape(3, n_tp, width, width)
    qkv_t = jnp.transpose(qkv_weight, (0, 2, 1))
    out_t = out_weight.T
    up_t = up_weight.T
    down_t = down_weight.T
    bias = up_bias.reshape(1, -1)

    qkv, acts, stats, mixed, lse = [], [], [], [], []
    for h in range(2):
        p, a, s = ln_qkv(scalars, xs[h], gains_rel, weight4)
        o, l = attend(scalars, p, h == 1)
        qkv.append(p)
        acts.append(a)
        stats.append(s)
        mixed.append(o)
        lse.append(l)
    mixed_all = [gather(o) for o in mixed]

    y, b, g, du, dy, d_up_bias, dz_own, two_sums = [], [], [], [], [], 0.0, [], 0.0
    for h in range(2):
        yh, bh, gh, duh, dyh, send, keep, bias_grad = feed(
            scalars, xs[h], mixed_all[h], dys[h], ows, gains, up_weight, up_t, down_t, bias
        )
        got = core_flip(send)
        got_x = x_flip((keep[1].astype(F32) + got[1].astype(F32)).astype(BF16))
        dz, sums = norm_back(scalars, keep, got, got_x, yh, dyh, gains)
        y.append(yh)
        b.append(bh)
        g.append(gh)
        du.append(duh)
        dy.append(dyh)
        dz_own.append(dz)
        d_up_bias = d_up_bias + bias_grad
        two_sums = two_sums + sums
    dzs = [gather(dz) for dz in dz_own]

    d_down = RowSum(r, n_rows, *weight_grad(scalars, g, [dy[0]], [dy[1]], 0), [0, 1, 2])
    d_up = RowSum(r, n_rows, *weight_grad(scalars, b, [du[0]], [du[1]], 1), [1, 0, 2])
    d_down.scatter()
    d_up.scatter()

    outs = []
    for h in range(2):
        send, keep = spread(scalars, [g[h]], [down_weight])
        got = core_flip(send)
        got_x = x_flip((keep[1].astype(F32) + got[1].astype(F32)).astype(BF16))
        y_mine = lax.dynamic_slice_in_dim(y[h], t * width, width, 1)
        total = keep[0].astype(F32) + got[0].astype(F32) + got_x.astype(F32)
        outs.append((y_mine + total + down_bias).astype(BF16))
    output = unroll(*outs)

    d_parts, dz_nat = [], []
    d_inputs, one_gain, one_shift = [], 0.0, 0.0
    for h in range(2):
        dq, dk, dv, dzn = attend_back(scalars, dzs[h], out_t, qkv[h], lse[h], h == 1)
        d_parts.append([dq, dk, dv])
        dz_nat.append(dzn)

    d_out = RowSum(
        r, n_rows, *weight_grad(scalars, mixed, [dz_nat[0]], [dz_nat[1]], 1), [1, 0, 2]
    )
    d_qkv = RowSum(r, n_rows, *weight_grad(scalars, acts, d_parts[0], d_parts[1], 0), [0, 1, 2])
    d_out.scatter()
    d_qkv.scatter()

    for h in range(2):
        send, keep = spread(scalars, d_parts[h], [qkv_t[0], qkv_t[1], qkv_t[2]], q_scale)
        got = core_flip(send)
        got_x = x_flip((keep[1].astype(F32) + got[1].astype(F32)).astype(BF16))
        da = keep[0].astype(F32) + got[0].astype(F32) + got_x.astype(F32)
        mean, rstd = stats[h][:, 0:1], stats[h][:, 1:2]
        nhat = (x_own[h].astype(F32) - mean) * rstd
        one_gain = one_gain + jnp.sum(da * nhat, axis=0)
        one_shift = one_shift + jnp.sum(da, axis=0)
        n = da * gain_one
        moments = jnp.stack([jnp.sum(n, axis=1), jnp.sum(n * nhat, axis=1)])
        moments = moments + core_flip(moments)
        moments = moments + x_flip(moments)
        first, second = moments[0][:, None] / count, moments[1][:, None] / count
        dz_mine = lax.dynamic_slice_in_dim(dz_nat[h], t * width, width, 1).astype(F32)
        d_inputs.append(dz_mine + rstd * (n - first - nhat * second))
    d_input = unroll(*d_inputs)

    d_down_bias = jnp.sum(grad_out.astype(F32), axis=0)
    two_sums = two_sums + core_flip(two_sums)
    two_sums = two_sums + x_flip(two_sums)
    two_mine = lax.dynamic_slice_in_dim(two_sums, t * width, width, 1)
    small = jnp.concatenate(
        [d_up_bias.reshape(-1), d_down_bias, one_gain, one_shift, two_mine[0], two_mine[1]]
    ).reshape(-1, 128)
    for bit in range(n_rows.bit_length() - 1):
        small = small + row_flip(small, bit)
    small = small.reshape(-1)
    hidden = up_bias.shape[0]
    d_up_bias = small[:hidden]
    d_down_bias, d_gain_one, d_shift_one, d_gain_two, d_shift_two = small[hidden:].reshape(5, width)

    d_qkv = jnp.transpose(d_qkv.gather().reshape(count, 3, width), (1, 0, 2))
    d_qkv = d_qkv * jnp.array([q_scale, 1.0, 1.0], F32)[:, None, None]
    return (
        output, d_input, d_qkv, d_out.gather(), d_up.gather(), d_up_bias, d_down.gather(),
        d_down_bias, d_gain_one, d_shift_one, d_gain_two, d_shift_two,
    )


def solution(mesh):
    grid = P("rows", "tp")
    placed = (
        grid, P("rows", None), P(None, None, "tp"), P("tp", None), P(None, "tp"), P("tp"),
        P("tp", None), P("tp"), P("tp"), P("tp"), P("tp"), P("tp"), grid,
    )
    return jax.shard_map(
        functools.partial(local, mesh.shape["tp"], mesh.shape["rows"]),
        mesh=mesh,
        in_specs=placed,
        out_specs=(
            grid, grid, P(None, None, "tp"), P("tp", None), P(None, "tp"), P("tp"),
            P("tp", None), P("tp"), P("tp"), P("tp"), P("tp"), P("tp"),
        ),
        check_vma=False,
    )
```

```python
import functools

import jax
import jax.numpy as jnp
from jax import lax
from jax.experimental import pallas as pl
from jax.experimental.pallas import tpu as pltpu
from jax.sharding import PartitionSpec as P

DH = 128
TILE = 256
EPS_NORM = 1e-05
NEG_FILL = -1e30
F32 = jnp.float32
BF16 = jnp.bfloat16
MIB = 1024 * 1024
COST = 1.0
GELU_C = 0.7978845608028654


def dot_nn(a, b):
    return jnp.dot(a, b, preferred_element_type=F32)


def dot_nt(a, b):
    return lax.dot_general(a, b, (((1,), (1,)), ((), ())), preferred_element_type=F32)


def dot_tn(a, b):
    return lax.dot_general(a, b, (((0,), (0,)), ((), ())), preferred_element_type=F32)


def call(body, grid, in_specs, out_specs, out_shape, scalars, operands, scratch=(), flops=0, vmem=24, hbm=()):
    bytes_moved = sum(o.size * o.dtype.itemsize for o in operands)
    bytes_moved += sum(
        o.size * jnp.dtype(o.dtype).itemsize for o in jax.tree_util.tree_leaves(out_shape)
    )
    operands = [
        pltpu.with_memory_space_constraint(o, pltpu.HBM) if i in hbm else o
        for i, o in enumerate(operands)
    ]
    return pl.pallas_call(
        body,
        grid_spec=pltpu.PrefetchScalarGridSpec(
            num_scalar_prefetch=1,
            grid=grid,
            in_specs=in_specs,
            out_specs=out_specs,
            scratch_shapes=list(scratch),
        ),
        out_shape=out_shape,
        compiler_params=pltpu.CompilerParams(
            vmem_limit_bytes=vmem * MIB,
            dimension_semantics=("arbitrary",) * len(grid),
        ),
        cost_estimate=pl.CostEstimate(
            flops=int(flops * COST), bytes_accessed=int(bytes_moved * COST), transcendentals=0
        ),
    )(scalars, *operands)


def full(shape):
    zeros = (0,) * len(shape)
    return pl.BlockSpec(shape, lambda *_: zeros, pipeline_mode=pl.Buffered(1))


def shape_of(shape, dtype):
    return jax.ShapeDtypeStruct(shape, dtype)


def far_first(i, n, sc):
    c = jnp.bitwise_and(sc[0], 1)
    return jnp.where(i < n // 2, (1 - c) * (n // 2) + i, c * (n // 2) + i - n // 2)


def first_body(
    masked, tile, sc, x0, x1, x2, x3, dy_other, dy_mine, gains, weight,
    qkv, acts, stats, o, lse, other, mine, q_all, k_all, v_all,
):
    t = sc[0]
    i = pl.program_id(0)
    n = pl.num_programs(0) // 2

    @pl.when(i == 0)
    def _():
        rows = dy_mine.shape[0]
        other[rows:, :] = dy_other[...]
        mine[rows:, :] = dy_mine[...]

    @pl.when(i < n)
    def _():
        pieces = [x[...].astype(F32) for x in (x0, x1, x2, x3)]
        width = pieces[0].shape[1]
        count = width * len(pieces)
        mean = sum(jnp.sum(x, axis=1, keepdims=True) for x in pieces) / count
        centered = [x - mean for x in pieces]
        var = sum(jnp.sum(c * c, axis=1, keepdims=True) for c in centered) / count
        rstd = lax.rsqrt(var + EPS_NORM)
        total = [0.0, 0.0, 0.0]
        for k, c in enumerate(centered):
            j = jnp.bitwise_xor(t, k)
            part = (c * rstd * gains[k, 0:1, :] + gains[k, 1:2, :]).astype(BF16)
            acts[:, pl.ds(pl.multiple_of(j * width, width), width)] = part
            for s in range(3):
                total[s] = total[s] + dot_nn(part, weight[s, j])
        rows = pl.ds(pl.multiple_of(i * tile, tile), tile)
        for s, (value, kept) in enumerate(zip(total, (q_all, k_all, v_all))):
            low = (value * (DH ** (-0.5)) if s == 0 else value).astype(BF16)
            qkv[s] = low
            kept[rows, :] = low
        stats[:, 0:1] = mean
        stats[:, 1:2] = rstd

    @pl.when(i >= n)
    def _():
        cols = k_all.shape[0]
        first = far_first(i - n, n, sc) * tile
        rows = pl.ds(pl.multiple_of(first, tile), tile)
        if masked:
            q_side = (first + lax.broadcasted_iota(jnp.int32, (tile, 1), 0)) < sc[1]
            k_side = lax.broadcasted_iota(jnp.int32, (1, cols), 1) < sc[1]
            apart = jnp.logical_xor(q_side, k_side)
        for h in range(q_all.shape[1] // DH):
            part = slice(h * DH, (h + 1) * DH)
            scores = dot_nt(q_all[rows, part], k_all[:, part])
            if masked:
                scores = jnp.where(apart, NEG_FILL, scores)
            top = jnp.max(scores, axis=1, keepdims=True)
            weights = jnp.exp(scores - top)
            total = jnp.sum(weights, axis=1, keepdims=True)
            mixed = dot_nn(weights.astype(BF16), v_all[:, part])
            low = (mixed / total).astype(BF16)
            o[:, part] = low
            to = lax.rem(i, n // 2) * tile
            to = pl.ds(pl.multiple_of(to, tile), tile)

            @pl.when(i < n + n // 2)
            def _():
                other[to, part] = low

            @pl.when(i >= n + n // 2)
            def _():
                mine[to, part] = low

            stat = jnp.broadcast_to(top + jnp.log(total), (tile, DH))
            lse[h] = jnp.transpose(stat)[0:1, :]


def first_layer(scalars, pieces, dy, gains, weight4, h):
    rows, width = pieces[0].shape
    n = len(pieces)
    heads = width // DH
    tile = 256
    steps = rows // tile

    def early(i, sc):
        return (jnp.minimum(i, steps - 1), 0)

    def late(i, sc):
        return far_first(jnp.maximum(i - steps, 0), steps, sc)

    def rows_of(mine):
        def index(i, sc):
            c = jnp.bitwise_and(sc[0], 1)
            return (2 * h + (c if mine else 1 - c), 0)

        return pl.BlockSpec((rows // 2, width), index, pipeline_mode=pl.Buffered(1))

    whole = pl.BlockSpec((rows, width), lambda i, sc: (0, 0))

    return call(
        functools.partial(first_body, h == 1, tile),
        (2 * steps,),
        [pl.BlockSpec((tile, width), early)] * n
        + [rows_of(False), rows_of(True), full(gains.shape), full(weight4.shape)],
        [
            pl.BlockSpec((3, tile, width), lambda i, sc: (0, jnp.minimum(i, steps - 1), 0)),
            pl.BlockSpec((tile, n * width), early),
            pl.BlockSpec((tile, 2), early),
            pl.BlockSpec((tile, width), lambda i, sc: (late(i, sc), 0)),
            pl.BlockSpec((heads, 1, tile), lambda i, sc: (0, 0, late(i, sc))),
            whole,
            whole,
        ],
        [
            shape_of((3, rows, width), BF16),
            shape_of((rows, n * width), BF16),
            shape_of((rows, 2), F32),
            shape_of((rows, width), BF16),
            shape_of((heads, 1, rows), F32),
            shape_of((rows, width), BF16),
            shape_of((rows, width), BF16),
        ],
        scalars,
        [*pieces, dy, dy, gains, weight4],
        scratch=[pltpu.VMEM((rows, width), BF16)] * 3,
        flops=2 * rows * n * width * 3 * width + 4 * rows * rows * width,
    )


def quarter(u):
    return 2 * jnp.bitwise_and(u, 1) + jnp.right_shift(u, 1)


def feed_body(
    sc, x0, x1, x2, x3, p0, p1, p2, p3, ow, gains, up, down, bias,
    y_cols, y_rows, dy_rows, b_out, dy_out, g_out, du_out, send, keep, bias_grad, y_acc, total,
):
    t = sc[0]
    i = pl.program_id(0)
    side = jnp.right_shift(t, 1)
    xs, ps = (x0, x1, x2, x3), (p0, p1, p2, p3)
    rows, width = x0.shape
    n = len(xs)
    count = n * width

    @pl.when(i == 0)
    def _():
        def block(k):
            j = jnp.bitwise_xor(t, k)
            return pl.ds(pl.multiple_of(j * width, width), width)

        for k in range(n):
            y_acc[:, block(k)] = xs[k][...].astype(F32)
            dy_out[:, block(k)] = ps[k][rows:, :]
        y = y_acc[...]
        for k in range(n):
            y = y + dot_nn(ps[k][:rows, :], ow[block(k), :])
        y_acc[...] = y
        mean = jnp.sum(y, axis=1, keepdims=True) / count
        centered = y - mean
        rstd = lax.rsqrt(jnp.sum(centered * centered, axis=1, keepdims=True) / count + EPS_NORM)
        b_out[...] = (centered * rstd * gains[2:3, :] + gains[3:4, :]).astype(BF16)
        total[...] = jnp.zeros_like(total)
        wide = y_cols.shape[1]
        y_cols[...] = y_acc[:, pl.ds(pl.multiple_of(side * wide, wide), wide)]
        part = y_rows.shape[0]
        mine = pl.ds(pl.multiple_of(side * part, part), part)
        y_rows[...] = y_acc[mine, :]
        dy_rows[...] = dy_out[mine, :]

    u = dot_nn(b_out[...], up[...]) + bias[...]
    dh = dot_nt(dy_out[...], down[...])
    square = u * u
    half = 0.5 + 0.5 * jnp.tanh(u * (GELU_C + (GELU_C * 0.044715) * square))
    g_out[...] = (u * half).astype(BF16)
    inner = u * (2 * GELU_C + (6 * 0.044715 * GELU_C) * square)
    du = (dh * (half + (half - half * half) * inner)).astype(BF16)
    du_out[...] = du
    bias_grad[...] = jnp.sum(du.astype(F32), axis=0, keepdims=True)
    total[...] += dot_nt(du, up[...])

    @pl.when(i == pl.num_programs(0) - 1)
    def _():
        part = send.shape[0]
        for out, at in ((send, 1 - side), (keep, side)):
            out[...] = total[pl.ds(pl.multiple_of(at * part, part), part), :].astype(BF16)


def feed(scalars, xs, pieces, ow, gains, up, down, bias):
    rows, width = xs[0].shape
    n = len(xs)
    count = n * width
    hidden = up.shape[1]
    half = rows // 2
    part = half // 2
    step = 512

    def mine(i, sc):
        return (jnp.bitwise_and(sc[0], 1), 0)

    def fixed(i, sc):
        return (0, 0)

    def along(i, sc):
        return (0, i)

    return call(
        feed_body,
        (hidden // step,),
        [pl.BlockSpec((half, width), mine, pipeline_mode=pl.Buffered(1))] * n
        + [full(p.shape) for p in pieces]
        + [full(ow.shape), full(gains.shape)]
        + [
            pl.BlockSpec((count, step), along),
            pl.BlockSpec((step, count), lambda i, sc: (i, 0)),
            pl.BlockSpec((1, step), along),
        ],
        [
            pl.BlockSpec((half, count // 2), fixed),
            pl.BlockSpec((part, count), fixed),
            pl.BlockSpec((part, count), fixed),
            pl.BlockSpec((half, count), fixed),
            pl.BlockSpec((half, count), fixed),
            pl.BlockSpec((half, step), along),
            pl.BlockSpec((half, step), along),
            pl.BlockSpec((part, count), fixed),
            pl.BlockSpec((part, count), fixed),
            pl.BlockSpec((1, step), along),
        ],
        [
            shape_of((half, count // 2), F32),
            shape_of((part, count), F32),
            shape_of((part, count), BF16),
            shape_of((half, count), BF16),
            shape_of((half, count), BF16),
            shape_of((half, hidden), BF16),
            shape_of((half, hidden), BF16),
            shape_of((part, count), BF16),
            shape_of((part, count), BF16),
            shape_of((1, hidden), F32),
        ],
        scalars,
        [*xs, *pieces, ow, gains, up, down, bias],
        scratch=[pltpu.VMEM((half, count), F32), pltpu.VMEM((half, count), F32)],
        flops=2 * half * count * (count + 3 * hidden),
        vmem=32,
    )


def norm_back_body(sc, p0, p1, y, dy, gains, dz, sums):
    db = p0[...].astype(F32) + p1[...].astype(F32)
    yv = y[...]
    count = yv.shape[1]
    mean = jnp.sum(yv, axis=1, keepdims=True) / count
    centered = yv - mean
    rstd = lax.rsqrt(jnp.sum(centered * centered, axis=1, keepdims=True) / count + EPS_NORM)
    nhat = centered * rstd
    n = db * gains[2:3, :]
    first = jnp.sum(n, axis=1, keepdims=True) / count
    second = jnp.sum(n * nhat, axis=1, keepdims=True) / count
    dz[...] = (dy[...].astype(F32) + rstd * (n - first - nhat * second)).astype(BF16)
    sums[0:1, :] = jnp.sum(db * nhat, axis=0, keepdims=True)
    sums[1:2, :] = jnp.sum(db, axis=0, keepdims=True)


def norm_back(scalars, keep, got_x, y, dy, gains):
    rows, count = got_x.shape
    return call(
        norm_back_body,
        (1,),
        [full(v.shape) for v in (keep, got_x, y, dy, gains)],
        [
            pl.BlockSpec((rows, count), lambda i, sc: (0, 0)),
            pl.BlockSpec((2, count), lambda i, sc: (0, 0)),
        ],
        [shape_of((rows, count), BF16), shape_of((2, count), F32)],
        scalars,
        [keep, got_x, y, dy, gains],
    )


def attend_back_body(masked, sc, z0, z1, z2, z3, out_w, q, k, v, lse, grads, dz_out, dk_acc, dv_acc):
    i = pl.program_id(0)
    place = quarter(jnp.bitwise_xor(sc[0], i))

    @pl.when(i == 0)
    def _():
        dk_acc[...] = jnp.zeros_like(dk_acc)
        dv_acc[...] = jnp.zeros_like(dv_acc)

    for j, z in enumerate((z0, z1, z2, z3)):

        @pl.when(i == j)
        def _(z=z):
            dz_out[...] = z[...]

    d_mixed = dot_nt(dz_out[...], out_w[...]).astype(BF16)
    rows = d_mixed.shape[0]
    keys = k.shape[1]
    for h in range(d_mixed.shape[1] // DH):
        cols = slice(h * DH, (h + 1) * DH)
        q_h, k_h, v_h, do_h = q[0, :, cols], k[0, :, cols], v[0, :, cols], d_mixed[:, cols]
        scores = dot_nt(k_h, q_h)
        if masked:
            base = place * rows
            q_side = (base + lax.broadcasted_iota(jnp.int32, (1, rows), 1)) < sc[1]
            k_side = lax.broadcasted_iota(jnp.int32, (keys, 1), 0) < sc[1]
            scores = jnp.where(jnp.logical_xor(q_side, k_side), NEG_FILL, scores)
        p = jnp.exp(scores - lse[h])
        d_p = dot_nt(v_h, do_h)
        prod = p * d_p
        delta = jnp.sum(prod, axis=0, keepdims=True)
        d_s = (prod - p * delta).astype(BF16)
        dv_acc[:, cols] += dot_nn(p.astype(BF16), do_h)
        dk_acc[:, cols] += dot_nn(d_s, q_h)
        here = pl.ds(pl.multiple_of(place * rows, rows), rows)
        grads[here, cols] = dot_tn(d_s, k_h).astype(BF16)

    @pl.when(i == pl.num_programs(0) - 1)
    def _():
        width = dk_acc.shape[1]
        grads[:, width : 2 * width] = dk_acc[...].astype(BF16)
        grads[:, 2 * width :] = dv_acc[...].astype(BF16)


def attend_back(scalars, dzs, out_w, qkv, lse, masked):
    _, rows, width = qkv.shape
    heads = width // DH
    count = out_w.shape[1]
    tiles = rows // TILE

    def tile(i, sc):
        return (quarter(jnp.bitwise_xor(sc[0], i)), 0)

    return call(
        functools.partial(attend_back_body, masked),
        (tiles,),
        [full(dz.shape) for dz in dzs]
        + [
            full(out_w.shape),
            pl.BlockSpec((1, TILE, width), lambda i, sc: (0, tile(i, sc)[0], 0)),
            pl.BlockSpec((1, rows, width), lambda i, sc: (1, 0, 0)),
            pl.BlockSpec((1, rows, width), lambda i, sc: (2, 0, 0)),
            pl.BlockSpec((heads, 1, TILE), lambda i, sc: (0, 0, tile(i, sc)[0])),
        ],
        [
            pl.BlockSpec((rows, 3 * width), lambda i, sc: (0, 0)),
            pl.BlockSpec((TILE, count), tile),
        ],
        [shape_of((rows, 3 * width), BF16), shape_of((rows, count), BF16)],
        scalars,
        [*dzs, out_w, qkv, qkv, qkv, lse],
        scratch=[pltpu.VMEM((rows, width), F32), pltpu.VMEM((rows, width), F32)],
        flops=2 * rows * count * width + 10 * rows * rows * width,
    )


def relative(i):
    return jnp.where(i < 2, 2 * i + 1, 2 * i - 4)


def spread_body(scales, flipped, n_left, sc, *refs):
    lefts, right, send, keep = refs[:n_left], refs[n_left], refs[-2], refs[-1]
    i = pl.program_id(0)
    rows = lefts[0].shape[0]
    parts = []
    for left in lefts:
        if flipped:
            width = right.shape[2]
            total = None
            for s, scale in enumerate(scales):
                part = dot_nt(left[:, s * width : (s + 1) * width], right[s])
                part = part * scale if scale != 1.0 else part
                total = part if total is None else total + part
        else:
            total = dot_nn(left[...], right[...])
        parts.append(total.astype(BF16))

    def put(out):
        for at, part in enumerate(parts):
            out[0, at * rows : (at + 1) * rows, :] = part

    @pl.when(i < 2)
    def _():
        put(send)

    @pl.when(i >= 2)
    def _():
        put(keep)


def spread(scalars, lefts, right, n_tp, scales=None):
    flipped = scales is not None
    rows = sum(a.shape[0] for a in lefts)
    count = right.shape[1]
    width = count // n_tp

    def cols(i, sc):
        j = jnp.bitwise_xor(sc[0], relative(i))
        return (0, j, 0) if flipped else (0, j)

    block = (right.shape[0], width, right.shape[2]) if flipped else (right.shape[0], width)
    return call(
        functools.partial(spread_body, scales, flipped, len(lefts)),
        (n_tp,),
        [full(a.shape) for a in lefts] + [pl.BlockSpec(block, cols)],
        [
            pl.BlockSpec((1, rows, width), lambda i, sc: (jnp.minimum(i, 1), 0, 0)),
            pl.BlockSpec((1, rows, width), lambda i, sc: (jnp.maximum(i - 2, 0), 0, 0)),
        ],
        [shape_of((2, rows, width), BF16), shape_of((2, rows, width), BF16)],
        scalars,
        [*lefts, right],
        flops=2 * rows * lefts[0].shape[1] * count,
    )


def out_body(n_left, sc, *refs):
    lefts, right, send, keep = refs[:n_left], refs[n_left], refs[-2], refs[-1]
    i = pl.program_id(0)
    rows = lefts[0].shape[0]
    parts = [dot_nn(left[...], right[...]).astype(BF16) for left in lefts]
    for step, out in enumerate((send, keep)):

        @pl.when(i == step)
        def _(out=out):
            for at, part in enumerate(parts):
                out[at * rows : (at + 1) * rows, :] = part


def out_product(scalars, lefts, right):
    rows = sum(a.shape[0] for a in lefts)
    hidden, count = right.shape

    def cols(i, sc):
        side = jnp.right_shift(sc[0], 1)
        return (0, jnp.where(i == 0, 1 - side, side))

    return call(
        functools.partial(out_body, len(lefts)),
        (2,),
        [full(a.shape) for a in lefts] + [pl.BlockSpec((hidden, count // 2), cols)],
        [pl.BlockSpec((rows, count // 2), lambda i, sc: (0, 0))] * 2,
        [shape_of((rows, count // 2), BF16)] * 2,
        scalars,
        [*lefts, right],
        flops=2 * rows * hidden * count,
    )


def pair_grad_body(sc, a0, a1, b0, b1, send, keep):
    i = pl.program_id(0)
    low = (dot_tn(a0[...], b0[...]) + dot_tn(a1[...], b1[...])).astype(BF16)
    for step, out in enumerate((send, keep)):

        @pl.when(i == step)
        def _(out=out):
            out[...] = low


def pair_grad(scalars, lefts, rights, split_left):
    rows = lefts[0].shape[0]
    halved = lambda i, sc: (0, 1 - i)
    m = lefts[0].shape[1] // (2 if split_left else 1)
    count = rights[0].shape[1] // (1 if split_left else 2)
    left = pl.BlockSpec((rows, m), halved) if split_left else full((rows, m))
    right = full((rows, count)) if split_left else pl.BlockSpec((rows, count), halved)
    return call(
        pair_grad_body,
        (2,),
        [left, left, right, right],
        [pl.BlockSpec((m, count), lambda i, sc: (0, 0))] * 2,
        [shape_of((m, count), BF16)] * 2,
        scalars,
        [*lefts, *rights],
        flops=8 * rows * m * count,
        vmem=32,
    )


def norm_sums_body(sc, da, x, stats, gain, moments, sums):
    d = da[...].astype(F32)
    nhat = (x[...].astype(F32) - stats[:, 0:1]) * stats[:, 1:2]
    n = d * gain[...]
    prod = d * nhat
    rows = d.shape[0]
    for at, v in enumerate((n, n * nhat)):
        total = jnp.broadcast_to(jnp.sum(v, axis=1, keepdims=True), (rows, 128))
        moments[at : at + 1, :] = jnp.transpose(total)[0:1, :]
    sums[0:1, :] = jnp.sum(prod, axis=0, keepdims=True)
    sums[1:2, :] = jnp.sum(d, axis=0, keepdims=True)


def norm_sums(scalars, da, x, stats, gain):
    rows, width = da.shape
    return call(
        norm_sums_body,
        (1,),
        [full(v.shape) for v in (da, x, stats, gain)],
        [pl.BlockSpec((2, rows), lambda i, sc: (0, 0)), pl.BlockSpec((2, width), lambda i, sc: (0, 0))],
        [shape_of((2, rows), F32), shape_of((2, width), F32)],
        scalars,
        [da, x, stats, gain],
    )


def attn_grad_body(sc, a0, a1, c0, c1, z0, z1, d0, d1, o0, o1, send1, keep1, send2, keep2):
    i = pl.program_id(0)
    width = o0.shape[1]
    low1 = dot_tn(a0[...], d0[:, : 2 * width]) + dot_tn(a1[...], d1[:, : 2 * width])
    low2 = dot_tn(c0[...], d0[:, 2 * width :]) + dot_tn(c1[...], d1[:, 2 * width :])
    low3 = dot_tn(z0[...], o0[...]) + dot_tn(z1[...], o1[...])
    low1, low2, low3 = low1.astype(BF16), low2.astype(BF16), low3.astype(BF16)
    for step, (out1, out2) in enumerate(((send1, send2), (keep1, keep2))):

        @pl.when(i == step)
        def _(out1=out1, out2=out2):
            out1[...] = low1
            out2[:, :width] = low2
            out2[:, width:] = low3


def attn_grad(scalars, acts, dzs, grads, mixed, bits):
    rows, m = acts[0].shape
    width = mixed[0].shape[1]

    def half(bit):
        def index(i, sc):
            mine = jnp.bitwise_and(jnp.right_shift(sc[2], bit), 1)
            return (0, jnp.where(i == 0, 1 - mine, mine))

        return pl.BlockSpec((rows, m // 2), index)

    shape = (m // 2, 2 * width)
    return call(
        attn_grad_body,
        (2,),
        [half(bits[0])] * 2 + [half(bits[1])] * 4 + [full(v.shape) for v in (*grads, *mixed)],
        [pl.BlockSpec(shape, lambda i, sc: (0, 0))] * 4,
        [shape_of(shape, BF16)] * 4,
        scalars,
        [*acts, *acts, *dzs, *grads, *mixed],
        flops=16 * rows * m * width,
        vmem=32,
    )


def place_body(blocks, sc, first, second, out):
    rows = first.shape[0] * 2 // blocks
    half = blocks // 2
    for k in range(blocks):
        src = first if k < half else second
        at = (k if k < half else k - half) * rows
        to = pl.ds(pl.multiple_of(jnp.bitwise_xor(sc[0], k) * rows, rows), rows)
        out[to, :] = src[at : at + rows, :].astype(F32)


def place(index, first, second, blocks, width):
    m, count = first.shape[0] * 2, first.shape[1]
    half = pl.BlockSpec((m // 2, width), lambda i, sc: (0, i))
    return call(
        functools.partial(place_body, blocks),
        (count // width,),
        [half, half],
        pl.BlockSpec((m, width), lambda i, sc: (0, i)),
        shape_of((m, count), F32),
        index,
        [first, second],
    )


def unpack_body(scale, blocks, sc, f1, s1, f2, s2, d_qkv, d_out):
    i = pl.program_id(0)
    rows = f1.shape[0] * 2 // blocks
    half = blocks // 2

    def each(first, second, index, put):
        for k in range(blocks):
            src = first if k < half else second
            at = (k if k < half else k - half) * rows
            to = pl.ds(pl.multiple_of(jnp.bitwise_xor(index, k) * rows, rows), rows)
            put(to, src[at : at + rows, :].astype(F32))

    def plain(to, value):
        d_qkv[0, to, :] = value

    def scaled(to, value):
        d_qkv[0, to, :] = value * jnp.where(i == 0, jnp.float32(scale), jnp.float32(1.0))

    def turned(to, value):
        d_out[:, to] = jnp.transpose(value)

    @pl.when(i < 2)
    def _():
        each(f1, s1, sc[0], scaled)

    @pl.when(i == 2)
    def _():
        each(f2, s2, sc[1], plain)

    @pl.when(i == 3)
    def _():
        each(f2, s2, sc[1], turned)


def unpack(index, first1, second1, first2, second2, blocks, scale):
    m, count = first1.shape[0] * 2, first1.shape[1]
    width = count // 2
    one = pl.BlockSpec((m // 2, width), lambda i, sc: (0, jnp.minimum(i, 1)))
    two = pl.BlockSpec((m // 2, width), lambda i, sc: (0, jnp.maximum(i - 2, 0)))
    return call(
        functools.partial(unpack_body, scale, blocks),
        (4,),
        [one, one, two, two],
        [
            pl.BlockSpec((1, m, width), lambda i, sc: (jnp.minimum(i, 2), 0, 0)),
            pl.BlockSpec((width, m), lambda i, sc: (0, 0)),
        ],
        [shape_of((3, m, width), F32), shape_of((width, m), F32)],
        index,
        [first1, second1, first2, second2],
    )


def halve_body(bits, sc, *refs):
    n = len(bits)
    keeps, gots, sends, nexts = refs[:n], refs[n : 2 * n], refs[2 * n : 3 * n], refs[3 * n :]
    for bit, keep, got, send, nxt in zip(bits, keeps, gots, sends, nexts):
        half = send.shape[0]
        mine = jnp.bitwise_and(jnp.right_shift(sc[2], bit), 1)
        for out, side in ((send, 1 - mine), (nxt, mine)):
            rows = pl.ds(pl.multiple_of(side * half, half), half)
            out[...] = (keep[rows, :].astype(F32) + got[rows, :].astype(F32)).astype(BF16)


def halve(scalars, keeps, gots, bits):
    shapes = [shape_of((k.shape[0] // 2, k.shape[1]), BF16) for k in keeps] * 2
    return call(
        functools.partial(halve_body, bits),
        (1,),
        [full(v.shape) for v in (*keeps, *gots)],
        [pl.BlockSpec(v.shape, lambda i, sc: (0, 0)) for v in shapes],
        shapes,
        scalars,
        [*keeps, *gots],
    )


def join_body(added, sc, *refs):
    n = len(refs) // 3
    for a, c, out in zip(refs[:n], refs[n : 2 * n], refs[2 * n :]):
        rows = a.shape[0]
        if added:
            out[...] = (a[...].astype(F32) + c[...].astype(F32)).astype(BF16)
        else:
            out[:rows, :] = a[...]
            out[rows:, :] = c[...]


def join(scalars, firsts, seconds, added):
    times = 1 if added else 2
    shapes = [shape_of((a.shape[0] * times, a.shape[1]), BF16) for a in firsts]
    return call(
        functools.partial(join_body, added),
        (1,),
        [full(v.shape) for v in (*firsts, *seconds)],
        [pl.BlockSpec(v.shape, lambda i, sc: (0, 0)) for v in shapes],
        shapes,
        scalars,
        [*firsts, *seconds],
    )


def prepare_body(half, lens, here, out):
    count = lens.shape[1]
    start, border, before = jnp.int32(0), jnp.int32(0), jnp.int32(0)
    for i in range(count):
        big = lens[0, i] == half
        start = jnp.where(big, before, start)
        border = jnp.where(big, lens[0, (i + 1) % count], border)
        before = before + lens[0, i]
    out[0] = here[0]
    out[1] = border
    out[2] = here[1]
    out[3] = start


def prepare(lengths, here, half):
    smem = pl.BlockSpec(memory_space=pltpu.SMEM)
    return pl.pallas_call(
        functools.partial(prepare_body, half),
        in_specs=[smem, smem],
        out_specs=smem,
        out_shape=shape_of((4,), jnp.int32),
    )(lengths, here)


class Chain:
    def __init__(self):
        self.last = ()

    def tie(self, value, *need):
        return lax.optimization_barrier((value, need, self.last))[0]

    def do(self, fn, *args, **keywords):
        leaves, tree = jax.tree_util.tree_flatten(args)
        arrays = iter(self.tie([v for v in leaves if isinstance(v, jax.Array)]))
        leaves = [next(arrays) if isinstance(v, jax.Array) else v for v in leaves]
        out = fn(*jax.tree_util.tree_unflatten(tree, leaves), **keywords)
        self.last = jax.tree_util.tree_leaves(out)[0]
        return out


class RowSums:
    def __init__(self, chain, scalars, r, n_rows, orders, pairs, core_flip=None):
        self.chain, self.scalars, self.r, self.n_rows = chain, scalars, r, n_rows
        self.orders = orders
        self.depth = len(orders[0])
        self.rest = [b for b in range(n_rows.bit_length() - 1) if b not in orders[0]]
        self.keeps = [keep for _, keep in pairs]
        sends = [send for send, _ in pairs]
        self.at = 0 if core_flip is None else -1
        self.gots = self.flips(sends) if core_flip is None else [core_flip(v) for v in sends]

    def flip(self, value, bit):
        return lax.ppermute(value, "rows", [(i, i ^ (1 << bit)) for i in range(self.n_rows)])

    def flips(self, values):
        return [self.flip(v, order[self.at]) for v, order in zip(values, self.orders)]

    def scatter(self):
        self.at += 1
        if self.at < self.depth:
            bits = [order[self.at] for order in self.orders]
            out = self.chain.do(halve, self.scalars, self.keeps, self.gots, bits)
            n = len(self.orders)
            self.keeps = out[n:]
            self.gots = self.flips(out[:n])
            return
        total = self.chain.do(join, self.scalars, self.keeps, self.gots, True)
        for b in self.rest:
            total = self.chain.do(join, self.scalars, total, [self.flip(v, b) for v in total], True)
        self.bufs = total
        self.at = self.depth - 1
        self.gots = self.flips(self.bufs)

    def gather(self):
        self.at -= 1
        self.bufs = self.chain.do(join, self.scalars, self.bufs, self.gots, False)
        self.gots = self.flips(self.bufs)

    def index(self, which):
        index = 0
        for b in self.orders[which]:
            index = index * 2 + jnp.bitwise_and(jnp.right_shift(self.r, b), 1)
        return index

    def finish(self, which, width):
        index = jnp.stack([self.index(which)] * 2).astype(jnp.int32)
        return self.chain.do(
            place, index, self.bufs[which], self.gots[which], 1 << self.depth, width
        )

    def finish_attn(self, scale):
        index = jnp.stack([self.index(0), self.index(1)]).astype(jnp.int32)
        return self.chain.do(
            unpack, index, self.bufs[0], self.gots[0], self.bufs[1], self.gots[1],
            1 << self.depth, scale,
        )


def local(
    n_tp, n_rows,
    datapoints, lengths, qkv_weight, out_weight, up_weight, up_bias, down_weight, down_bias,
    gain_one, shift_one, gain_two, shift_two, grad_out,
):
    tok, width = datapoints.shape
    count = n_tp * width
    half = tok // 2
    q_scale = DH ** (-0.5)
    t, r = lax.axis_index("tp"), lax.axis_index("rows")
    chain = Chain()
    do, tie = chain.do, chain.tie

    def core_flip(v):
        return lax.ppermute(v, "tp", [(i, i ^ 1) for i in range(n_tp)])

    def x_flip(v):
        return lax.ppermute(v, "tp", [(i, i ^ 2) for i in range(n_tp)])

    def row_flip(v, b):
        return lax.ppermute(v, "rows", [(i, i ^ (1 << b)) for i in range(n_rows)])

    def first_half(v, start):
        return lax.dynamic_slice_in_dim(v, start, half, 0)

    def second_half(v, start):
        turned = jnp.concatenate([v[half:], v[:half]], 0)
        return lax.dynamic_slice_in_dim(turned, start, half, 0)

    def rolled(v, start):
        return lax.dynamic_slice_in_dim(jnp.concatenate([v, v[:half]], 0), start, tok, 0)

    ow = lax.all_gather(out_weight, "tp", axis=0, tiled=True)
    vectors = jnp.concatenate([gain_one, shift_one, gain_two, shift_two, down_bias])
    vec_x = x_flip(vectors)
    vec_c = core_flip(jnp.concatenate([vectors, up_bias]))
    scalars = prepare(lengths, jnp.stack([t, r]).astype(jnp.int32), half)
    start = scalars[3]
    x0 = do(first_half, datapoints, start)
    x0_x, x0_c = x_flip(x0), core_flip(x0)
    x1 = do(second_half, datapoints, start)
    dy = do(rolled, grad_out, start)
    vec_d = core_flip(tie(vec_x))
    d_down_bias = do(lambda v: jnp.sum(v.astype(F32), axis=0), grad_out)
    n_vec = vectors.shape[0] // width

    def vector_orders(*pieces):
        rel = jnp.stack([p[: n_vec * width].reshape(n_vec, width) for p in pieces])
        order = jnp.bitwise_xor(t, jnp.arange(n_tp))
        return rel, jnp.transpose(rel[order], (1, 0, 2)).reshape(n_vec, count)

    gains_rel, gains = do(vector_orders, vectors, vec_c, vec_x, vec_d)
    weight4 = qkv_weight.reshape(3, n_tp, width, width)

    x0_d = core_flip(x0_x)
    x1 = tie(x1, x0_x)
    x1_x, x1_c = x_flip(x1), core_flip(x1)
    xs = [[x0, x0_c, x0_x, x0_d], None]
    qkv, acts, stats, mixed, lse, pieces = [[None] * 2 for _ in range(6)]

    def first(h):
        qkv[h], acts[h], stats[h], mixed[h], lse[h], other, mine = do(
            first_layer, scalars, xs[h], dy, gains_rel, weight4, h
        )
        diag = lax.ppermute(other, "tp", [(i, i ^ 3) for i in range(n_tp)])
        pieces[h] = [mine, core_flip(other), x_flip(mine), diag]

    first(0)
    up_c, down_c = core_flip(tie(up_weight)), core_flip(tie(down_weight))
    x1_d = core_flip(tie(x1_x))
    xs[1] = [x1, x1_c, x1_x, x1_d]
    first(1)

    def both(up_w, down_w, up_b, up_w_c, down_w_c, vec):
        up_b_c = vec[n_vec * width :]
        return (
            jnp.concatenate([up_w, up_w_c], 1),
            jnp.concatenate([down_w, down_w_c], 0),
            jnp.concatenate([up_b, up_b_c]).reshape(1, -1),
        )

    up2, down2, bias2 = do(both, up_weight, down_weight, up_bias, up_c, down_c, vec_c)
    weights = [ow, gains, up2, down2, bias2]
    fed0 = do(feed, scalars, xs[0], pieces[0], *weights)
    db0_x = x_flip(fed0[7])
    fed1 = do(feed, scalars, xs[1], pieces[1], *weights)
    db1_x = x_flip(fed1[7])
    y_cols, b, dyn, g, du = [[fed0[k], fed1[k]] for k in (0, 3, 4, 5, 6)]
    dz0, sums0 = do(norm_back, scalars, fed0[8], db0_x, fed0[1], fed0[2], gains)
    dz0_x, dz0_c = x_flip(dz0), core_flip(dz0)
    down_pair = do(pair_grad, scalars, g, dyn, True)
    up_pair = do(pair_grad, scalars, b, du, False)
    sums = RowSums(
        chain, scalars, r, n_rows, [[0, 1, 2], [1, 0, 2]], [down_pair, up_pair], core_flip
    )
    sums.scatter()
    dz1, sums1 = do(norm_back, scalars, fed1[8], db1_x, fed1[1], fed1[2], gains)
    dz1_x, dz1_c = x_flip(dz1), core_flip(dz1)
    dz0_d = core_flip(tie(dz0_x))
    two_sums = sums0 + sums1
    hidden = up_bias.shape[0]
    bias_grad = do(jnp.add, fed0[9], fed1[9])
    bias_got = core_flip(bias_grad[:, hidden:])

    grads0, dzn0 = do(
        attend_back, scalars, [dz0, dz0_c, dz0_x, dz0_d], out_weight, qkv[0], lse[0], False
    )
    dz1_d = core_flip(tie(dz1_x))
    sums.scatter()
    grads1, dzn1 = do(
        attend_back, scalars, [dz1, dz1_c, dz1_x, dz1_d], out_weight, qkv[1], lse[1], True
    )
    sums.scatter()
    parts = do(attn_grad, scalars, acts, [dzn0, dzn1], [grads0, grads1], mixed, (0, 1))
    attn = RowSums(chain, scalars, r, n_rows, [[0, 1, 2], [1, 0, 2]], [parts[:2], parts[2:]])

    def middle(keep, got):
        return (keep[1].astype(F32) + got[1].astype(F32)).astype(BF16)

    def total_of(keep, got, got_x):
        return keep[0].astype(F32) + got[0].astype(F32) + got_x.astype(F32)

    sums.scatter()
    send, keep_a = do(spread, scalars, [grads0, grads1], qkv_weight, n_tp, (q_scale, 1.0, 1.0))
    got_a = core_flip(send)
    attn.scatter()
    sums.gather()
    da_x = x_flip(do(middle, keep_a, got_a))
    out_send, out_keep = do(out_product, scalars, g, down2)
    attn.scatter()
    sums.gather()
    out_x = x_flip(tie(out_send, da_x))
    gain_row = gain_one.reshape(1, -1)

    def joined(*parts):
        return total_of(*parts).astype(BF16)

    da = do(joined, keep_a, got_a, da_x)
    m0, ones0 = do(norm_sums, scalars, da[:half], x0, stats[0], gain_row)
    m1, ones1 = do(norm_sums, scalars, da[half:], x1, stats[1], gain_row)
    attn.scatter()
    m = do(lambda *a: jnp.concatenate(a, 0), two_sums, m0, m1)
    m_c = core_flip(m)
    c, side = jnp.bitwise_and(t, 1), jnp.right_shift(t, 1)

    def output_rows(keep, got, y0, y1, vecs):
        wide = 2 * width
        extra = lax.dynamic_slice_in_dim(vecs[4], side * wide, wide, 0)
        total = keep.astype(F32) + got.astype(F32) + jnp.concatenate([y0, y1], 0) + extra
        low = total.astype(BF16)
        return (
            lax.dynamic_slice_in_dim(low, (1 - c) * width, width, 1),
            lax.dynamic_slice_in_dim(low, c * width, width, 1),
        )

    rows_send, rows_keep = do(output_rows, out_keep, out_x, *y_cols, gains)
    rows_got = core_flip(rows_send)
    m = do(jnp.add, m, m_c)
    m_x = x_flip(m)
    attn.gather()

    def unroll(first, second):
        thrice = jnp.concatenate([second, first, second], 0)
        return lax.dynamic_slice_in_dim(thrice, half - start, tok, 0)

    def output_of(mine, other):
        part = half // 2
        halves = []
        for h in range(2):
            a, b = mine[h * part : (h + 1) * part], other[h * part : (h + 1) * part]
            halves.append(
                jnp.where(c == 0, jnp.concatenate([a, b], 0), jnp.concatenate([b, a], 0))
            )
        return unroll(*halves)

    output = do(output_of, rows_keep, rows_got)
    m = do(jnp.add, m, m_x)

    def small_of(up_b, down_b, m, ones0, ones1):
        two = lax.dynamic_slice_in_dim(m[:2], t * width, width, 1)
        return jnp.concatenate(
            [up_b.reshape(-1), down_b, (ones0 + ones1).reshape(-1), two.reshape(-1)]
        ).reshape(-1, 128)

    d_up_bias = bias_grad[:, :hidden] + bias_got
    small = do(small_of, d_up_bias, d_down_bias, m, ones0, ones1)
    bits = list(range(n_rows.bit_length() - 1))
    small_got = row_flip(small, bits[0])

    def d_input_of(m, da, *parts):
        halves = []
        for h, (x, stat, dzn) in enumerate((parts[:3], parts[3:])):
            nhat = (x.astype(F32) - stat[:, 0:1]) * stat[:, 1:2]
            first, second = m[2 + 2 * h][:, None] / count, m[3 + 2 * h][:, None] / count
            dz = lax.dynamic_slice_in_dim(dzn, t * width, width, 1).astype(F32)
            n = da[h * half : (h + 1) * half].astype(F32) * gain_one
            halves.append(dz + stat[:, 1:2] * (n - first - nhat * second))
        return unroll(*halves)

    attn.gather()
    d_input = do(d_input_of, m, da, x0, stats[0], dzn0, x1, stats[1], dzn1)
    d_down = sums.finish(0, width)
    for bit in bits[1:]:
        small = do(jnp.add, small, small_got)
        small_got = row_flip(small, bit)
    d_up = sums.finish(1, width)
    small = do(jnp.add, small, small_got).reshape(-1)
    d_qkv, d_out = attn.finish_attn(q_scale)
    d_down_bias, d_gain_one, d_shift_one, d_gain_two, d_shift_two = small[hidden:].reshape(5, width)
    return (
        output, d_input, d_qkv, d_out, d_up, small[:hidden],
        d_down, d_down_bias, d_gain_one, d_shift_one, d_gain_two, d_shift_two,
    )


def solution(mesh):
    grid = P("rows", "tp")
    placed = (
        grid, P("rows", None), P(None, None, "tp"), P("tp", None), P(None, "tp"), P("tp"),
        P("tp", None), P("tp"), P("tp"), P("tp"), P("tp"), P("tp"), grid,
    )
    return jax.shard_map(
        functools.partial(local, mesh.shape["tp"], mesh.shape["rows"]),
        mesh=mesh,
        in_specs=placed,
        out_specs=(
            grid, grid, P(None, None, "tp"), P("tp", None), P(None, "tp"), P("tp"),
            P("tp", None), P("tp"), P("tp"), P("tp"), P("tp"), P("tp"),
        ),
        check_vma=False,
    )
```

```python
import functools

import jax
import jax.numpy as jnp
from jax import lax
from jax.experimental import pallas as pl
from jax.experimental.pallas import tpu as pltpu
from jax.sharding import PartitionSpec as P

DH = 128
TILE = 256
EPS_NORM = 1e-05
NEG_FILL = -1e30
F32 = jnp.float32
BF16 = jnp.bfloat16
MIB = 1024 * 1024
COST = 8.0
GELU_C = 0.7978845608028654


def dot_nn(a, b):
    return jnp.dot(a, b, preferred_element_type=F32)


def dot_nt(a, b):
    return lax.dot_general(a, b, (((1,), (1,)), ((), ())), preferred_element_type=F32)


def dot_tn(a, b):
    return lax.dot_general(a, b, (((0,), (0,)), ((), ())), preferred_element_type=F32)


def call(body, grid, in_specs, out_specs, out_shape, scalars, operands, scratch=(), flops=0, vmem=24, hbm=False, cost=2e10):
    bytes_moved = sum(o.size * o.dtype.itemsize for o in operands)
    bytes_moved += sum(
        o.size * jnp.dtype(o.dtype).itemsize for o in jax.tree_util.tree_leaves(out_shape)
    )
    operands = [
        pltpu.with_memory_space_constraint(o, pltpu.HBM) if hbm else o for o in operands
    ]
    if hbm:
        out_shape = jax.tree_util.tree_map(lambda o: pltpu.HBM(o.shape, o.dtype), out_shape)
    return pl.pallas_call(
        body,
        grid_spec=pltpu.PrefetchScalarGridSpec(
            num_scalar_prefetch=1,
            grid=grid,
            in_specs=in_specs,
            out_specs=out_specs,
            scratch_shapes=list(scratch),
        ),
        out_shape=out_shape,
        compiler_params=pltpu.CompilerParams(
            vmem_limit_bytes=vmem * MIB,
            dimension_semantics=("arbitrary",) * len(grid),
        ),
        cost_estimate=pl.CostEstimate(
            flops=int(cost), bytes_accessed=int(bytes_moved), transcendentals=0
        ),
    )(scalars, *operands)


def full(shape):
    zeros = (0,) * len(shape)
    return pl.BlockSpec(shape, lambda *_: zeros, pipeline_mode=pl.Buffered(1))


def shape_of(shape, dtype):
    return jax.ShapeDtypeStruct(shape, dtype)


def far_first(i, n, sc):
    c = jnp.bitwise_and(sc[0], 1)
    return jnp.where(i < n // 2, (1 - c) * (n // 2) + i, c * (n // 2) + i - n // 2)


def first_body(
    masked, tile, sc, x0, x1, x2, x3, dy_other, dy_mine, gains, weight,
    qkv, acts, stats, o, lse, other, mine, q_all, k_all, v_all,
):
    t = sc[0]
    i = pl.program_id(0)
    n = pl.num_programs(0) // 2

    @pl.when(i == 0)
    def _():
        rows = dy_mine.shape[0]
        other[rows:, :] = dy_other[...]
        mine[rows:, :] = dy_mine[...]

    @pl.when(i < n)
    def _():
        pieces = [x[...].astype(F32) for x in (x0, x1, x2, x3)]
        width = pieces[0].shape[1]
        count = width * len(pieces)
        mean = sum(jnp.sum(x, axis=1, keepdims=True) for x in pieces) / count
        centered = [x - mean for x in pieces]
        var = sum(jnp.sum(c * c, axis=1, keepdims=True) for c in centered) / count
        rstd = lax.rsqrt(var + EPS_NORM)
        total = [0.0, 0.0, 0.0]
        for k, c in enumerate(centered):
            j = jnp.bitwise_xor(t, k)
            part = (c * rstd * gains[k, 0:1, :] + gains[k, 1:2, :]).astype(BF16)
            acts[:, pl.ds(pl.multiple_of(j * width, width), width)] = part
            for s in range(3):
                total[s] = total[s] + dot_nn(part, weight[s, j])
        rows = pl.ds(pl.multiple_of(i * tile, tile), tile)
        for s, (value, kept) in enumerate(zip(total, (q_all, k_all, v_all))):
            low = (value * (DH ** (-0.5)) if s == 0 else value).astype(BF16)
            qkv[s] = low
            kept[rows, :] = low
        stats[:, 0:1] = mean
        stats[:, 1:2] = rstd

    @pl.when(i >= n)
    def _():
        cols = k_all.shape[0]
        first = far_first(i - n, n, sc) * tile
        rows = pl.ds(pl.multiple_of(first, tile), tile)
        if masked:
            q_side = (first + lax.broadcasted_iota(jnp.int32, (tile, 1), 0)) < sc[1]
            k_side = lax.broadcasted_iota(jnp.int32, (1, cols), 1) < sc[1]
            apart = jnp.logical_xor(q_side, k_side)
        for h in range(q_all.shape[1] // DH):
            part = slice(h * DH, (h + 1) * DH)
            scores = dot_nt(q_all[rows, part], k_all[:, part])
            if masked:
                scores = jnp.where(apart, NEG_FILL, scores)
            top = jnp.max(scores, axis=1, keepdims=True)
            weights = jnp.exp(scores - top)
            total = jnp.sum(weights, axis=1, keepdims=True)
            mixed = dot_nn(weights.astype(BF16), v_all[:, part])
            low = (mixed / total).astype(BF16)
            o[:, part] = low
            to = lax.rem(i, n // 2) * tile
            to = pl.ds(pl.multiple_of(to, tile), tile)

            @pl.when(i < n + n // 2)
            def _():
                other[to, part] = low

            @pl.when(i >= n + n // 2)
            def _():
                mine[to, part] = low

            stat = jnp.broadcast_to(top + jnp.log(total), (tile, DH))
            lse[h] = jnp.transpose(stat)[0:1, :]


def first_layer(scalars, pieces, dy, gains, weight4, h):
    rows, width = pieces[0].shape
    n = len(pieces)
    heads = width // DH
    tile = 256
    steps = rows // tile

    def early(i, sc):
        return (jnp.minimum(i, steps - 1), 0)

    def late(i, sc):
        return far_first(jnp.maximum(i - steps, 0), steps, sc)

    def rows_of(mine):
        def index(i, sc):
            c = jnp.bitwise_and(sc[0], 1)
            return (2 * h + (c if mine else 1 - c), 0)

        return pl.BlockSpec((rows // 2, width), index, pipeline_mode=pl.Buffered(1))

    whole = pl.BlockSpec((rows, width), lambda i, sc: (0, 0))

    return call(
        functools.partial(first_body, h == 1, tile),
        (2 * steps,),
        [pl.BlockSpec((tile, width), early)] * n
        + [rows_of(False), rows_of(True), full(gains.shape), full(weight4.shape)],
        [
            pl.BlockSpec((3, tile, width), lambda i, sc: (0, jnp.minimum(i, steps - 1), 0)),
            pl.BlockSpec((tile, n * width), early),
            pl.BlockSpec((tile, 2), early),
            pl.BlockSpec((tile, width), lambda i, sc: (late(i, sc), 0)),
            pl.BlockSpec((heads, 1, tile), lambda i, sc: (0, 0, late(i, sc))),
            whole,
            whole,
        ],
        [
            shape_of((3, rows, width), BF16),
            shape_of((rows, n * width), BF16),
            shape_of((rows, 2), F32),
            shape_of((rows, width), BF16),
            shape_of((heads, 1, rows), F32),
            shape_of((rows, width), BF16),
            shape_of((rows, width), BF16),
        ],
        scalars,
        [*pieces, dy, dy, gains, weight4],
        scratch=[pltpu.VMEM((rows, width), BF16)] * 3,
        hbm=True,
        flops=2 * rows * n * width * 3 * width + 4 * rows * rows * width,
    )


def quarter(u):
    return 2 * jnp.bitwise_and(u, 1) + jnp.right_shift(u, 1)


def feed_body(
    sc, x0, x1, x2, x3, p0, p1, p2, p3, ow, gains, up, up_c, down, down_c, bias,
    y_cols, y_rows, dy_rows, b_out, dy_out, g_out, du_out, send, keep, bias_grad, y_acc, total,
):
    t = sc[0]
    i = pl.program_id(0)
    side = jnp.right_shift(t, 1)
    xs, ps = (x0, x1, x2, x3), (p0, p1, p2, p3)
    rows, width = x0.shape
    n = len(xs)
    count = n * width

    @pl.when(i == 0)
    def _():
        def block(k):
            j = jnp.bitwise_xor(t, k)
            return pl.ds(pl.multiple_of(j * width, width), width)

        for k in range(n):
            y_acc[:, block(k)] = xs[k][...].astype(F32)
            dy_out[:, block(k)] = ps[k][rows:, :]
        y = y_acc[...]
        for k in range(n):
            y = y + dot_nn(ps[k][:rows, :], ow[block(k), :])
        y_acc[...] = y
        mean = jnp.sum(y, axis=1, keepdims=True) / count
        centered = y - mean
        rstd = lax.rsqrt(jnp.sum(centered * centered, axis=1, keepdims=True) / count + EPS_NORM)
        b_out[...] = (centered * rstd * gains[2:3, :] + gains[3:4, :]).astype(BF16)
        total[...] = jnp.zeros_like(total)
        wide = y_cols.shape[1]
        y_cols[...] = y_acc[:, pl.ds(pl.multiple_of(side * wide, wide), wide)]
        part = y_rows.shape[0]
        mine = pl.ds(pl.multiple_of(side * part, part), part)
        y_rows[...] = y_acc[mine, :]
        dy_rows[...] = dy_out[mine, :]

    def chunk(up, down):
        u = dot_nn(b_out[...], up[...]) + bias[...]
        dh = dot_nt(dy_out[...], down[...])
        square = u * u
        half = 0.5 + 0.5 * jnp.tanh(u * (GELU_C + (GELU_C * 0.044715) * square))
        g_out[...] = (u * half).astype(BF16)
        inner = u * (2 * GELU_C + (6 * 0.044715 * GELU_C) * square)
        du = (dh * (half + (half - half * half) * inner)).astype(BF16)
        du_out[...] = du
        bias_grad[...] = jnp.sum(du.astype(F32), axis=0, keepdims=True)
        total[...] += dot_nt(du, up[...])

    steps = pl.num_programs(0)

    @pl.when(i < steps // 2)
    def _():
        chunk(up, down)

    @pl.when(i >= steps // 2)
    def _():
        chunk(up_c, down_c)

    @pl.when(i == pl.num_programs(0) - 1)
    def _():
        part = send.shape[0]
        for out, at in ((send, 1 - side), (keep, side)):
            out[...] = total[pl.ds(pl.multiple_of(at * part, part), part), :].astype(BF16)


def feed(scalars, xs, pieces, ow, gains, up, up_c, down, down_c, bias):
    rows, width = xs[0].shape
    n = len(xs)
    count = n * width
    step = 512
    near = up.shape[1] // step
    hidden = 2 * up.shape[1]
    half = rows // 2
    part = half // 2

    def own(i):
        return jnp.minimum(i, near - 1)

    def other(i):
        return jnp.maximum(i - near, 0)

    def mine(i, sc):
        return (jnp.bitwise_and(sc[0], 1), 0)

    def fixed(i, sc):
        return (0, 0)

    def along(i, sc):
        return (0, i)

    return call(
        feed_body,
        (hidden // step,),
        [pl.BlockSpec((half, width), mine, pipeline_mode=pl.Buffered(1))] * n
        + [full(p.shape) for p in pieces]
        + [full(ow.shape), full(gains.shape)]
        + [
            pl.BlockSpec((count, step), lambda i, sc: (0, own(i))),
            pl.BlockSpec((count, step), lambda i, sc: (0, other(i))),
            pl.BlockSpec((step, count), lambda i, sc: (own(i), 0)),
            pl.BlockSpec((step, count), lambda i, sc: (other(i), 0)),
            pl.BlockSpec((1, step), along),
        ],
        [
            pl.BlockSpec((half, count // 2), fixed),
            pl.BlockSpec((part, count), fixed),
            pl.BlockSpec((part, count), fixed),
            pl.BlockSpec((half, count), fixed),
            pl.BlockSpec((half, count), fixed),
            pl.BlockSpec((half, step), along),
            pl.BlockSpec((half, step), along),
            pl.BlockSpec((part, count), fixed),
            pl.BlockSpec((part, count), fixed),
            pl.BlockSpec((1, step), along),
        ],
        [
            shape_of((half, count // 2), F32),
            shape_of((part, count), F32),
            shape_of((part, count), BF16),
            shape_of((half, count), BF16),
            shape_of((half, count), BF16),
            shape_of((half, hidden), BF16),
            shape_of((half, hidden), BF16),
            shape_of((part, count), BF16),
            shape_of((part, count), BF16),
            shape_of((1, hidden), F32),
        ],
        scalars,
        [*xs, *pieces, ow, gains, up, up_c, down, down_c, bias],
        scratch=[pltpu.VMEM((half, count), F32), pltpu.VMEM((half, count), F32)],
        hbm=True,
        flops=2 * half * count * (count + 3 * hidden),
        vmem=32,
    )


def norm_back_body(sc, p0, p1, y, dy, gains, dz, sums):
    db = p0[...].astype(F32) + p1[...].astype(F32)
    yv = y[...]
    count = yv.shape[1]
    mean = jnp.sum(yv, axis=1, keepdims=True) / count
    centered = yv - mean
    rstd = lax.rsqrt(jnp.sum(centered * centered, axis=1, keepdims=True) / count + EPS_NORM)
    nhat = centered * rstd
    n = db * gains[2:3, :]
    first = jnp.sum(n, axis=1, keepdims=True) / count
    second = jnp.sum(n * nhat, axis=1, keepdims=True) / count
    dz[...] = (dy[...].astype(F32) + rstd * (n - first - nhat * second)).astype(BF16)
    sums[0:1, :] = jnp.sum(db * nhat, axis=0, keepdims=True)
    sums[1:2, :] = jnp.sum(db, axis=0, keepdims=True)


def norm_back(scalars, keep, got_x, y, dy, gains):
    rows, count = got_x.shape
    return call(
        norm_back_body,
        (1,),
        [full(v.shape) for v in (keep, got_x, y, dy, gains)],
        [
            pl.BlockSpec((rows, count), lambda i, sc: (0, 0)),
            pl.BlockSpec((2, count), lambda i, sc: (0, 0)),
        ],
        [shape_of((rows, count), BF16), shape_of((2, count), F32)],
        scalars,
        [keep, got_x, y, dy, gains],
    )


def attend_back_body(masked, sc, z0, z1, z2, z3, out_w, q, k, v, lse, grads, dz_out, dk_acc, dv_acc):
    i = pl.program_id(0)
    place = quarter(jnp.bitwise_xor(sc[0], i))

    @pl.when(i == 0)
    def _():
        dk_acc[...] = jnp.zeros_like(dk_acc)
        dv_acc[...] = jnp.zeros_like(dv_acc)

    for j, z in enumerate((z0, z1, z2, z3)):

        @pl.when(i == j)
        def _(z=z):
            dz_out[...] = z[...]

    d_mixed = dot_nt(dz_out[...], out_w[...]).astype(BF16)
    rows = d_mixed.shape[0]
    keys = k.shape[1]
    for h in range(d_mixed.shape[1] // DH):
        cols = slice(h * DH, (h + 1) * DH)
        q_h, k_h, v_h, do_h = q[0, :, cols], k[0, :, cols], v[0, :, cols], d_mixed[:, cols]
        scores = dot_nt(k_h, q_h)
        if masked:
            base = place * rows
            q_side = (base + lax.broadcasted_iota(jnp.int32, (1, rows), 1)) < sc[1]
            k_side = lax.broadcasted_iota(jnp.int32, (keys, 1), 0) < sc[1]
            scores = jnp.where(jnp.logical_xor(q_side, k_side), NEG_FILL, scores)
        p = jnp.exp(scores - lse[h])
        d_p = dot_nt(v_h, do_h)
        prod = p * d_p
        delta = jnp.sum(prod, axis=0, keepdims=True)
        d_s = (prod - p * delta).astype(BF16)
        dv_acc[:, cols] += dot_nn(p.astype(BF16), do_h)
        dk_acc[:, cols] += dot_nn(d_s, q_h)
        here = pl.ds(pl.multiple_of(place * rows, rows), rows)
        grads[here, cols] = dot_tn(d_s, k_h).astype(BF16)

    @pl.when(i == pl.num_programs(0) - 1)
    def _():
        width = dk_acc.shape[1]
        grads[:, width : 2 * width] = dk_acc[...].astype(BF16)
        grads[:, 2 * width :] = dv_acc[...].astype(BF16)


def attend_back(scalars, dzs, out_w, qkv, lse, masked):
    _, rows, width = qkv.shape
    heads = width // DH
    count = out_w.shape[1]
    tiles = rows // TILE

    def tile(i, sc):
        return (quarter(jnp.bitwise_xor(sc[0], i)), 0)

    return call(
        functools.partial(attend_back_body, masked),
        (tiles,),
        [full(dz.shape) for dz in dzs]
        + [
            full(out_w.shape),
            pl.BlockSpec((1, TILE, width), lambda i, sc: (0, tile(i, sc)[0], 0)),
            pl.BlockSpec((1, rows, width), lambda i, sc: (1, 0, 0)),
            pl.BlockSpec((1, rows, width), lambda i, sc: (2, 0, 0)),
            pl.BlockSpec((heads, 1, TILE), lambda i, sc: (0, 0, tile(i, sc)[0])),
        ],
        [
            pl.BlockSpec((rows, 3 * width), lambda i, sc: (0, 0)),
            pl.BlockSpec((TILE, count), tile),
        ],
        [shape_of((rows, 3 * width), BF16), shape_of((rows, count), BF16)],
        scalars,
        [*dzs, out_w, qkv, qkv, qkv, lse],
        scratch=[pltpu.VMEM((rows, width), F32), pltpu.VMEM((rows, width), F32)],
        hbm=True,
        flops=2 * rows * count * width + 10 * rows * rows * width,
    )


def relative(i):
    return jnp.where(i < 2, 2 * i + 1, 2 * i - 4)


def spread_body(scales, flipped, n_left, sc, *refs):
    lefts, right, send, keep = refs[:n_left], refs[n_left], refs[-2], refs[-1]
    i = pl.program_id(0)
    rows = lefts[0].shape[0]
    parts = []
    for left in lefts:
        if flipped:
            width = right.shape[2]
            total = None
            for s, scale in enumerate(scales):
                part = dot_nt(left[:, s * width : (s + 1) * width], right[s])
                part = part * scale if scale != 1.0 else part
                total = part if total is None else total + part
        else:
            total = dot_nn(left[...], right[...])
        parts.append(total.astype(BF16))

    def put(out):
        for at, part in enumerate(parts):
            out[0, at * rows : (at + 1) * rows, :] = part

    @pl.when(i < 2)
    def _():
        put(send)

    @pl.when(i >= 2)
    def _():
        put(keep)


def spread(scalars, lefts, right, n_tp, scales=None):
    flipped = scales is not None
    rows = sum(a.shape[0] for a in lefts)
    count = right.shape[1]
    width = count // n_tp

    def cols(i, sc):
        j = jnp.bitwise_xor(sc[0], relative(i))
        return (0, j, 0) if flipped else (0, j)

    block = (right.shape[0], width, right.shape[2]) if flipped else (right.shape[0], width)
    return call(
        functools.partial(spread_body, scales, flipped, len(lefts)),
        (n_tp,),
        [full(a.shape) for a in lefts] + [pl.BlockSpec(block, cols)],
        [
            pl.BlockSpec((1, rows, width), lambda i, sc: (jnp.minimum(i, 1), 0, 0)),
            pl.BlockSpec((1, rows, width), lambda i, sc: (jnp.maximum(i - 2, 0), 0, 0)),
        ],
        [shape_of((2, rows, width), BF16), shape_of((2, rows, width), BF16)],
        scalars,
        [*lefts, right],
        hbm=True,
        flops=2 * rows * lefts[0].shape[1] * count,
    )


def out_body(n_left, sc, *refs):
    lefts, right, right_c, send, keep = refs[:n_left], *refs[n_left:]
    i = pl.program_id(0)
    rows, near = lefts[0].shape[0], right.shape[0]
    parts = [
        (dot_nn(left[:, :near], right[...]) + dot_nn(left[:, near:], right_c[...])).astype(BF16)
        for left in lefts
    ]
    for step, out in enumerate((send, keep)):

        @pl.when(i == step)
        def _(out=out):
            for at, part in enumerate(parts):
                out[at * rows : (at + 1) * rows, :] = part


def out_product(scalars, lefts, right, right_c):
    rows = sum(a.shape[0] for a in lefts)
    hidden, count = right.shape

    def cols(i, sc):
        side = jnp.right_shift(sc[0], 1)
        return (0, jnp.where(i == 0, 1 - side, side))

    return call(
        functools.partial(out_body, len(lefts)),
        (2,),
        [full(a.shape) for a in lefts] + [pl.BlockSpec((hidden, count // 2), cols)] * 2,
        [pl.BlockSpec((rows, count // 2), lambda i, sc: (0, 0))] * 2,
        [shape_of((rows, count // 2), BF16)] * 2,
        scalars,
        [*lefts, right, right_c],
        cost=1e11,
        hbm=True,
        flops=4 * rows * hidden * count,
    )


def pair_grad_body(sc, a0, a1, b0, b1, send, keep):
    i = pl.program_id(0)
    low = (dot_tn(a0[...], b0[...]) + dot_tn(a1[...], b1[...])).astype(BF16)
    for step, out in enumerate((send, keep)):

        @pl.when(i == step)
        def _(out=out):
            out[...] = low


def pair_grad(scalars, lefts, rights, split_left):
    rows = lefts[0].shape[0]
    halved = lambda i, sc: (0, 1 - i)
    m = lefts[0].shape[1] // (2 if split_left else 1)
    count = rights[0].shape[1] // (1 if split_left else 2)
    left = pl.BlockSpec((rows, m), halved) if split_left else full((rows, m))
    right = full((rows, count)) if split_left else pl.BlockSpec((rows, count), halved)
    return call(
        pair_grad_body,
        (2,),
        [left, left, right, right],
        [pl.BlockSpec((m, count), lambda i, sc: (0, 0))] * 2,
        [shape_of((m, count), BF16)] * 2,
        scalars,
        [*lefts, *rights],
        hbm=True,
        flops=8 * rows * m * count,
        vmem=32,
    )


def norm_sums_body(sc, da, x, stats, gain, moments, sums):
    d = da[...].astype(F32)
    nhat = (x[...].astype(F32) - stats[:, 0:1]) * stats[:, 1:2]
    n = d * gain[...]
    prod = d * nhat
    rows = d.shape[0]
    for at, v in enumerate((n, n * nhat)):
        total = jnp.broadcast_to(jnp.sum(v, axis=1, keepdims=True), (rows, 128))
        moments[at : at + 1, :] = jnp.transpose(total)[0:1, :]
    sums[0:1, :] = jnp.sum(prod, axis=0, keepdims=True)
    sums[1:2, :] = jnp.sum(d, axis=0, keepdims=True)


def norm_sums(scalars, da, x, stats, gain):
    rows, width = da.shape
    return call(
        norm_sums_body,
        (1,),
        [full(v.shape) for v in (da, x, stats, gain)],
        [pl.BlockSpec((2, rows), lambda i, sc: (0, 0)), pl.BlockSpec((2, width), lambda i, sc: (0, 0))],
        [shape_of((2, rows), F32), shape_of((2, width), F32)],
        scalars,
        [da, x, stats, gain],
    )


def attn_grad_body(sc, a0, a1, z0, z1, d0, d1, o0, o1, send, keep):
    i = pl.program_id(0)
    wide = d0.shape[1]
    low1 = (dot_tn(a0[...], d0[...]) + dot_tn(a1[...], d1[...])).astype(BF16)
    low2 = (dot_tn(z0[...], o0[...]) + dot_tn(z1[...], o1[...])).astype(BF16)
    for step, out in enumerate((send, keep)):

        @pl.when(i == step)
        def _(out=out):
            out[:, :wide] = low1
            out[:, wide:] = low2


def attn_grad(scalars, acts, dzs, grads, mixed, bit):
    rows, m = acts[0].shape
    count = grads[0].shape[1] + mixed[0].shape[1]

    def index(i, sc):
        mine = jnp.bitwise_and(jnp.right_shift(sc[2], bit), 1)
        return (0, jnp.where(i == 0, 1 - mine, mine))

    return call(
        attn_grad_body,
        (2,),
        [pl.BlockSpec((rows, m // 2), index)] * 4 + [full(v.shape) for v in (*grads, *mixed)],
        [pl.BlockSpec((m // 2, count), lambda i, sc: (0, 0))] * 2,
        [shape_of((m // 2, count), BF16)] * 2,
        scalars,
        [*acts, *dzs, *grads, *mixed],
        hbm=True,
        flops=4 * rows * m * count,
        vmem=32,
    )


def place_body(blocks, sc, first, second, out):
    rows = first.shape[0] * 2 // blocks
    half = blocks // 2
    for k in range(blocks):
        src = first if k < half else second
        at = (k if k < half else k - half) * rows
        to = pl.ds(pl.multiple_of(jnp.bitwise_xor(sc[0], k) * rows, rows), rows)
        out[to, :] = src[at : at + rows, :].astype(F32)


def place(index, first, second, blocks, width):
    m, count = first.shape[0] * 2, first.shape[1]
    half = pl.BlockSpec((m // 2, width), lambda i, sc: (0, i))
    return call(
        functools.partial(place_body, blocks),
        (count // width,),
        [half, half],
        pl.BlockSpec((m, width), lambda i, sc: (0, i)),
        shape_of((m, count), F32),
        index,
        [first, second],
    )


def unpack_body(scale, blocks, sc, first, second, d_qkv, d_out):
    i = pl.program_id(0)
    n = pl.num_programs(0) - 1
    rows = first.shape[0] * 2 // blocks
    half = blocks // 2

    def each(put):
        for k in range(blocks):
            src = first if k < half else second
            at = (k if k < half else k - half) * rows
            to = pl.ds(pl.multiple_of(jnp.bitwise_xor(sc[0], k) * rows, rows), rows)
            put(to, src[at : at + rows, :].astype(F32))

    def scaled(to, value):
        d_qkv[0, to, :] = value * jnp.where(i == 0, jnp.float32(scale), jnp.float32(1.0))

    def turned(to, value):
        d_out[:, to] = jnp.transpose(value)

    @pl.when(i < n)
    def _():
        each(scaled)

    @pl.when(i == n)
    def _():
        each(turned)


def unpack(index, first, second, blocks, width, scale):
    m, count = first.shape[0] * 2, first.shape[1]
    n = count // width - 1
    return call(
        functools.partial(unpack_body, scale, blocks),
        (n + 1,),
        [pl.BlockSpec((m // 2, width), lambda i, sc: (0, i))] * 2,
        [
            pl.BlockSpec((1, m, width), lambda i, sc: (jnp.minimum(i, n - 1), 0, 0)),
            pl.BlockSpec((width, m), lambda i, sc: (0, 0)),
        ],
        [shape_of((n, m, width), F32), shape_of((width, m), F32)],
        index,
        [first, second],
    )


def halve_body(bit, sc, keep, got, send, nxt):
    half = send.shape[0]
    mine = jnp.bitwise_and(jnp.right_shift(sc[2], bit), 1)
    for out, side in ((send, 1 - mine), (nxt, mine)):
        rows = pl.ds(pl.multiple_of(side * half, half), half)
        out[...] = (keep[rows, :].astype(F32) + got[rows, :].astype(F32)).astype(BF16)


def halve(scalars, keep, got, bit):
    shape = shape_of((keep.shape[0] // 2, keep.shape[1]), BF16)
    return call(
        functools.partial(halve_body, bit),
        (1,),
        [full(keep.shape)] * 2,
        [pl.BlockSpec(shape.shape, lambda i, sc: (0, 0))] * 2,
        [shape] * 2,
        scalars,
        [keep, got],
    )


def join_body(added, sc, a, c, out):
    rows = a.shape[0]
    if added:
        out[...] = (a[...].astype(F32) + c[...].astype(F32)).astype(BF16)
    else:
        out[:rows, :] = a[...]
        out[rows:, :] = c[...]


def join(scalars, first, second, added):
    shape = shape_of((first.shape[0] * (1 if added else 2), first.shape[1]), BF16)
    return call(
        functools.partial(join_body, added),
        (1,),
        [full(first.shape)] * 2,
        pl.BlockSpec(shape.shape, lambda i, sc: (0, 0)),
        shape,
        scalars,
        [first, second],
    )


def place_of_largest(lens, half):
    count = lens.shape[1]
    start, border, before = jnp.int32(0), jnp.int32(0), jnp.int32(0)
    for i in range(count):
        big = lens[0, i] == half
        start = jnp.where(big, before, start)
        border = jnp.where(big, lens[0, (i + 1) % count], border)
        before = before + lens[0, i]
    return start, border


def turn_body(half, lens, here, x, *outs):
    start, border = place_of_largest(lens, half)
    rows = x.shape[0]
    turned = pltpu.roll(x[...].astype(F32), lax.rem(rows - start, rows), 0).astype(BF16)
    if len(outs) == 1:
        outs[0][...] = turned
        return
    first, second, out = outs
    first[...] = turned[:half]
    second[...] = turned[half:]
    out[0] = here[0]
    out[1] = border
    out[2] = here[1]
    out[3] = start


def turn(lengths, here, x, half, split):
    smem = pl.BlockSpec(memory_space=pltpu.SMEM)
    vmem = pl.BlockSpec(memory_space=pltpu.VMEM)
    piece = shape_of((half, x.shape[1]), BF16)
    if split:
        out_specs, out_shape = [vmem, vmem, smem], [piece, piece, shape_of((4,), jnp.int32)]
    else:
        out_specs, out_shape = [vmem], [shape_of(x.shape, BF16)]
    return pl.pallas_call(
        functools.partial(turn_body, half),
        in_specs=[smem, smem, vmem],
        out_specs=out_specs,
        out_shape=out_shape,
        compiler_params=pltpu.CompilerParams(vmem_limit_bytes=16 * MIB),
    )(lengths, here, x)


class Chain:
    def __init__(self):
        self.last = ()

    def tie(self, value, *need):
        return lax.optimization_barrier((value, need, self.last))[0]

    def do(self, fn, *args, **keywords):
        leaves, tree = jax.tree_util.tree_flatten(args)
        arrays = iter(self.tie([v for v in leaves if isinstance(v, jax.Array)]))
        leaves = [next(arrays) if isinstance(v, jax.Array) else v for v in leaves]
        out = fn(*jax.tree_util.tree_unflatten(tree, leaves), **keywords)
        self.last = jax.tree_util.tree_leaves(out)[0]
        return out


class RowSum:
    def __init__(self, chain, scalars, r, n_rows, order, pair, core_flip=None):
        self.chain, self.scalars, self.r, self.n_rows = chain, scalars, r, n_rows
        self.order, self.depth = order, len(order)
        self.rest = [b for b in range(n_rows.bit_length() - 1) if b not in order]
        send, self.keep = pair
        self.at = 0 if core_flip is None else -1
        self.got = self.flip(send, order[0]) if core_flip is None else core_flip(send)

    def flip(self, value, bit):
        return lax.ppermute(value, "rows", [(i, i ^ (1 << bit)) for i in range(self.n_rows)])

    def step(self):
        do = self.chain.do
        if self.at < self.depth:
            self.at += 1
            if self.at < self.depth:
                bit = self.order[self.at]
                send, self.keep = do(halve, self.scalars, self.keep, self.got, bit)
                self.got = self.flip(send, bit)
                return
            self.buf = do(join, self.scalars, self.keep, self.got, True)
            for b in self.rest:
                self.buf = do(join, self.scalars, self.buf, self.flip(self.buf, b), True)
            self.left = self.depth - 1
        else:
            self.left -= 1
            self.buf = do(join, self.scalars, self.buf, self.got, False)
        self.got = self.flip(self.buf, self.order[self.left])

    def finish(self, fn, *args):
        index = 0
        for b in self.order:
            index = index * 2 + jnp.bitwise_and(jnp.right_shift(self.r, b), 1)
        index = jnp.stack([index, index]).astype(jnp.int32)
        return self.chain.do(fn, index, self.buf, self.got, 1 << self.depth, *args)


def local(
    n_tp, n_rows,
    datapoints, lengths, qkv_weight, out_weight, up_weight, up_bias, down_weight, down_bias,
    gain_one, shift_one, gain_two, shift_two, grad_out,
):
    tok, width = datapoints.shape
    count = n_tp * width
    half = tok // 2
    q_scale = DH ** (-0.5)
    t, r = lax.axis_index("tp"), lax.axis_index("rows")
    chain = Chain()
    do, tie = chain.do, chain.tie

    def core_flip(v):
        return lax.ppermute(v, "tp", [(i, i ^ 1) for i in range(n_tp)])

    def x_flip(v):
        return lax.ppermute(v, "tp", [(i, i ^ 2) for i in range(n_tp)])

    def diag_flip(v):
        return lax.ppermute(v, "tp", [(i, i ^ 3) for i in range(n_tp)])

    def row_flip(v, b):
        return lax.ppermute(v, "rows", [(i, i ^ (1 << b)) for i in range(n_rows)])

    ow = lax.all_gather(out_weight, "tp", axis=0, tiled=True)
    vectors = jnp.concatenate([gain_one, shift_one, gain_two, shift_two, down_bias])
    vec_x = x_flip(vectors)
    vec_c = core_flip(jnp.concatenate([vectors, up_bias]))
    here = jnp.stack([t, r]).astype(jnp.int32)
    x0, x1, scalars = do(turn, lengths, here, datapoints, half, True)
    start = scalars[3]
    x0_x, x0_c = x_flip(x0), core_flip(x0)
    d_down_bias = do(lambda v: jnp.sum(v.astype(F32), axis=0), grad_out)
    vec_d = core_flip(tie(vec_x))
    n_vec = vectors.shape[0] // width

    def relative_vectors(*pieces):
        return jnp.stack([p[: n_vec * width].reshape(n_vec, width) for p in pieces])

    def vector_orders(rel, vec_c):
        order = jnp.bitwise_xor(t, jnp.arange(n_tp))
        bias = jnp.concatenate([up_bias, vec_c[n_vec * width :]]).reshape(1, -1)
        return jnp.transpose(rel[order], (1, 0, 2)).reshape(n_vec, count), bias

    weight4 = qkv_weight.reshape(3, n_tp, width, width)
    gains_rel = do(relative_vectors, vectors, vec_c, vec_x, vec_d)
    x0_d = core_flip(x0_x)
    x1 = tie(x1, x0_x)
    x1_x, x1_c = x_flip(x1), core_flip(x1)
    (dy,) = do(turn, lengths, here, grad_out, half, False)
    wide = tie((up_weight, down_weight), x0_x)
    up_c, down_c = core_flip(wide[0]), core_flip(wide[1])
    xs = [[x0, x0_c, x0_x, x0_d], None]
    qkv, acts, stats, mixed, lse, pieces = [[None] * 2 for _ in range(6)]

    def first(h):
        qkv[h], acts[h], stats[h], mixed[h], lse[h], other, mine = do(
            first_layer, scalars, xs[h], dy, gains_rel, weight4, h
        )
        pieces[h] = [mine, core_flip(other), x_flip(mine), diag_flip(other)]

    first(0)
    x1_d = core_flip(tie(x1_x, up_c, down_c))
    xs[1] = [x1, x1_c, x1_x, x1_d]
    first(1)
    gains, bias2 = do(vector_orders, gains_rel, vec_c)

    weights = [ow, gains, up_weight, up_c, down_weight, down_c, bias2]
    fed0 = do(feed, scalars, xs[0], pieces[0], *weights)
    db0_x = x_flip(fed0[7])
    fed1 = do(feed, scalars, xs[1], pieces[1], *weights)
    db1_x = x_flip(fed1[7])
    y_cols, b, dyn, g, du = [[fed0[k], fed1[k]] for k in (0, 3, 4, 5, 6)]
    def row_sum(order, pair, *core):
        return RowSum(chain, scalars, r, n_rows, order, pair, *core)

    def spread_rows(v):
        return [v, core_flip(v), x_flip(v), diag_flip(v)]

    dz0, sums0 = do(norm_back, scalars, fed0[8], db0_x, fed0[1], fed0[2], gains)
    dzs0 = spread_rows(dz0)
    up = row_sum([1, 0, 2], do(pair_grad, scalars, b, du, False), core_flip)
    down = row_sum([0, 1, 2], do(pair_grad, scalars, g, dyn, True), core_flip)
    dz1, sums1 = do(
        norm_back, scalars, fed1[8], tie(db1_x, dzs0), fed1[1], fed1[2], gains
    )
    dzs1 = spread_rows(dz1)
    hidden = up_bias.shape[0]
    up.step()
    down.step()

    grads0, dzn0 = do(attend_back, scalars, dzs0, out_weight, qkv[0], lse[0], False)
    grads1, dzn1 = do(attend_back, scalars, dzs1, out_weight, qkv[1], lse[1], True)
    up.step()
    down.step()
    attn = row_sum(
        [0, 1, 2],
        do(attn_grad, scalars, acts, [dzn0, dzn1], [grads0, grads1], mixed, 0),
    )
    up.step()
    down.step()

    def middle(keep, got):
        return (keep[1].astype(F32) + got[1].astype(F32)).astype(BF16)

    def total_of(keep, got, got_x):
        return keep[0].astype(F32) + got[0].astype(F32) + got_x.astype(F32)

    send, keep_a = do(spread, scalars, [grads0, grads1], qkv_weight, n_tp, (q_scale, 1.0, 1.0))
    got_a = core_flip(send)
    out_send, out_keep = do(out_product, scalars, g, down_weight, down_c)
    da_x = x_flip(do(middle, keep_a, got_a))
    attn.step()
    up.step()
    down.step()
    bias_grad = do(jnp.add, fed0[9], fed1[9])
    attn.step()
    gain_row = gain_one.reshape(1, -1)

    def joined(*parts):
        return total_of(*parts).astype(BF16)

    da = do(joined, keep_a, got_a, da_x)
    out_x = x_flip(tie(out_send))
    up.step()
    down.step()
    m0, ones0 = do(norm_sums, scalars, da[:half], x0, stats[0], gain_row)
    m1, ones1 = do(norm_sums, scalars, da[half:], x1, stats[1], gain_row)
    attn.step()
    m = do(lambda a, b, *c: jnp.concatenate([a + b, *c], 0), sums0, sums1, m0, m1)
    m_c = core_flip(m)
    bias_got = core_flip(bias_grad[:, hidden:])
    up.step()
    down.step()
    m = do(jnp.add, m, m_c)
    m_x = x_flip(m)
    attn.step()
    c, side = jnp.bitwise_and(t, 1), jnp.right_shift(t, 1)

    def output_rows(keep, got, y0, y1, vecs):
        wide = 2 * width
        extra = lax.dynamic_slice_in_dim(vecs[4], side * wide, wide, 0)
        total = keep.astype(F32) + got.astype(F32) + jnp.concatenate([y0, y1], 0) + extra
        low = total.astype(BF16)
        return (
            lax.dynamic_slice_in_dim(low, (1 - c) * width, width, 1),
            lax.dynamic_slice_in_dim(low, c * width, width, 1),
        )

    rows_send, rows_keep = do(output_rows, out_keep, out_x, *y_cols, gains)
    rows_got = core_flip(rows_send)

    def unroll(first, second):
        thrice = jnp.concatenate([second, first, second], 0)
        return lax.dynamic_slice_in_dim(thrice, half - start, tok, 0)

    def output_of(mine, other):
        part = half // 2
        halves = []
        for h in range(2):
            a, b = mine[h * part : (h + 1) * part], other[h * part : (h + 1) * part]
            halves.append(
                jnp.where(c == 0, jnp.concatenate([a, b], 0), jnp.concatenate([b, a], 0))
            )
        return unroll(*halves)

    m = do(jnp.add, m, m_x)

    def small_of(up_b, down_b, m, ones0, ones1):
        two = lax.dynamic_slice_in_dim(m[:2], t * width, width, 1)
        return jnp.concatenate(
            [up_b.reshape(-1), down_b, (ones0 + ones1).reshape(-1), two.reshape(-1)]
        ).reshape(-1, 128)

    d_up_bias = bias_grad[:, :hidden] + bias_got
    small = do(small_of, d_up_bias, d_down_bias, m, ones0, ones1)
    bits = list(range(n_rows.bit_length() - 1))
    small_got = row_flip(small, bits[0])

    def d_input_of(m, da, *parts):
        halves = []
        for h, (x, stat, dzn) in enumerate((parts[:3], parts[3:])):
            nhat = (x.astype(F32) - stat[:, 0:1]) * stat[:, 1:2]
            first, second = m[2 + 2 * h][:, None] / count, m[3 + 2 * h][:, None] / count
            dz = lax.dynamic_slice_in_dim(dzn, t * width, width, 1).astype(F32)
            n = da[h * half : (h + 1) * half].astype(F32) * gain_one
            halves.append(dz + stat[:, 1:2] * (n - first - nhat * second))
        return unroll(*halves)

    attn.step()
    small = do(jnp.add, small, small_got)
    small_got = row_flip(small, bits[1])
    d_input = do(d_input_of, m, da, x0, stats[0], dzn0, x1, stats[1], dzn1)
    output = do(output_of, rows_keep, rows_got)
    d_down = down.finish(place, width)
    d_up = up.finish(place, width)
    for bit in bits[2:]:
        small = do(jnp.add, small, small_got)
        small_got = row_flip(small, bit)
    small = do(jnp.add, small, small_got).reshape(-1)
    d_qkv, d_out = attn.finish(unpack, width, q_scale)
    d_down_bias, d_gain_one, d_shift_one, d_gain_two, d_shift_two = small[hidden:].reshape(5, width)
    return (
        output, d_input, d_qkv, d_out, d_up, small[:hidden],
        d_down, d_down_bias, d_gain_one, d_shift_one, d_gain_two, d_shift_two,
    )


def solution(mesh):
    grid = P("rows", "tp")
    placed = (
        grid, P("rows", None), P(None, None, "tp"), P("tp", None), P(None, "tp"), P("tp"),
        P("tp", None), P("tp"), P("tp"), P("tp"), P("tp"), P("tp"), grid,
    )
    return jax.shard_map(
        functools.partial(local, mesh.shape["tp"], mesh.shape["rows"]),
        mesh=mesh,
        in_specs=placed,
        out_specs=(
            grid, grid, P(None, None, "tp"), P("tp", None), P(None, "tp"), P("tp"),
            P("tp", None), P("tp"), P("tp"), P("tp"), P("tp"), P("tp"),
        ),
        check_vma=False,
    )
```

```python
import functools

import jax
import jax.numpy as jnp
from jax import lax
from jax.experimental import pallas as pl
from jax.experimental.pallas import tpu as pltpu
from jax.sharding import PartitionSpec as P

DH = 128
TILE = 256
EPS_NORM = 1e-05
NEG_FILL = -1e30
F32 = jnp.float32
BF16 = jnp.bfloat16
MIB = 1024 * 1024
COST = 8.0
GELU_C = 0.7978845608028654


def dot_nn(a, b):
    return jnp.dot(a, b, preferred_element_type=F32)


def dot_nt(a, b):
    return lax.dot_general(a, b, (((1,), (1,)), ((), ())), preferred_element_type=F32)


def dot_tn(a, b):
    return lax.dot_general(a, b, (((0,), (0,)), ((), ())), preferred_element_type=F32)


def call(body, grid, in_specs, out_specs, out_shape, scalars, operands, scratch=(), flops=0, vmem=24, hbm=False, cost=2e10):
    bytes_moved = sum(o.size * o.dtype.itemsize for o in operands)
    bytes_moved += sum(
        o.size * jnp.dtype(o.dtype).itemsize for o in jax.tree_util.tree_leaves(out_shape)
    )
    operands = [
        pltpu.with_memory_space_constraint(o, pltpu.HBM) if hbm else o for o in operands
    ]
    if hbm:
        out_shape = jax.tree_util.tree_map(lambda o: pltpu.HBM(o.shape, o.dtype), out_shape)
    return pl.pallas_call(
        body,
        grid_spec=pltpu.PrefetchScalarGridSpec(
            num_scalar_prefetch=1,
            grid=grid,
            in_specs=in_specs,
            out_specs=out_specs,
            scratch_shapes=list(scratch),
        ),
        out_shape=out_shape,
        compiler_params=pltpu.CompilerParams(
            vmem_limit_bytes=vmem * MIB,
            dimension_semantics=("arbitrary",) * len(grid),
        ),
        cost_estimate=pl.CostEstimate(
            flops=int(cost), bytes_accessed=int(bytes_moved), transcendentals=0
        ),
    )(scalars, *operands)


def full(shape):
    zeros = (0,) * len(shape)
    return pl.BlockSpec(shape, lambda *_: zeros, pipeline_mode=pl.Buffered(1))


def shape_of(shape, dtype):
    return jax.ShapeDtypeStruct(shape, dtype)


def far_first(i, n, sc):
    c = jnp.bitwise_and(sc[0], 1)
    return jnp.where(i < n // 2, (1 - c) * (n // 2) + i, c * (n // 2) + i - n // 2)


def first_body(
    masked, tile, sc, x0, x1, x2, x3, dy_other, dy_mine, gains, weight,
    qkv, acts, stats, o, lse, other, mine, q_all, k_all, v_all,
):
    t = sc[0]
    i = pl.program_id(0)
    n = pl.num_programs(0) // 2

    @pl.when(i == 0)
    def _():
        rows = dy_mine.shape[0]
        other[rows:, :] = dy_other[...]
        mine[rows:, :] = dy_mine[...]

    @pl.when(i < n)
    def _():
        pieces = [x[...].astype(F32) for x in (x0, x1, x2, x3)]
        width = pieces[0].shape[1]
        count = width * len(pieces)
        mean = sum(jnp.sum(x, axis=1, keepdims=True) for x in pieces) / count
        centered = [x - mean for x in pieces]
        var = sum(jnp.sum(c * c, axis=1, keepdims=True) for c in centered) / count
        rstd = lax.rsqrt(var + EPS_NORM)
        total = [0.0, 0.0, 0.0]
        for k, c in enumerate(centered):
            j = jnp.bitwise_xor(t, k)
            part = (c * rstd * gains[k, 0:1, :] + gains[k, 1:2, :]).astype(BF16)
            acts[:, pl.ds(pl.multiple_of(j * width, width), width)] = part
            for s in range(3):
                total[s] = total[s] + dot_nn(part, weight[s, j])
        rows = pl.ds(pl.multiple_of(i * tile, tile), tile)
        for s, (value, kept) in enumerate(zip(total, (q_all, k_all, v_all))):
            low = (value * (DH ** (-0.5)) if s == 0 else value).astype(BF16)
            qkv[s] = low
            kept[rows, :] = low
        stats[:, 0:1] = mean
        stats[:, 1:2] = rstd

    @pl.when(i >= n)
    def _():
        cols = k_all.shape[0]
        first = far_first(i - n, n, sc) * tile
        rows = pl.ds(pl.multiple_of(first, tile), tile)
        if masked:
            q_side = (first + lax.broadcasted_iota(jnp.int32, (tile, 1), 0)) < sc[1]
            k_side = lax.broadcasted_iota(jnp.int32, (1, cols), 1) < sc[1]
            apart = jnp.logical_xor(q_side, k_side)
        for h in range(q_all.shape[1] // DH):
            part = slice(h * DH, (h + 1) * DH)
            scores = dot_nt(q_all[rows, part], k_all[:, part])
            if masked:
                scores = jnp.where(apart, NEG_FILL, scores)
            top = jnp.max(scores, axis=1, keepdims=True)
            weights = jnp.exp(scores - top)
            total = jnp.sum(weights, axis=1, keepdims=True)
            mixed = dot_nn(weights.astype(BF16), v_all[:, part])
            low = (mixed / total).astype(BF16)
            o[:, part] = low
            to = lax.rem(i, n // 2) * tile
            to = pl.ds(pl.multiple_of(to, tile), tile)

            @pl.when(i < n + n // 2)
            def _():
                other[to, part] = low

            @pl.when(i >= n + n // 2)
            def _():
                mine[to, part] = low

            stat = jnp.broadcast_to(top + jnp.log(total), (tile, DH))
            lse[h] = jnp.transpose(stat)[0:1, :]


def first_layer(scalars, pieces, dy, gains, weight4, h):
    rows, width = pieces[0].shape
    n = len(pieces)
    heads = width // DH
    tile = 256
    steps = rows // tile

    def early(i, sc):
        return (jnp.minimum(i, steps - 1), 0)

    def late(i, sc):
        return far_first(jnp.maximum(i - steps, 0), steps, sc)

    def rows_of(mine):
        def index(i, sc):
            c = jnp.bitwise_and(sc[0], 1)
            return (2 * h + (c if mine else 1 - c), 0)

        return pl.BlockSpec((rows // 2, width), index, pipeline_mode=pl.Buffered(1))

    whole = pl.BlockSpec((rows, width), lambda i, sc: (0, 0))

    return call(
        functools.partial(first_body, h == 1, tile),
        (2 * steps,),
        [pl.BlockSpec((tile, width), early)] * n
        + [rows_of(False), rows_of(True), full(gains.shape), full(weight4.shape)],
        [
            pl.BlockSpec((3, tile, width), lambda i, sc: (0, jnp.minimum(i, steps - 1), 0)),
            pl.BlockSpec((tile, n * width), early),
            pl.BlockSpec((tile, 2), early),
            pl.BlockSpec((tile, width), lambda i, sc: (late(i, sc), 0)),
            pl.BlockSpec((heads, 1, tile), lambda i, sc: (0, 0, late(i, sc))),
            whole,
            whole,
        ],
        [
            shape_of((3, rows, width), BF16),
            shape_of((rows, n * width), BF16),
            shape_of((rows, 2), F32),
            shape_of((rows, width), BF16),
            shape_of((heads, 1, rows), F32),
            shape_of((rows, width), BF16),
            shape_of((rows, width), BF16),
        ],
        scalars,
        [*pieces, dy, dy, gains, weight4],
        scratch=[pltpu.VMEM((rows, width), BF16)] * 3,
        hbm=True,
        flops=2 * rows * n * width * 3 * width + 4 * rows * rows * width,
    )


def quarter(u):
    return 2 * jnp.bitwise_and(u, 1) + jnp.right_shift(u, 1)


def feed_body(
    sc, x0, x1, x2, x3, p0, p1, p2, p3, ow, gains, up, up_c, down, down_c, bias,
    y_cols, y_rows, dy_rows, b_out, dy_out, g_out, du_out, send, keep, bias_grad, y_acc, total,
):
    t = sc[0]
    i = pl.program_id(0)
    side = jnp.right_shift(t, 1)
    xs, ps = (x0, x1, x2, x3), (p0, p1, p2, p3)
    rows, width = x0.shape
    n = len(xs)
    count = n * width

    @pl.when(i == 0)
    def _():
        def block(k):
            j = jnp.bitwise_xor(t, k)
            return pl.ds(pl.multiple_of(j * width, width), width)

        for k in range(n):
            y_acc[:, block(k)] = xs[k][...].astype(F32)
            dy_out[:, block(k)] = ps[k][rows:, :]
        y = y_acc[...]
        for k in range(n):
            y = y + dot_nn(ps[k][:rows, :], ow[block(k), :])
        y_acc[...] = y
        mean = jnp.sum(y, axis=1, keepdims=True) / count
        centered = y - mean
        rstd = lax.rsqrt(jnp.sum(centered * centered, axis=1, keepdims=True) / count + EPS_NORM)
        b_out[...] = (centered * rstd * gains[2:3, :] + gains[3:4, :]).astype(BF16)
        total[...] = jnp.zeros_like(total)
        wide = y_cols.shape[1]
        y_cols[...] = y_acc[:, pl.ds(pl.multiple_of(side * wide, wide), wide)]
        part = y_rows.shape[0]
        mine = pl.ds(pl.multiple_of(side * part, part), part)
        y_rows[...] = y_acc[mine, :]
        dy_rows[...] = dy_out[mine, :]

    def chunk(up, down):
        u = dot_nn(b_out[...], up[...]) + bias[...]
        dh = dot_nt(dy_out[...], down[...])
        square = u * u
        half = 0.5 + 0.5 * jnp.tanh(u * (GELU_C + (GELU_C * 0.044715) * square))
        g_out[...] = (u * half).astype(BF16)
        inner = u * (2 * GELU_C + (6 * 0.044715 * GELU_C) * square)
        du = (dh * (half + (half - half * half) * inner)).astype(BF16)
        du_out[...] = du
        bias_grad[...] = jnp.sum(du.astype(F32), axis=0, keepdims=True)
        total[...] += dot_nt(du, up[...])

    steps = pl.num_programs(0)

    @pl.when(i < steps // 2)
    def _():
        chunk(up, down)

    @pl.when(i >= steps // 2)
    def _():
        chunk(up_c, down_c)

    @pl.when(i == pl.num_programs(0) - 1)
    def _():
        part = send.shape[0]
        for out, at in ((send, 1 - side), (keep, side)):
            out[...] = total[pl.ds(pl.multiple_of(at * part, part), part), :].astype(BF16)


def feed(scalars, xs, pieces, ow, gains, up, up_c, down, down_c, bias):
    rows, width = xs[0].shape
    n = len(xs)
    count = n * width
    step = 512
    near = up.shape[1] // step
    hidden = 2 * up.shape[1]
    half = rows // 2
    part = half // 2

    def own(i):
        return jnp.minimum(i, near - 1)

    def other(i):
        return jnp.maximum(i - near, 0)

    def mine(i, sc):
        return (jnp.bitwise_and(sc[0], 1), 0)

    def fixed(i, sc):
        return (0, 0)

    def along(i, sc):
        return (0, i)

    return call(
        feed_body,
        (hidden // step,),
        [pl.BlockSpec((half, width), mine, pipeline_mode=pl.Buffered(1))] * n
        + [full(p.shape) for p in pieces]
        + [full(ow.shape), full(gains.shape)]
        + [
            pl.BlockSpec((count, step), lambda i, sc: (0, own(i))),
            pl.BlockSpec((count, step), lambda i, sc: (0, other(i))),
            pl.BlockSpec((step, count), lambda i, sc: (own(i), 0)),
            pl.BlockSpec((step, count), lambda i, sc: (other(i), 0)),
            pl.BlockSpec((1, step), along),
        ],
        [
            pl.BlockSpec((half, count // 2), fixed),
            pl.BlockSpec((part, count), fixed),
            pl.BlockSpec((part, count), fixed),
            pl.BlockSpec((half, count), fixed),
            pl.BlockSpec((half, count), fixed),
            pl.BlockSpec((half, step), along),
            pl.BlockSpec((half, step), along),
            pl.BlockSpec((part, count), fixed),
            pl.BlockSpec((part, count), fixed),
            pl.BlockSpec((1, step), along),
        ],
        [
            shape_of((half, count // 2), F32),
            shape_of((part, count), F32),
            shape_of((part, count), BF16),
            shape_of((half, count), BF16),
            shape_of((half, count), BF16),
            shape_of((half, hidden), BF16),
            shape_of((half, hidden), BF16),
            shape_of((part, count), BF16),
            shape_of((part, count), BF16),
            shape_of((1, hidden), F32),
        ],
        scalars,
        [*xs, *pieces, ow, gains, up, up_c, down, down_c, bias],
        scratch=[pltpu.VMEM((half, count), F32), pltpu.VMEM((half, count), F32)],
        hbm=True,
        flops=2 * half * count * (count + 3 * hidden),
        vmem=32,
    )


def norm_back_body(sc, p0, p1, y, dy, gains, dz, sums):
    db = p0[...].astype(F32) + p1[...].astype(F32)
    yv = y[...]
    count = yv.shape[1]
    mean = jnp.sum(yv, axis=1, keepdims=True) / count
    centered = yv - mean
    rstd = lax.rsqrt(jnp.sum(centered * centered, axis=1, keepdims=True) / count + EPS_NORM)
    nhat = centered * rstd
    n = db * gains[2:3, :]
    first = jnp.sum(n, axis=1, keepdims=True) / count
    second = jnp.sum(n * nhat, axis=1, keepdims=True) / count
    dz[...] = (dy[...].astype(F32) + rstd * (n - first - nhat * second)).astype(BF16)
    sums[0:1, :] = jnp.sum(db * nhat, axis=0, keepdims=True)
    sums[1:2, :] = jnp.sum(db, axis=0, keepdims=True)


def norm_back(scalars, keep, got_x, y, dy, gains):
    rows, count = got_x.shape
    return call(
        norm_back_body,
        (1,),
        [full(v.shape) for v in (keep, got_x, y, dy, gains)],
        [
            pl.BlockSpec((rows, count), lambda i, sc: (0, 0)),
            pl.BlockSpec((2, count), lambda i, sc: (0, 0)),
        ],
        [shape_of((rows, count), BF16), shape_of((2, count), F32)],
        scalars,
        [keep, got_x, y, dy, gains],
    )


def attend_back_body(masked, sc, z0, z1, z2, z3, out_w, q, k, v, lse, grads, dz_out, dk_acc, dv_acc):
    i = pl.program_id(0)
    place = quarter(jnp.bitwise_xor(sc[0], i))

    @pl.when(i == 0)
    def _():
        dk_acc[...] = jnp.zeros_like(dk_acc)
        dv_acc[...] = jnp.zeros_like(dv_acc)

    for j, z in enumerate((z0, z1, z2, z3)):

        @pl.when(i == j)
        def _(z=z):
            dz_out[...] = z[...]

    d_mixed = dot_nt(dz_out[...], out_w[...]).astype(BF16)
    rows = d_mixed.shape[0]
    keys = k.shape[1]
    for h in range(d_mixed.shape[1] // DH):
        cols = slice(h * DH, (h + 1) * DH)
        q_h, k_h, v_h, do_h = q[0, :, cols], k[0, :, cols], v[0, :, cols], d_mixed[:, cols]
        scores = dot_nt(k_h, q_h)
        if masked:
            base = place * rows
            q_side = (base + lax.broadcasted_iota(jnp.int32, (1, rows), 1)) < sc[1]
            k_side = lax.broadcasted_iota(jnp.int32, (keys, 1), 0) < sc[1]
            scores = jnp.where(jnp.logical_xor(q_side, k_side), NEG_FILL, scores)
        p = jnp.exp(scores - lse[h])
        d_p = dot_nt(v_h, do_h)
        prod = p * d_p
        delta = jnp.sum(prod, axis=0, keepdims=True)
        d_s = (prod - p * delta).astype(BF16)
        dv_acc[:, cols] += dot_nn(p.astype(BF16), do_h)
        dk_acc[:, cols] += dot_nn(d_s, q_h)
        here = pl.ds(pl.multiple_of(place * rows, rows), rows)
        grads[here, cols] = dot_tn(d_s, k_h).astype(BF16)

    @pl.when(i == pl.num_programs(0) - 1)
    def _():
        width = dk_acc.shape[1]
        grads[:, width : 2 * width] = dk_acc[...].astype(BF16)
        grads[:, 2 * width :] = dv_acc[...].astype(BF16)


def attend_back(scalars, dzs, out_w, qkv, lse, masked):
    _, rows, width = qkv.shape
    heads = width // DH
    count = out_w.shape[1]
    tiles = rows // TILE

    def tile(i, sc):
        return (quarter(jnp.bitwise_xor(sc[0], i)), 0)

    return call(
        functools.partial(attend_back_body, masked),
        (tiles,),
        [full(dz.shape) for dz in dzs]
        + [
            full(out_w.shape),
            pl.BlockSpec((1, TILE, width), lambda i, sc: (0, tile(i, sc)[0], 0)),
            pl.BlockSpec((1, rows, width), lambda i, sc: (1, 0, 0)),
            pl.BlockSpec((1, rows, width), lambda i, sc: (2, 0, 0)),
            pl.BlockSpec((heads, 1, TILE), lambda i, sc: (0, 0, tile(i, sc)[0])),
        ],
        [
            pl.BlockSpec((rows, 3 * width), lambda i, sc: (0, 0)),
            pl.BlockSpec((TILE, count), tile),
        ],
        [shape_of((rows, 3 * width), BF16), shape_of((rows, count), BF16)],
        scalars,
        [*dzs, out_w, qkv, qkv, qkv, lse],
        scratch=[pltpu.VMEM((rows, width), F32), pltpu.VMEM((rows, width), F32)],
        hbm=True,
        flops=2 * rows * count * width + 10 * rows * rows * width,
    )


def relative(i):
    return jnp.where(i < 2, 2 * i + 1, 2 * i - 4)


def spread_body(scales, flipped, n_left, sc, *refs):
    lefts, right, send, keep = refs[:n_left], refs[n_left], refs[-2], refs[-1]
    i = pl.program_id(0)
    rows = lefts[0].shape[0]
    parts = []
    for left in lefts:
        if flipped:
            width = right.shape[2]
            total = None
            for s, scale in enumerate(scales):
                part = dot_nt(left[:, s * width : (s + 1) * width], right[s])
                part = part * scale if scale != 1.0 else part
                total = part if total is None else total + part
        else:
            total = dot_nn(left[...], right[...])
        parts.append(total.astype(BF16))

    def put(out):
        for at, part in enumerate(parts):
            out[0, at * rows : (at + 1) * rows, :] = part

    @pl.when(i < 2)
    def _():
        put(send)

    @pl.when(i >= 2)
    def _():
        put(keep)


def spread(scalars, lefts, right, n_tp, scales=None):
    flipped = scales is not None
    rows = sum(a.shape[0] for a in lefts)
    count = right.shape[1]
    width = count // n_tp

    def cols(i, sc):
        j = jnp.bitwise_xor(sc[0], relative(i))
        return (0, j, 0) if flipped else (0, j)

    block = (right.shape[0], width, right.shape[2]) if flipped else (right.shape[0], width)
    return call(
        functools.partial(spread_body, scales, flipped, len(lefts)),
        (n_tp,),
        [full(a.shape) for a in lefts] + [pl.BlockSpec(block, cols)],
        [
            pl.BlockSpec((1, rows, width), lambda i, sc: (jnp.minimum(i, 1), 0, 0)),
            pl.BlockSpec((1, rows, width), lambda i, sc: (jnp.maximum(i - 2, 0), 0, 0)),
        ],
        [shape_of((2, rows, width), BF16), shape_of((2, rows, width), BF16)],
        scalars,
        [*lefts, right],
        hbm=True,
        flops=2 * rows * lefts[0].shape[1] * count,
    )


def out_body(n_left, sc, *refs):
    lefts, right, right_c, send, keep = refs[:n_left], *refs[n_left:]
    i = pl.program_id(0)
    rows, near = lefts[0].shape[0], right.shape[0]
    parts = [
        (dot_nn(left[:, :near], right[...]) + dot_nn(left[:, near:], right_c[...])).astype(BF16)
        for left in lefts
    ]
    for step, out in enumerate((send, keep)):

        @pl.when(i == step)
        def _(out=out):
            for at, part in enumerate(parts):
                out[at * rows : (at + 1) * rows, :] = part


def out_product(scalars, lefts, right, right_c):
    rows = sum(a.shape[0] for a in lefts)
    hidden, count = right.shape

    def cols(i, sc):
        side = jnp.right_shift(sc[0], 1)
        return (0, jnp.where(i == 0, 1 - side, side))

    return call(
        functools.partial(out_body, len(lefts)),
        (2,),
        [full(a.shape) for a in lefts] + [pl.BlockSpec((hidden, count // 2), cols)] * 2,
        [pl.BlockSpec((rows, count // 2), lambda i, sc: (0, 0))] * 2,
        [shape_of((rows, count // 2), BF16)] * 2,
        scalars,
        [*lefts, right, right_c],
        cost=1e11,
        hbm=True,
        flops=4 * rows * hidden * count,
    )


def pair_grad_body(sc, a0, a1, b0, b1, send, keep):
    i = pl.program_id(0)
    low = (dot_tn(a0[...], b0[...]) + dot_tn(a1[...], b1[...])).astype(BF16)
    for step, out in enumerate((send, keep)):

        @pl.when(i == step)
        def _(out=out):
            out[...] = low


def pair_grad(scalars, lefts, rights, split_left):
    rows = lefts[0].shape[0]
    halved = lambda i, sc: (0, 1 - i)
    m = lefts[0].shape[1] // (2 if split_left else 1)
    count = rights[0].shape[1] // (1 if split_left else 2)
    left = pl.BlockSpec((rows, m), halved) if split_left else full((rows, m))
    right = full((rows, count)) if split_left else pl.BlockSpec((rows, count), halved)
    return call(
        pair_grad_body,
        (2,),
        [left, left, right, right],
        [pl.BlockSpec((m, count), lambda i, sc: (0, 0))] * 2,
        [shape_of((m, count), BF16)] * 2,
        scalars,
        [*lefts, *rights],
        hbm=True,
        flops=8 * rows * m * count,
        vmem=32,
    )


def norm_sums_body(sc, da, x, stats, gain, moments, sums):
    d = da[...].astype(F32)
    nhat = (x[...].astype(F32) - stats[:, 0:1]) * stats[:, 1:2]
    n = d * gain[...]
    prod = d * nhat
    rows = d.shape[0]
    for at, v in enumerate((n, n * nhat)):
        total = jnp.broadcast_to(jnp.sum(v, axis=1, keepdims=True), (rows, 128))
        moments[at : at + 1, :] = jnp.transpose(total)[0:1, :]
    sums[0:1, :] = jnp.sum(prod, axis=0, keepdims=True)
    sums[1:2, :] = jnp.sum(d, axis=0, keepdims=True)


def norm_sums(scalars, da, x, stats, gain):
    rows, width = da.shape
    return call(
        norm_sums_body,
        (1,),
        [full(v.shape) for v in (da, x, stats, gain)],
        [pl.BlockSpec((2, rows), lambda i, sc: (0, 0)), pl.BlockSpec((2, width), lambda i, sc: (0, 0))],
        [shape_of((2, rows), F32), shape_of((2, width), F32)],
        scalars,
        [da, x, stats, gain],
    )


def attn_grad_body(sc, a0, a1, z0, z1, d0, d1, o0, o1, send, keep):
    i = pl.program_id(0)
    wide = d0.shape[1]
    low1 = (dot_tn(a0[...], d0[...]) + dot_tn(a1[...], d1[...])).astype(BF16)
    low2 = (dot_tn(z0[...], o0[...]) + dot_tn(z1[...], o1[...])).astype(BF16)
    for step, out in enumerate((send, keep)):

        @pl.when(i == step)
        def _(out=out):
            out[:, :wide] = low1
            out[:, wide:] = low2


def attn_grad(scalars, acts, dzs, grads, mixed, bit):
    rows, m = acts[0].shape
    count = grads[0].shape[1] + mixed[0].shape[1]

    def index(i, sc):
        mine = jnp.bitwise_and(jnp.right_shift(sc[2], bit), 1)
        return (0, jnp.where(i == 0, 1 - mine, mine))

    return call(
        attn_grad_body,
        (2,),
        [pl.BlockSpec((rows, m // 2), index)] * 4 + [full(v.shape) for v in (*grads, *mixed)],
        [pl.BlockSpec((m // 2, count), lambda i, sc: (0, 0))] * 2,
        [shape_of((m // 2, count), BF16)] * 2,
        scalars,
        [*acts, *dzs, *grads, *mixed],
        hbm=True,
        flops=4 * rows * m * count,
        vmem=32,
    )


def place_body(blocks, sc, first, second, out):
    rows = first.shape[0] * 2 // blocks
    half = blocks // 2
    for k in range(blocks):
        src = first if k < half else second
        at = (k if k < half else k - half) * rows
        to = pl.ds(pl.multiple_of(jnp.bitwise_xor(sc[0], k) * rows, rows), rows)
        out[to, :] = src[at : at + rows, :].astype(F32)


def place(index, first, second, blocks, width):
    m, count = first.shape[0] * 2, first.shape[1]
    half = pl.BlockSpec((m // 2, width), lambda i, sc: (0, i))
    return call(
        functools.partial(place_body, blocks),
        (count // width,),
        [half, half],
        pl.BlockSpec((m, width), lambda i, sc: (0, i)),
        shape_of((m, count), F32),
        index,
        [first, second],
    )


def unpack_body(scale, blocks, sc, first, second, d_qkv, d_out):
    i = pl.program_id(0)
    n = pl.num_programs(0) - 1
    rows = first.shape[0] * 2 // blocks
    half = blocks // 2

    def each(put):
        for k in range(blocks):
            src = first if k < half else second
            at = (k if k < half else k - half) * rows
            to = pl.ds(pl.multiple_of(jnp.bitwise_xor(sc[0], k) * rows, rows), rows)
            put(to, src[at : at + rows, :].astype(F32))

    def scaled(to, value):
        d_qkv[0, to, :] = value * jnp.where(i == 0, jnp.float32(scale), jnp.float32(1.0))

    def turned(to, value):
        d_out[:, to] = jnp.transpose(value)

    @pl.when(i < n)
    def _():
        each(scaled)

    @pl.when(i == n)
    def _():
        each(turned)


def unpack(index, first, second, blocks, width, scale):
    m, count = first.shape[0] * 2, first.shape[1]
    n = count // width - 1
    return call(
        functools.partial(unpack_body, scale, blocks),
        (n + 1,),
        [pl.BlockSpec((m // 2, width), lambda i, sc: (0, i))] * 2,
        [
            pl.BlockSpec((1, m, width), lambda i, sc: (jnp.minimum(i, n - 1), 0, 0)),
            pl.BlockSpec((width, m), lambda i, sc: (0, 0)),
        ],
        [shape_of((n, m, width), F32), shape_of((width, m), F32)],
        index,
        [first, second],
    )


def halve_body(bit, sc, keep, got, send, nxt):
    half = send.shape[0]
    mine = jnp.bitwise_and(jnp.right_shift(sc[2], bit), 1)
    for out, side in ((send, 1 - mine), (nxt, mine)):
        rows = pl.ds(pl.multiple_of(side * half, half), half)
        out[...] = (keep[rows, :].astype(F32) + got[rows, :].astype(F32)).astype(BF16)


def halve(scalars, keep, got, bit):
    shape = shape_of((keep.shape[0] // 2, keep.shape[1]), BF16)
    return call(
        functools.partial(halve_body, bit),
        (1,),
        [full(keep.shape)] * 2,
        [pl.BlockSpec(shape.shape, lambda i, sc: (0, 0))] * 2,
        [shape] * 2,
        scalars,
        [keep, got],
    )


def join_body(added, sc, a, c, out):
    rows = a.shape[0]
    if added:
        out[...] = (a[...].astype(F32) + c[...].astype(F32)).astype(BF16)
    else:
        out[:rows, :] = a[...]
        out[rows:, :] = c[...]


def join(scalars, first, second, added):
    shape = shape_of((first.shape[0] * (1 if added else 2), first.shape[1]), BF16)
    return call(
        functools.partial(join_body, added),
        (1,),
        [full(first.shape)] * 2,
        pl.BlockSpec(shape.shape, lambda i, sc: (0, 0)),
        shape,
        scalars,
        [first, second],
    )


def place_of_largest(lens, half):
    count = lens.shape[1]
    start, border, before = jnp.int32(0), jnp.int32(0), jnp.int32(0)
    for i in range(count):
        big = lens[0, i] == half
        start = jnp.where(big, before, start)
        border = jnp.where(big, lens[0, (i + 1) % count], border)
        before = before + lens[0, i]
    return start, border


def turn_body(half, lens, here, x, *outs):
    start, border = place_of_largest(lens, half)
    rows = x.shape[0]
    turned = pltpu.roll(x[...].astype(F32), lax.rem(rows - start, rows), 0).astype(BF16)
    if len(outs) == 1:
        outs[0][...] = turned
        return
    first, second, out = outs
    first[...] = turned[:half]
    second[...] = turned[half:]
    out[0] = here[0]
    out[1] = border
    out[2] = here[1]
    out[3] = start


def turn(lengths, here, x, half, split):
    smem = pl.BlockSpec(memory_space=pltpu.SMEM)
    vmem = pl.BlockSpec(memory_space=pltpu.VMEM)
    piece = shape_of((half, x.shape[1]), BF16)
    if split:
        out_specs, out_shape = [vmem, vmem, smem], [piece, piece, shape_of((4,), jnp.int32)]
    else:
        out_specs, out_shape = [vmem], [shape_of(x.shape, BF16)]
    return pl.pallas_call(
        functools.partial(turn_body, half),
        in_specs=[smem, smem, vmem],
        out_specs=out_specs,
        out_shape=out_shape,
        compiler_params=pltpu.CompilerParams(vmem_limit_bytes=16 * MIB),
    )(lengths, here, x)


class Chain:
    def __init__(self):
        self.last = ()

    def tie(self, value, *need):
        return lax.optimization_barrier((value, need, self.last))[0]

    def do(self, fn, *args, **keywords):
        leaves, tree = jax.tree_util.tree_flatten(args)
        arrays = iter(self.tie([v for v in leaves if isinstance(v, jax.Array)]))
        leaves = [next(arrays) if isinstance(v, jax.Array) else v for v in leaves]
        out = fn(*jax.tree_util.tree_unflatten(tree, leaves), **keywords)
        self.last = jax.tree_util.tree_leaves(out)[0]
        return out


class RowSum:
    def __init__(self, chain, scalars, r, n_rows, order, pair, core_flip=None):
        self.chain, self.scalars, self.r, self.n_rows = chain, scalars, r, n_rows
        self.order, self.depth = order, len(order)
        self.rest = [b for b in range(n_rows.bit_length() - 1) if b not in order]
        send, self.keep = pair
        self.at = 0 if core_flip is None else -1
        self.got = self.flip(send, order[0]) if core_flip is None else core_flip(send)

    def flip(self, value, bit):
        return lax.ppermute(value, "rows", [(i, i ^ (1 << bit)) for i in range(self.n_rows)])

    def step(self):
        do = self.chain.do
        if self.at < self.depth:
            self.at += 1
            if self.at < self.depth:
                bit = self.order[self.at]
                send, self.keep = do(halve, self.scalars, self.keep, self.got, bit)
                self.got = self.flip(send, bit)
                return
            self.buf = do(join, self.scalars, self.keep, self.got, True)
            for b in self.rest:
                self.buf = do(join, self.scalars, self.buf, self.flip(self.buf, b), True)
            self.left = self.depth - 1
        else:
            self.left -= 1
            self.buf = do(join, self.scalars, self.buf, self.got, False)
        self.got = self.flip(self.buf, self.order[self.left])

    def finish(self, fn, *args):
        index = 0
        for b in self.order:
            index = index * 2 + jnp.bitwise_and(jnp.right_shift(self.r, b), 1)
        index = jnp.stack([index, index]).astype(jnp.int32)
        return self.chain.do(fn, index, self.buf, self.got, 1 << self.depth, *args)


def local(
    n_tp, n_rows,
    datapoints, lengths, qkv_weight, out_weight, up_weight, up_bias, down_weight, down_bias,
    gain_one, shift_one, gain_two, shift_two, grad_out,
):
    tok, width = datapoints.shape
    count = n_tp * width
    half = tok // 2
    q_scale = DH ** (-0.5)
    t, r = lax.axis_index("tp"), lax.axis_index("rows")
    chain = Chain()
    do, tie = chain.do, chain.tie

    def core_flip(v):
        return lax.ppermute(v, "tp", [(i, i ^ 1) for i in range(n_tp)])

    def x_flip(v):
        return lax.ppermute(v, "tp", [(i, i ^ 2) for i in range(n_tp)])

    def diag_flip(v):
        return lax.ppermute(v, "tp", [(i, i ^ 3) for i in range(n_tp)])

    def row_flip(v, b):
        return lax.ppermute(v, "rows", [(i, i ^ (1 << b)) for i in range(n_rows)])

    ow = lax.all_gather(out_weight, "tp", axis=0, tiled=True)
    vectors = jnp.concatenate([gain_one, shift_one, gain_two, shift_two, down_bias])
    vec_x = x_flip(vectors)
    vec_c = core_flip(jnp.concatenate([vectors, up_bias]))
    here = jnp.stack([t, r]).astype(jnp.int32)
    x0, x1, scalars = do(turn, lengths, here, datapoints, half, True)
    start = scalars[3]
    x0_x, x0_c = x_flip(x0), core_flip(x0)
    d_down_bias = do(lambda v: jnp.sum(v.astype(F32), axis=0), grad_out)
    vec_d = core_flip(tie(vec_x))
    n_vec = vectors.shape[0] // width

    def relative_vectors(*pieces):
        return jnp.stack([p[: n_vec * width].reshape(n_vec, width) for p in pieces])

    def vector_orders(rel, vec_c):
        order = jnp.bitwise_xor(t, jnp.arange(n_tp))
        bias = jnp.concatenate([up_bias, vec_c[n_vec * width :]]).reshape(1, -1)
        return jnp.transpose(rel[order], (1, 0, 2)).reshape(n_vec, count), bias

    weight4 = qkv_weight.reshape(3, n_tp, width, width)
    gains_rel = do(relative_vectors, vectors, vec_c, vec_x, vec_d)
    x0_d = core_flip(x0_x)
    x1 = tie(x1, x0_x)
    x1_x, x1_c = x_flip(x1), core_flip(x1)
    (dy,) = do(turn, lengths, here, grad_out, half, False)
    wide = tie((up_weight, down_weight), x0_x)
    up_c, down_c = core_flip(wide[0]), core_flip(wide[1])
    xs = [[x0, x0_c, x0_x, x0_d], None]
    qkv, acts, stats, mixed, lse, pieces = [[None] * 2 for _ in range(6)]

    def first(h):
        qkv[h], acts[h], stats[h], mixed[h], lse[h], other, mine = do(
            first_layer, scalars, xs[h], dy, gains_rel, weight4, h
        )
        pieces[h] = [mine, core_flip(other), x_flip(mine), diag_flip(other)]

    first(0)
    x1_d = core_flip(tie(x1_x, up_c, down_c))
    xs[1] = [x1, x1_c, x1_x, x1_d]
    first(1)
    gains, bias2 = do(vector_orders, gains_rel, vec_c)

    weights = [ow, gains, up_weight, up_c, down_weight, down_c, bias2]
    fed0 = do(feed, scalars, xs[0], pieces[0], *weights)
    db0_x = x_flip(fed0[7])
    fed1 = do(feed, scalars, xs[1], pieces[1], *weights)
    db1_x = x_flip(fed1[7])
    y_cols, b, dyn, g, du = [[fed0[k], fed1[k]] for k in (0, 3, 4, 5, 6)]
    def row_sum(order, pair, *core):
        return RowSum(chain, scalars, r, n_rows, order, pair, *core)

    def spread_rows(v):
        return [v, core_flip(v), x_flip(v), diag_flip(v)]

    dz0, sums0 = do(norm_back, scalars, fed0[8], db0_x, fed0[1], fed0[2], gains)
    dz0_x, dz0_c = x_flip(dz0), core_flip(dz0)
    up = row_sum([1, 0, 2], do(pair_grad, scalars, b, du, False), core_flip)
    db1_x = tie(db1_x, dz0_c)
    down = row_sum([0, 1, 2], do(pair_grad, scalars, g, dyn, True), core_flip)
    dz0_x = tie(dz0_x)
    dzs0 = [dz0, dz0_c, dz0_x, core_flip(dz0_x)]
    dz1, sums1 = do(norm_back, scalars, fed1[8], db1_x, fed1[1], fed1[2], gains)
    dzs1 = spread_rows(dz1)
    hidden = up_bias.shape[0]
    up.step()
    down.step()

    grads0, dzn0 = do(attend_back, scalars, dzs0, out_weight, qkv[0], lse[0], False)
    up.step()
    down.step()
    grads1, dzn1 = do(attend_back, scalars, dzs1, out_weight, qkv[1], lse[1], True)
    up.step()
    down.step()
    attn = row_sum(
        [0, 1, 2],
        do(attn_grad, scalars, acts, [dzn0, dzn1], [grads0, grads1], mixed, 0),
    )

    def middle(keep, got):
        return (keep[1].astype(F32) + got[1].astype(F32)).astype(BF16)

    def total_of(keep, got, got_x):
        return keep[0].astype(F32) + got[0].astype(F32) + got_x.astype(F32)

    send, keep_a = do(spread, scalars, [grads0, grads1], qkv_weight, n_tp, (q_scale, 1.0, 1.0))
    got_a = core_flip(send)
    up.step()
    down.step()
    out_send, out_keep = do(out_product, scalars, g, down_weight, down_c)
    da_x = x_flip(do(middle, keep_a, got_a))
    attn.step()
    up.step()
    down.step()
    bias_grad = do(jnp.add, fed0[9], fed1[9])
    attn.step()
    up.step()
    down.step()
    attn.step()
    gain_row = gain_one.reshape(1, -1)

    def joined(*parts):
        return total_of(*parts).astype(BF16)

    da = do(joined, keep_a, got_a, da_x)
    out_x = x_flip(tie(out_send))
    m0, ones0 = do(norm_sums, scalars, da[:half], x0, stats[0], gain_row)
    m1, ones1 = do(norm_sums, scalars, da[half:], x1, stats[1], gain_row)
    m = do(lambda a, b, *c: jnp.concatenate([a + b, *c], 0), sums0, sums1, m0, m1)
    m_c = core_flip(m)
    bias_got = core_flip(bias_grad[:, hidden:])
    attn.step()
    m = do(jnp.add, m, m_c)
    m_x = x_flip(m)
    c, side = jnp.bitwise_and(t, 1), jnp.right_shift(t, 1)

    def output_rows(keep, got, y0, y1, vecs):
        wide = 2 * width
        extra = lax.dynamic_slice_in_dim(vecs[4], side * wide, wide, 0)
        total = keep.astype(F32) + got.astype(F32) + jnp.concatenate([y0, y1], 0) + extra
        low = total.astype(BF16)
        return (
            lax.dynamic_slice_in_dim(low, (1 - c) * width, width, 1),
            lax.dynamic_slice_in_dim(low, c * width, width, 1),
        )

    rows_send, rows_keep = do(output_rows, out_keep, out_x, *y_cols, gains)
    rows_got = core_flip(rows_send)

    def unroll(first, second):
        thrice = jnp.concatenate([second, first, second], 0)
        return lax.dynamic_slice_in_dim(thrice, half - start, tok, 0)

    def output_of(mine, other):
        part = half // 2
        halves = []
        for h in range(2):
            a, b = mine[h * part : (h + 1) * part], other[h * part : (h + 1) * part]
            halves.append(
                jnp.where(c == 0, jnp.concatenate([a, b], 0), jnp.concatenate([b, a], 0))
            )
        return unroll(*halves)

    m = do(jnp.add, m, m_x)

    def small_of(up_b, down_b, m, ones0, ones1):
        two = lax.dynamic_slice_in_dim(m[:2], t * width, width, 1)
        return jnp.concatenate(
            [up_b.reshape(-1), down_b, (ones0 + ones1).reshape(-1), two.reshape(-1)]
        ).reshape(-1, 128)

    d_up_bias = bias_grad[:, :hidden] + bias_got
    small = do(small_of, d_up_bias, d_down_bias, m, ones0, ones1)
    bits = list(range(n_rows.bit_length() - 1))
    small_got = row_flip(small, bits[0])

    def d_input_of(m, da, *parts):
        halves = []
        for h, (x, stat, dzn) in enumerate((parts[:3], parts[3:])):
            nhat = (x.astype(F32) - stat[:, 0:1]) * stat[:, 1:2]
            first, second = m[2 + 2 * h][:, None] / count, m[3 + 2 * h][:, None] / count
            dz = lax.dynamic_slice_in_dim(dzn, t * width, width, 1).astype(F32)
            n = da[h * half : (h + 1) * half].astype(F32) * gain_one
            halves.append(dz + stat[:, 1:2] * (n - first - nhat * second))
        return unroll(*halves)

    attn.step()
    small = do(jnp.add, small, small_got)
    small_got = row_flip(small, bits[1])
    d_input = do(d_input_of, m, da, x0, stats[0], dzn0, x1, stats[1], dzn1)
    output = do(output_of, rows_keep, rows_got)
    d_down = down.finish(place, width)
    d_up = up.finish(place, width)
    for bit in bits[2:]:
        small = do(jnp.add, small, small_got)
        small_got = row_flip(small, bit)
    small = do(jnp.add, small, small_got).reshape(-1)
    d_qkv, d_out = attn.finish(unpack, width, q_scale)
    d_down_bias, d_gain_one, d_shift_one, d_gain_two, d_shift_two = small[hidden:].reshape(5, width)
    return (
        output, d_input, d_qkv, d_out, d_up, small[:hidden],
        d_down, d_down_bias, d_gain_one, d_shift_one, d_gain_two, d_shift_two,
    )


def solution(mesh):
    grid = P("rows", "tp")
    placed = (
        grid, P("rows", None), P(None, None, "tp"), P("tp", None), P(None, "tp"), P("tp"),
        P("tp", None), P("tp"), P("tp"), P("tp"), P("tp"), P("tp"), grid,
    )
    return jax.shard_map(
        functools.partial(local, mesh.shape["tp"], mesh.shape["rows"]),
        mesh=mesh,
        in_specs=placed,
        out_specs=(
            grid, grid, P(None, None, "tp"), P("tp", None), P(None, "tp"), P("tp"),
            P("tp", None), P("tp"), P("tp"), P("tp"), P("tp"), P("tp"),
        ),
        check_vma=False,
    )
```

```python
import functools

import jax
import jax.numpy as jnp
from jax import lax
from jax.experimental import pallas as pl
from jax.experimental.pallas import tpu as pltpu
from jax.sharding import PartitionSpec as P

DH = 128
TILE = 256
EPS_NORM = 1e-05
NEG_FILL = -1e30
F32 = jnp.float32
BF16 = jnp.bfloat16
MIB = 1024 * 1024
COST = 8.0
GELU_C = 0.7978845608028654


def dot_nn(a, b):
    return jnp.dot(a, b, preferred_element_type=F32)


def dot_nt(a, b):
    return lax.dot_general(a, b, (((1,), (1,)), ((), ())), preferred_element_type=F32)


def dot_tn(a, b):
    return lax.dot_general(a, b, (((0,), (0,)), ((), ())), preferred_element_type=F32)


def call(body, grid, in_specs, out_specs, out_shape, scalars, operands, scratch=(), flops=0, vmem=24, hbm=False, cost=2e10):
    bytes_moved = sum(o.size * o.dtype.itemsize for o in operands)
    bytes_moved += sum(
        o.size * jnp.dtype(o.dtype).itemsize for o in jax.tree_util.tree_leaves(out_shape)
    )
    operands = [
        pltpu.with_memory_space_constraint(o, pltpu.HBM) if hbm else o for o in operands
    ]
    if hbm:
        out_shape = jax.tree_util.tree_map(lambda o: pltpu.HBM(o.shape, o.dtype), out_shape)
    return pl.pallas_call(
        body,
        grid_spec=pltpu.PrefetchScalarGridSpec(
            num_scalar_prefetch=1,
            grid=grid,
            in_specs=in_specs,
            out_specs=out_specs,
            scratch_shapes=list(scratch),
        ),
        out_shape=out_shape,
        compiler_params=pltpu.CompilerParams(
            vmem_limit_bytes=vmem * MIB,
            dimension_semantics=("arbitrary",) * len(grid),
        ),
        cost_estimate=pl.CostEstimate(
            flops=int(cost), bytes_accessed=int(bytes_moved), transcendentals=0
        ),
    )(scalars, *operands)


def full(shape):
    zeros = (0,) * len(shape)
    return pl.BlockSpec(shape, lambda *_: zeros, pipeline_mode=pl.Buffered(1))


def shape_of(shape, dtype):
    return jax.ShapeDtypeStruct(shape, dtype)


def far_first(i, n, sc):
    c = jnp.bitwise_and(sc[0], 1)
    return jnp.where(i < n // 2, (1 - c) * (n // 2) + i, c * (n // 2) + i - n // 2)


def first_body(
    masked, tile, sc, x0, x1, x2, x3, dy_other, dy_mine, gains, weight,
    qkv, acts, stats, o, lse, other, mine, q_all, k_all, v_all,
):
    t = sc[0]
    i = pl.program_id(0)
    n = pl.num_programs(0) // 2

    @pl.when(i == 0)
    def _():
        rows = dy_mine.shape[0]
        other[rows:, :] = dy_other[...]
        mine[rows:, :] = dy_mine[...]

    @pl.when(i < n)
    def _():
        pieces = [x[...].astype(F32) for x in (x0, x1, x2, x3)]
        width = pieces[0].shape[1]
        count = width * len(pieces)
        mean = sum(jnp.sum(x, axis=1, keepdims=True) for x in pieces) / count
        centered = [x - mean for x in pieces]
        var = sum(jnp.sum(c * c, axis=1, keepdims=True) for c in centered) / count
        rstd = lax.rsqrt(var + EPS_NORM)
        total = [0.0, 0.0, 0.0]
        for k, c in enumerate(centered):
            j = jnp.bitwise_xor(t, k)
            part = (c * rstd * gains[k, 0:1, :] + gains[k, 1:2, :]).astype(BF16)
            acts[:, pl.ds(pl.multiple_of(j * width, width), width)] = part
            for s in range(3):
                total[s] = total[s] + dot_nn(part, weight[s, j])
        rows = pl.ds(pl.multiple_of(i * tile, tile), tile)
        for s, (value, kept) in enumerate(zip(total, (q_all, k_all, v_all))):
            low = (value * (DH ** (-0.5)) if s == 0 else value).astype(BF16)
            qkv[s] = low
            kept[rows, :] = low
        stats[:, 0:1] = mean
        stats[:, 1:2] = rstd

    @pl.when(i >= n)
    def _():
        cols = k_all.shape[0]
        first = far_first(i - n, n, sc) * tile
        rows = pl.ds(pl.multiple_of(first, tile), tile)
        if masked:
            q_side = (first + lax.broadcasted_iota(jnp.int32, (tile, 1), 0)) < sc[1]
            k_side = lax.broadcasted_iota(jnp.int32, (1, cols), 1) < sc[1]
            apart = jnp.logical_xor(q_side, k_side)
        for h in range(q_all.shape[1] // DH):
            part = slice(h * DH, (h + 1) * DH)
            scores = dot_nt(q_all[rows, part], k_all[:, part])
            if masked:
                scores = jnp.where(apart, NEG_FILL, scores)
            top = jnp.max(scores, axis=1, keepdims=True)
            weights = jnp.exp(scores - top)
            total = jnp.sum(weights, axis=1, keepdims=True)
            mixed = dot_nn(weights.astype(BF16), v_all[:, part])
            low = (mixed / total).astype(BF16)
            o[:, part] = low
            to = lax.rem(i, n // 2) * tile
            to = pl.ds(pl.multiple_of(to, tile), tile)

            @pl.when(i < n + n // 2)
            def _():
                other[to, part] = low

            @pl.when(i >= n + n // 2)
            def _():
                mine[to, part] = low

            stat = jnp.broadcast_to(top + jnp.log(total), (tile, DH))
            lse[h] = jnp.transpose(stat)[0:1, :]


def first_layer(scalars, pieces, dy, gains, weight4, h):
    rows, width = pieces[0].shape
    n = len(pieces)
    heads = width // DH
    tile = 256
    steps = rows // tile

    def early(i, sc):
        return (jnp.minimum(i, steps - 1), 0)

    def late(i, sc):
        return far_first(jnp.maximum(i - steps, 0), steps, sc)

    def rows_of(mine):
        def index(i, sc):
            c = jnp.bitwise_and(sc[0], 1)
            return (2 * h + (c if mine else 1 - c), 0)

        return pl.BlockSpec((rows // 2, width), index, pipeline_mode=pl.Buffered(1))

    whole = pl.BlockSpec((rows, width), lambda i, sc: (0, 0))

    return call(
        functools.partial(first_body, h == 1, tile),
        (2 * steps,),
        [pl.BlockSpec((tile, width), early)] * n
        + [rows_of(False), rows_of(True), full(gains.shape), full(weight4.shape)],
        [
            pl.BlockSpec((3, tile, width), lambda i, sc: (0, jnp.minimum(i, steps - 1), 0)),
            pl.BlockSpec((tile, n * width), early),
            pl.BlockSpec((tile, 2), early),
            pl.BlockSpec((tile, width), lambda i, sc: (late(i, sc), 0)),
            pl.BlockSpec((heads, 1, tile), lambda i, sc: (0, 0, late(i, sc))),
            whole,
            whole,
        ],
        [
            shape_of((3, rows, width), BF16),
            shape_of((rows, n * width), BF16),
            shape_of((rows, 2), F32),
            shape_of((rows, width), BF16),
            shape_of((heads, 1, rows), F32),
            shape_of((rows, width), BF16),
            shape_of((rows, width), BF16),
        ],
        scalars,
        [*pieces, dy, dy, gains, weight4],
        scratch=[pltpu.VMEM((rows, width), BF16)] * 3,
        hbm=True,
        flops=2 * rows * n * width * 3 * width + 4 * rows * rows * width,
    )


def quarter(u):
    return 2 * jnp.bitwise_and(u, 1) + jnp.right_shift(u, 1)


def feed_body(
    sc, x0, x1, x2, x3, p0, p1, p2, p3, ow, gains, up, up_c, down, down_c, bias,
    y_cols, y_rows, dy_rows, b_out, dy_out, g_out, du_out, send, keep, bias_grad, y_acc, total,
):
    t = sc[0]
    i = pl.program_id(0)
    side = jnp.right_shift(t, 1)
    xs, ps = (x0, x1, x2, x3), (p0, p1, p2, p3)
    rows, width = x0.shape
    n = len(xs)
    count = n * width

    @pl.when(i == 0)
    def _():
        def block(k):
            j = jnp.bitwise_xor(t, k)
            return pl.ds(pl.multiple_of(j * width, width), width)

        for k in range(n):
            y_acc[:, block(k)] = xs[k][...].astype(F32)
            dy_out[:, block(k)] = ps[k][rows:, :]
        y = y_acc[...]
        for k in range(n):
            y = y + dot_nn(ps[k][:rows, :], ow[block(k), :])
        y_acc[...] = y
        mean = jnp.sum(y, axis=1, keepdims=True) / count
        centered = y - mean
        rstd = lax.rsqrt(jnp.sum(centered * centered, axis=1, keepdims=True) / count + EPS_NORM)
        b_out[...] = (centered * rstd * gains[2:3, :] + gains[3:4, :]).astype(BF16)
        total[...] = jnp.zeros_like(total)
        wide = y_cols.shape[1]
        y_cols[...] = y_acc[:, pl.ds(pl.multiple_of(side * wide, wide), wide)]
        part = y_rows.shape[0]
        mine = pl.ds(pl.multiple_of(side * part, part), part)
        y_rows[...] = y_acc[mine, :]
        dy_rows[...] = dy_out[mine, :]

    def chunk(up, down):
        u = dot_nn(b_out[...], up[...]) + bias[...]
        dh = dot_nt(dy_out[...], down[...])
        square = u * u
        half = 0.5 + 0.5 * jnp.tanh(u * (GELU_C + (GELU_C * 0.044715) * square))
        g_out[...] = (u * half).astype(BF16)
        inner = u * (2 * GELU_C + (6 * 0.044715 * GELU_C) * square)
        du = (dh * (half + (half - half * half) * inner)).astype(BF16)
        du_out[...] = du
        bias_grad[...] = jnp.sum(du.astype(F32), axis=0, keepdims=True)
        total[...] += dot_nt(du, up[...])

    steps = pl.num_programs(0)

    @pl.when(i < steps // 2)
    def _():
        chunk(up, down)

    @pl.when(i >= steps // 2)
    def _():
        chunk(up_c, down_c)

    @pl.when(i == pl.num_programs(0) - 1)
    def _():
        part = send.shape[0]
        for out, at in ((send, 1 - side), (keep, side)):
            out[...] = total[pl.ds(pl.multiple_of(at * part, part), part), :].astype(BF16)


def feed(scalars, xs, pieces, ow, gains, up, up_c, down, down_c, bias):
    rows, width = xs[0].shape
    n = len(xs)
    count = n * width
    step = 512
    near = up.shape[1] // step
    hidden = 2 * up.shape[1]
    half = rows // 2
    part = half // 2

    def own(i):
        return jnp.minimum(i, near - 1)

    def other(i):
        return jnp.maximum(i - near, 0)

    def mine(i, sc):
        return (jnp.bitwise_and(sc[0], 1), 0)

    def fixed(i, sc):
        return (0, 0)

    def along(i, sc):
        return (0, i)

    return call(
        feed_body,
        (hidden // step,),
        [pl.BlockSpec((half, width), mine, pipeline_mode=pl.Buffered(1))] * n
        + [full(p.shape) for p in pieces]
        + [full(ow.shape), full(gains.shape)]
        + [
            pl.BlockSpec((count, step), lambda i, sc: (0, own(i))),
            pl.BlockSpec((count, step), lambda i, sc: (0, other(i))),
            pl.BlockSpec((step, count), lambda i, sc: (own(i), 0)),
            pl.BlockSpec((step, count), lambda i, sc: (other(i), 0)),
            pl.BlockSpec((1, step), along),
        ],
        [
            pl.BlockSpec((half, count // 2), fixed),
            pl.BlockSpec((part, count), fixed),
            pl.BlockSpec((part, count), fixed),
            pl.BlockSpec((half, count), fixed),
            pl.BlockSpec((half, count), fixed),
            pl.BlockSpec((half, step), along),
            pl.BlockSpec((half, step), along),
            pl.BlockSpec((part, count), fixed),
            pl.BlockSpec((part, count), fixed),
            pl.BlockSpec((1, step), along),
        ],
        [
            shape_of((half, count // 2), F32),
            shape_of((part, count), F32),
            shape_of((part, count), BF16),
            shape_of((half, count), BF16),
            shape_of((half, count), BF16),
            shape_of((half, hidden), BF16),
            shape_of((half, hidden), BF16),
            shape_of((part, count), BF16),
            shape_of((part, count), BF16),
            shape_of((1, hidden), F32),
        ],
        scalars,
        [*xs, *pieces, ow, gains, up, up_c, down, down_c, bias],
        scratch=[pltpu.VMEM((half, count), F32), pltpu.VMEM((half, count), F32)],
        hbm=True,
        flops=2 * half * count * (count + 3 * hidden),
        vmem=32,
    )


def norm_back_body(sc, p0, p1, y, dy, gains, dz, sums):
    db = p0[...].astype(F32) + p1[...].astype(F32)
    yv = y[...]
    count = yv.shape[1]
    mean = jnp.sum(yv, axis=1, keepdims=True) / count
    centered = yv - mean
    rstd = lax.rsqrt(jnp.sum(centered * centered, axis=1, keepdims=True) / count + EPS_NORM)
    nhat = centered * rstd
    n = db * gains[2:3, :]
    first = jnp.sum(n, axis=1, keepdims=True) / count
    second = jnp.sum(n * nhat, axis=1, keepdims=True) / count
    dz[...] = (dy[...].astype(F32) + rstd * (n - first - nhat * second)).astype(BF16)
    sums[0:1, :] = jnp.sum(db * nhat, axis=0, keepdims=True)
    sums[1:2, :] = jnp.sum(db, axis=0, keepdims=True)


def norm_back(scalars, keep, got_x, y, dy, gains):
    rows, count = got_x.shape
    return call(
        norm_back_body,
        (1,),
        [full(v.shape) for v in (keep, got_x, y, dy, gains)],
        [
            pl.BlockSpec((rows, count), lambda i, sc: (0, 0)),
            pl.BlockSpec((2, count), lambda i, sc: (0, 0)),
        ],
        [shape_of((rows, count), BF16), shape_of((2, count), F32)],
        scalars,
        [keep, got_x, y, dy, gains],
    )


def attend_back_body(masked, sc, z0, z1, z2, z3, out_w, q, k, v, lse, grads, dz_out, dk_acc, dv_acc):
    i = pl.program_id(0)
    place = quarter(jnp.bitwise_xor(sc[0], i))

    @pl.when(i == 0)
    def _():
        dk_acc[...] = jnp.zeros_like(dk_acc)
        dv_acc[...] = jnp.zeros_like(dv_acc)

    for j, z in enumerate((z0, z1, z2, z3)):

        @pl.when(i == j)
        def _(z=z):
            dz_out[...] = z[...]

    d_mixed = dot_nt(dz_out[...], out_w[...]).astype(BF16)
    rows = d_mixed.shape[0]
    keys = k.shape[1]
    for h in range(d_mixed.shape[1] // DH):
        cols = slice(h * DH, (h + 1) * DH)
        q_h, k_h, v_h, do_h = q[0, :, cols], k[0, :, cols], v[0, :, cols], d_mixed[:, cols]
        scores = dot_nt(k_h, q_h)
        if masked:
            base = place * rows
            q_side = (base + lax.broadcasted_iota(jnp.int32, (1, rows), 1)) < sc[1]
            k_side = lax.broadcasted_iota(jnp.int32, (keys, 1), 0) < sc[1]
            scores = jnp.where(jnp.logical_xor(q_side, k_side), NEG_FILL, scores)
        p = jnp.exp(scores - lse[h])
        d_p = dot_nt(v_h, do_h)
        prod = p * d_p
        delta = jnp.sum(prod, axis=0, keepdims=True)
        d_s = (prod - p * delta).astype(BF16)
        dv_acc[:, cols] += dot_nn(p.astype(BF16), do_h)
        dk_acc[:, cols] += dot_nn(d_s, q_h)
        here = pl.ds(pl.multiple_of(place * rows, rows), rows)
        grads[here, cols] = dot_tn(d_s, k_h).astype(BF16)

    @pl.when(i == pl.num_programs(0) - 1)
    def _():
        width = dk_acc.shape[1]
        grads[:, width : 2 * width] = dk_acc[...].astype(BF16)
        grads[:, 2 * width :] = dv_acc[...].astype(BF16)


def attend_back(scalars, dzs, out_w, qkv, lse, masked):
    _, rows, width = qkv.shape
    heads = width // DH
    count = out_w.shape[1]
    tiles = rows // TILE

    def tile(i, sc):
        return (quarter(jnp.bitwise_xor(sc[0], i)), 0)

    return call(
        functools.partial(attend_back_body, masked),
        (tiles,),
        [full(dz.shape) for dz in dzs]
        + [
            full(out_w.shape),
            pl.BlockSpec((1, TILE, width), lambda i, sc: (0, tile(i, sc)[0], 0)),
            pl.BlockSpec((1, rows, width), lambda i, sc: (1, 0, 0)),
            pl.BlockSpec((1, rows, width), lambda i, sc: (2, 0, 0)),
            pl.BlockSpec((heads, 1, TILE), lambda i, sc: (0, 0, tile(i, sc)[0])),
        ],
        [
            pl.BlockSpec((rows, 3 * width), lambda i, sc: (0, 0)),
            pl.BlockSpec((TILE, count), tile),
        ],
        [shape_of((rows, 3 * width), BF16), shape_of((rows, count), BF16)],
        scalars,
        [*dzs, out_w, qkv, qkv, qkv, lse],
        scratch=[pltpu.VMEM((rows, width), F32), pltpu.VMEM((rows, width), F32)],
        hbm=True,
        flops=2 * rows * count * width + 10 * rows * rows * width,
    )


def relative(i):
    return jnp.where(i < 2, 2 * i + 1, 2 * i - 4)


def spread_body(scales, flipped, n_left, sc, *refs):
    lefts, right, send, keep = refs[:n_left], refs[n_left], refs[-2], refs[-1]
    i = pl.program_id(0)
    rows = lefts[0].shape[0]
    parts = []
    for left in lefts:
        if flipped:
            width = right.shape[2]
            total = None
            for s, scale in enumerate(scales):
                part = dot_nt(left[:, s * width : (s + 1) * width], right[s])
                part = part * scale if scale != 1.0 else part
                total = part if total is None else total + part
        else:
            total = dot_nn(left[...], right[...])
        parts.append(total.astype(BF16))

    def put(out):
        for at, part in enumerate(parts):
            out[0, at * rows : (at + 1) * rows, :] = part

    @pl.when(i < 2)
    def _():
        put(send)

    @pl.when(i >= 2)
    def _():
        put(keep)


def spread(scalars, lefts, right, n_tp, scales=None):
    flipped = scales is not None
    rows = sum(a.shape[0] for a in lefts)
    count = right.shape[1]
    width = count // n_tp

    def cols(i, sc):
        j = jnp.bitwise_xor(sc[0], relative(i))
        return (0, j, 0) if flipped else (0, j)

    block = (right.shape[0], width, right.shape[2]) if flipped else (right.shape[0], width)
    return call(
        functools.partial(spread_body, scales, flipped, len(lefts)),
        (n_tp,),
        [full(a.shape) for a in lefts] + [pl.BlockSpec(block, cols)],
        [
            pl.BlockSpec((1, rows, width), lambda i, sc: (jnp.minimum(i, 1), 0, 0)),
            pl.BlockSpec((1, rows, width), lambda i, sc: (jnp.maximum(i - 2, 0), 0, 0)),
        ],
        [shape_of((2, rows, width), BF16), shape_of((2, rows, width), BF16)],
        scalars,
        [*lefts, right],
        hbm=True,
        flops=2 * rows * lefts[0].shape[1] * count,
    )


def out_body(n_left, sc, *refs):
    lefts, right, right_c, send, keep = refs[:n_left], *refs[n_left:]
    i = pl.program_id(0)
    rows, near = lefts[0].shape[0], right.shape[0]
    parts = [
        (dot_nn(left[:, :near], right[...]) + dot_nn(left[:, near:], right_c[...])).astype(BF16)
        for left in lefts
    ]
    for step, out in enumerate((send, keep)):

        @pl.when(i == step)
        def _(out=out):
            for at, part in enumerate(parts):
                out[at * rows : (at + 1) * rows, :] = part


def out_product(scalars, lefts, right, right_c):
    rows = sum(a.shape[0] for a in lefts)
    hidden, count = right.shape

    def cols(i, sc):
        side = jnp.right_shift(sc[0], 1)
        return (0, jnp.where(i == 0, 1 - side, side))

    return call(
        functools.partial(out_body, len(lefts)),
        (2,),
        [full(a.shape) for a in lefts] + [pl.BlockSpec((hidden, count // 2), cols)] * 2,
        [pl.BlockSpec((rows, count // 2), lambda i, sc: (0, 0))] * 2,
        [shape_of((rows, count // 2), BF16)] * 2,
        scalars,
        [*lefts, right, right_c],
        cost=1e11,
        hbm=True,
        flops=4 * rows * hidden * count,
    )


def pair_grad_body(sc, a0, a1, b0, b1, send, keep):
    i = pl.program_id(0)
    low = (dot_tn(a0[...], b0[...]) + dot_tn(a1[...], b1[...])).astype(BF16)
    for step, out in enumerate((send, keep)):

        @pl.when(i == step)
        def _(out=out):
            out[...] = low


def pair_grad(scalars, lefts, rights, split_left):
    rows = lefts[0].shape[0]
    halved = lambda i, sc: (0, 1 - i)
    m = lefts[0].shape[1] // (2 if split_left else 1)
    count = rights[0].shape[1] // (1 if split_left else 2)
    left = pl.BlockSpec((rows, m), halved) if split_left else full((rows, m))
    right = full((rows, count)) if split_left else pl.BlockSpec((rows, count), halved)
    return call(
        pair_grad_body,
        (2,),
        [left, left, right, right],
        [pl.BlockSpec((m, count), lambda i, sc: (0, 0))] * 2,
        [shape_of((m, count), BF16)] * 2,
        scalars,
        [*lefts, *rights],
        hbm=True,
        flops=8 * rows * m * count,
        vmem=32,
    )


def norm_sums_body(sc, da, x, stats, gain, moments, sums):
    d = da[...].astype(F32)
    nhat = (x[...].astype(F32) - stats[:, 0:1]) * stats[:, 1:2]
    n = d * gain[...]
    prod = d * nhat
    rows = d.shape[0]
    for at, v in enumerate((n, n * nhat)):
        total = jnp.broadcast_to(jnp.sum(v, axis=1, keepdims=True), (rows, 128))
        moments[at : at + 1, :] = jnp.transpose(total)[0:1, :]
    sums[0:1, :] = jnp.sum(prod, axis=0, keepdims=True)
    sums[1:2, :] = jnp.sum(d, axis=0, keepdims=True)


def norm_sums(scalars, da, x, stats, gain):
    rows, width = da.shape
    return call(
        norm_sums_body,
        (1,),
        [full(v.shape) for v in (da, x, stats, gain)],
        [pl.BlockSpec((2, rows), lambda i, sc: (0, 0)), pl.BlockSpec((2, width), lambda i, sc: (0, 0))],
        [shape_of((2, rows), F32), shape_of((2, width), F32)],
        scalars,
        [da, x, stats, gain],
    )


def attn_grad_body(sc, a0, a1, z0, z1, d0, d1, o0, o1, send, keep):
    i = pl.program_id(0)
    wide = d0.shape[1]
    low1 = (dot_tn(a0[...], d0[...]) + dot_tn(a1[...], d1[...])).astype(BF16)
    low2 = (dot_tn(z0[...], o0[...]) + dot_tn(z1[...], o1[...])).astype(BF16)
    for step, out in enumerate((send, keep)):

        @pl.when(i == step)
        def _(out=out):
            out[:, :wide] = low1
            out[:, wide:] = low2


def attn_grad(scalars, acts, dzs, grads, mixed, bit):
    rows, m = acts[0].shape
    count = grads[0].shape[1] + mixed[0].shape[1]

    def index(i, sc):
        mine = jnp.bitwise_and(jnp.right_shift(sc[2], bit), 1)
        return (0, jnp.where(i == 0, 1 - mine, mine))

    return call(
        attn_grad_body,
        (2,),
        [pl.BlockSpec((rows, m // 2), index)] * 4 + [full(v.shape) for v in (*grads, *mixed)],
        [pl.BlockSpec((m // 2, count), lambda i, sc: (0, 0))] * 2,
        [shape_of((m // 2, count), BF16)] * 2,
        scalars,
        [*acts, *dzs, *grads, *mixed],
        hbm=True,
        flops=4 * rows * m * count,
        vmem=32,
    )


def place_body(blocks, sc, first, second, out):
    rows = first.shape[0] * 2 // blocks
    half = blocks // 2
    for k in range(blocks):
        src = first if k < half else second
        at = (k if k < half else k - half) * rows
        to = pl.ds(pl.multiple_of(jnp.bitwise_xor(sc[0], k) * rows, rows), rows)
        out[to, :] = src[at : at + rows, :].astype(F32)


def place(index, first, second, blocks, width):
    m, count = first.shape[0] * 2, first.shape[1]
    half = pl.BlockSpec((m // 2, width), lambda i, sc: (0, i))
    return call(
        functools.partial(place_body, blocks),
        (count // width,),
        [half, half],
        pl.BlockSpec((m, width), lambda i, sc: (0, i)),
        shape_of((m, count), F32),
        index,
        [first, second],
    )


def unpack_body(scale, blocks, sc, first, second, d_qkv, d_out):
    i = pl.program_id(0)
    n = pl.num_programs(0) - 1
    rows = first.shape[0] * 2 // blocks
    half = blocks // 2

    def each(put):
        for k in range(blocks):
            src = first if k < half else second
            at = (k if k < half else k - half) * rows
            to = pl.ds(pl.multiple_of(jnp.bitwise_xor(sc[0], k) * rows, rows), rows)
            put(to, src[at : at + rows, :].astype(F32))

    def scaled(to, value):
        d_qkv[0, to, :] = value * jnp.where(i == 0, jnp.float32(scale), jnp.float32(1.0))

    def turned(to, value):
        d_out[:, to] = jnp.transpose(value)

    @pl.when(i < n)
    def _():
        each(scaled)

    @pl.when(i == n)
    def _():
        each(turned)


def unpack(index, first, second, blocks, width, scale):
    m, count = first.shape[0] * 2, first.shape[1]
    n = count // width - 1
    return call(
        functools.partial(unpack_body, scale, blocks),
        (n + 1,),
        [pl.BlockSpec((m // 2, width), lambda i, sc: (0, i))] * 2,
        [
            pl.BlockSpec((1, m, width), lambda i, sc: (jnp.minimum(i, n - 1), 0, 0)),
            pl.BlockSpec((width, m), lambda i, sc: (0, 0)),
        ],
        [shape_of((n, m, width), F32), shape_of((width, m), F32)],
        index,
        [first, second],
    )


def halve_body(bit, sc, keep, got, send, nxt):
    half = send.shape[0]
    mine = jnp.bitwise_and(jnp.right_shift(sc[2], bit), 1)
    for out, side in ((send, 1 - mine), (nxt, mine)):
        rows = pl.ds(pl.multiple_of(side * half, half), half)
        out[...] = (keep[rows, :].astype(F32) + got[rows, :].astype(F32)).astype(BF16)


def halve(scalars, keep, got, bit):
    shape = shape_of((keep.shape[0] // 2, keep.shape[1]), BF16)
    return call(
        functools.partial(halve_body, bit),
        (1,),
        [full(keep.shape)] * 2,
        [pl.BlockSpec(shape.shape, lambda i, sc: (0, 0))] * 2,
        [shape] * 2,
        scalars,
        [keep, got],
    )


def join_body(added, sc, a, c, out):
    rows = a.shape[0]
    if added:
        out[...] = (a[...].astype(F32) + c[...].astype(F32)).astype(BF16)
    else:
        out[:rows, :] = a[...]
        out[rows:, :] = c[...]


def join(scalars, first, second, added):
    shape = shape_of((first.shape[0] * (1 if added else 2), first.shape[1]), BF16)
    return call(
        functools.partial(join_body, added),
        (1,),
        [full(first.shape)] * 2,
        pl.BlockSpec(shape.shape, lambda i, sc: (0, 0)),
        shape,
        scalars,
        [first, second],
    )


def place_of_largest(lens, half):
    count = lens.shape[1]
    start, border, before = jnp.int32(0), jnp.int32(0), jnp.int32(0)
    for i in range(count):
        big = lens[0, i] == half
        start = jnp.where(big, before, start)
        border = jnp.where(big, lens[0, (i + 1) % count], border)
        before = before + lens[0, i]
    return start, border


def turn_body(half, lens, here, x, *outs):
    start, border = place_of_largest(lens, half)
    rows = x.shape[0]
    turned = pltpu.roll(x[...].astype(F32), lax.rem(rows - start, rows), 0).astype(BF16)
    if len(outs) == 1:
        outs[0][...] = turned
        return
    first, second, out = outs
    first[...] = turned[:half]
    second[...] = turned[half:]
    out[0] = here[0]
    out[1] = border
    out[2] = here[1]
    out[3] = start


def turn(lengths, here, x, half, split):
    smem = pl.BlockSpec(memory_space=pltpu.SMEM)
    vmem = pl.BlockSpec(memory_space=pltpu.VMEM)
    piece = shape_of((half, x.shape[1]), BF16)
    if split:
        out_specs, out_shape = [vmem, vmem, smem], [piece, piece, shape_of((4,), jnp.int32)]
    else:
        out_specs, out_shape = [vmem], [shape_of(x.shape, BF16)]
    return pl.pallas_call(
        functools.partial(turn_body, half),
        in_specs=[smem, smem, vmem],
        out_specs=out_specs,
        out_shape=out_shape,
        compiler_params=pltpu.CompilerParams(vmem_limit_bytes=16 * MIB),
    )(lengths, here, x)


class Chain:
    def __init__(self):
        self.last = ()

    def tie(self, value, *need):
        return lax.optimization_barrier((value, need, self.last))[0]

    def do(self, fn, *args, **keywords):
        leaves, tree = jax.tree_util.tree_flatten(args)
        arrays = iter(self.tie([v for v in leaves if isinstance(v, jax.Array)]))
        leaves = [next(arrays) if isinstance(v, jax.Array) else v for v in leaves]
        out = fn(*jax.tree_util.tree_unflatten(tree, leaves), **keywords)
        self.last = jax.tree_util.tree_leaves(out)[0]
        return out


class RowSum:
    def __init__(self, chain, scalars, r, n_rows, order, pair, core_flip=None):
        self.chain, self.scalars, self.r, self.n_rows = chain, scalars, r, n_rows
        self.order, self.depth = order, len(order)
        self.rest = [b for b in range(n_rows.bit_length() - 1) if b not in order]
        send, self.keep = pair
        self.at = 0 if core_flip is None else -1
        self.got = self.flip(send, order[0]) if core_flip is None else core_flip(send)

    def flip(self, value, bit):
        return lax.ppermute(value, "rows", [(i, i ^ (1 << bit)) for i in range(self.n_rows)])

    def step(self):
        do = self.chain.do
        if self.at < self.depth:
            self.at += 1
            if self.at < self.depth:
                bit = self.order[self.at]
                send, self.keep = do(halve, self.scalars, self.keep, self.got, bit)
                self.got = self.flip(send, bit)
                return
            self.buf = do(join, self.scalars, self.keep, self.got, True)
            for b in self.rest:
                self.buf = do(join, self.scalars, self.buf, self.flip(self.buf, b), True)
            self.left = self.depth - 1
        else:
            self.left -= 1
            self.buf = do(join, self.scalars, self.buf, self.got, False)
        self.got = self.flip(self.buf, self.order[self.left])

    def finish(self, fn, *args):
        index = 0
        for b in self.order:
            index = index * 2 + jnp.bitwise_and(jnp.right_shift(self.r, b), 1)
        index = jnp.stack([index, index]).astype(jnp.int32)
        return self.chain.do(fn, index, self.buf, self.got, 1 << self.depth, *args)


def local(
    n_tp, n_rows,
    datapoints, lengths, qkv_weight, out_weight, up_weight, up_bias, down_weight, down_bias,
    gain_one, shift_one, gain_two, shift_two, grad_out,
):
    tok, width = datapoints.shape
    count = n_tp * width
    half = tok // 2
    q_scale = DH ** (-0.5)
    t, r = lax.axis_index("tp"), lax.axis_index("rows")
    chain = Chain()
    do, tie = chain.do, chain.tie

    def core_flip(v):
        return lax.ppermute(v, "tp", [(i, i ^ 1) for i in range(n_tp)])

    def x_flip(v):
        return lax.ppermute(v, "tp", [(i, i ^ 2) for i in range(n_tp)])

    def diag_flip(v):
        return lax.ppermute(v, "tp", [(i, i ^ 3) for i in range(n_tp)])

    def row_flip(v, b):
        return lax.ppermute(v, "rows", [(i, i ^ (1 << b)) for i in range(n_rows)])

    ow = lax.all_gather(out_weight, "tp", axis=0, tiled=True)
    vectors = jnp.concatenate([gain_one, shift_one, gain_two, shift_two, down_bias])
    vec_x = x_flip(vectors)
    vec_c = core_flip(jnp.concatenate([vectors, up_bias]))
    here = jnp.stack([t, r]).astype(jnp.int32)
    x0, x1, scalars = do(turn, lengths, here, datapoints, half, True)
    start = scalars[3]
    x0_x, x0_c = x_flip(x0), core_flip(x0)
    d_down_bias = do(lambda v: jnp.sum(v.astype(F32), axis=0), grad_out)
    vec_d = core_flip(tie(vec_x))
    n_vec = vectors.shape[0] // width

    def relative_vectors(*pieces):
        return jnp.stack([p[: n_vec * width].reshape(n_vec, width) for p in pieces])

    def vector_orders(rel, vec_c):
        order = jnp.bitwise_xor(t, jnp.arange(n_tp))
        bias = jnp.concatenate([up_bias, vec_c[n_vec * width :]]).reshape(1, -1)
        return jnp.transpose(rel[order], (1, 0, 2)).reshape(n_vec, count), bias

    weight4 = qkv_weight.reshape(3, n_tp, width, width)
    gains_rel = do(relative_vectors, vectors, vec_c, vec_x, vec_d)
    x0_d = core_flip(x0_x)
    x1 = tie(x1, x0_x)
    x1_x, x1_c = x_flip(x1), core_flip(x1)
    (dy,) = do(turn, lengths, here, grad_out, half, False)
    wide = tie((up_weight, down_weight), x0_x)
    up_c, down_c = core_flip(wide[0]), core_flip(wide[1])
    xs = [[x0, x0_c, x0_x, x0_d], None]
    qkv, acts, stats, mixed, lse, pieces = [[None] * 2 for _ in range(6)]

    def first(h):
        qkv[h], acts[h], stats[h], mixed[h], lse[h], other, mine = do(
            first_layer, scalars, xs[h], dy, gains_rel, weight4, h
        )
        pieces[h] = [mine, core_flip(other), x_flip(mine), diag_flip(other)]

    first(0)
    x1_d = core_flip(tie(x1_x, up_c, down_c))
    xs[1] = [x1, x1_c, x1_x, x1_d]
    first(1)
    gains, bias2 = do(vector_orders, gains_rel, vec_c)

    weights = [ow, gains, up_weight, up_c, down_weight, down_c, bias2]
    fed0 = do(feed, scalars, xs[0], pieces[0], *weights)
    db0_x = x_flip(fed0[7])
    fed1 = do(feed, scalars, xs[1], pieces[1], *weights)
    db1_x = x_flip(fed1[7])
    y_cols, b, dyn, g, du = [[fed0[k], fed1[k]] for k in (0, 3, 4, 5, 6)]
    def row_sum(order, pair, *core):
        return RowSum(chain, scalars, r, n_rows, order, pair, *core)

    def spread_rows(v):
        return [v, core_flip(v), x_flip(v), diag_flip(v)]

    dz0, sums0 = do(norm_back, scalars, fed0[8], db0_x, fed0[1], fed0[2], gains)
    dz0_x, dz0_c = x_flip(dz0), core_flip(dz0)
    up = row_sum([1, 0, 2], do(pair_grad, scalars, b, du, False), core_flip)
    db1_x = tie(db1_x, dz0_c)
    down = row_sum([0, 1, 2], do(pair_grad, scalars, g, dyn, True), core_flip)
    dz0_x = tie(dz0_x)
    dzs0 = [dz0, dz0_c, dz0_x, core_flip(dz0_x)]
    dz1, sums1 = do(norm_back, scalars, fed1[8], db1_x, fed1[1], fed1[2], gains)
    dzs1 = spread_rows(dz1)
    hidden = up_bias.shape[0]
    up.step()
    down.step()

    grads0, dzn0 = do(attend_back, scalars, dzs0, out_weight, qkv[0], lse[0], False)
    up.step()
    down.step()
    grads1, dzn1 = do(attend_back, scalars, dzs1, out_weight, qkv[1], lse[1], True)
    up.step()
    down.step()
    attn = row_sum(
        [0, 1, 2],
        do(attn_grad, scalars, acts, [dzn0, dzn1], [grads0, grads1], mixed, 0),
    )

    def middle(keep, got):
        return (keep[1].astype(F32) + got[1].astype(F32)).astype(BF16)

    def total_of(keep, got, got_x):
        return keep[0].astype(F32) + got[0].astype(F32) + got_x.astype(F32)

    send, keep_a = do(spread, scalars, [grads0, grads1], qkv_weight, n_tp, (q_scale, 1.0, 1.0))
    got_a = core_flip(send)
    up.step()
    down.step()
    out_send, out_keep = do(out_product, scalars, g, down_weight, down_c)
    da_x = x_flip(do(middle, keep_a, got_a))
    attn.step()
    up.step()
    down.step()
    bias_grad = do(jnp.add, fed0[9], fed1[9])
    attn.step()
    up.step()
    down.step()
    attn.step()
    gain_row = gain_one.reshape(1, -1)

    def joined(*parts):
        return total_of(*parts).astype(BF16)

    da = do(joined, keep_a, got_a, da_x)
    out_x = x_flip(tie(out_send))
    m0, ones0 = do(norm_sums, scalars, da[:half], x0, stats[0], gain_row)
    m1, ones1 = do(norm_sums, scalars, da[half:], x1, stats[1], gain_row)
    m = do(lambda a, b, *c: jnp.concatenate([a + b, *c], 0), sums0, sums1, m0, m1)
    m_c = core_flip(m)
    bias_got = core_flip(bias_grad[:, hidden:])
    attn.step()
    m = do(jnp.add, m, m_c)
    m_x = x_flip(m)
    d_up = up.finish(place, width)
    d_down = down.finish(place, width)
    c, side = jnp.bitwise_and(t, 1), jnp.right_shift(t, 1)

    def output_rows(keep, got, y0, y1, vecs):
        wide = 2 * width
        extra = lax.dynamic_slice_in_dim(vecs[4], side * wide, wide, 0)
        total = keep.astype(F32) + got.astype(F32) + jnp.concatenate([y0, y1], 0) + extra
        low = total.astype(BF16)
        return (
            lax.dynamic_slice_in_dim(low, (1 - c) * width, width, 1),
            lax.dynamic_slice_in_dim(low, c * width, width, 1),
        )

    rows_send, rows_keep = do(output_rows, out_keep, out_x, *y_cols, gains)
    rows_got = core_flip(rows_send)

    def unroll(first, second):
        thrice = jnp.concatenate([second, first, second], 0)
        return lax.dynamic_slice_in_dim(thrice, half - start, tok, 0)

    def output_of(mine, other):
        part = half // 2
        halves = []
        for h in range(2):
            a, b = mine[h * part : (h + 1) * part], other[h * part : (h + 1) * part]
            halves.append(
                jnp.where(c == 0, jnp.concatenate([a, b], 0), jnp.concatenate([b, a], 0))
            )
        return unroll(*halves)

    m = do(jnp.add, m, m_x)

    def small_of(up_b, down_b, m, ones0, ones1):
        two = lax.dynamic_slice_in_dim(m[:2], t * width, width, 1)
        return jnp.concatenate(
            [up_b.reshape(-1), down_b, (ones0 + ones1).reshape(-1), two.reshape(-1)]
        ).reshape(-1, 128)

    d_up_bias = bias_grad[:, :hidden] + bias_got
    small = do(small_of, d_up_bias, d_down_bias, m, ones0, ones1)
    bits = list(range(n_rows.bit_length() - 1))
    small_got = row_flip(small, bits[0])

    def d_input_of(m, da, *parts):
        halves = []
        for h, (x, stat, dzn) in enumerate((parts[:3], parts[3:])):
            nhat = (x.astype(F32) - stat[:, 0:1]) * stat[:, 1:2]
            first, second = m[2 + 2 * h][:, None] / count, m[3 + 2 * h][:, None] / count
            dz = lax.dynamic_slice_in_dim(dzn, t * width, width, 1).astype(F32)
            n = da[h * half : (h + 1) * half].astype(F32) * gain_one
            halves.append(dz + stat[:, 1:2] * (n - first - nhat * second))
        return unroll(*halves)

    attn.step()
    small = do(jnp.add, small, small_got)
    small_got = row_flip(small, bits[1])
    d_input = do(d_input_of, m, da, x0, stats[0], dzn0, x1, stats[1], dzn1)
    for bit in bits[2:]:
        small = do(jnp.add, small, small_got)
        small_got = row_flip(small, bit)
    output = do(output_of, rows_keep, rows_got)
    small = do(jnp.add, small, small_got).reshape(-1)
    d_qkv, d_out = attn.finish(unpack, width, q_scale)
    d_down_bias, d_gain_one, d_shift_one, d_gain_two, d_shift_two = small[hidden:].reshape(5, width)
    return (
        output, d_input, d_qkv, d_out, d_up, small[:hidden],
        d_down, d_down_bias, d_gain_one, d_shift_one, d_gain_two, d_shift_two,
    )


def solution(mesh):
    grid = P("rows", "tp")
    placed = (
        grid, P("rows", None), P(None, None, "tp"), P("tp", None), P(None, "tp"), P("tp"),
        P("tp", None), P("tp"), P("tp"), P("tp"), P("tp"), P("tp"), grid,
    )
    return jax.shard_map(
        functools.partial(local, mesh.shape["tp"], mesh.shape["rows"]),
        mesh=mesh,
        in_specs=placed,
        out_specs=(
            grid, grid, P(None, None, "tp"), P("tp", None), P(None, "tp"), P("tp"),
            P("tp", None), P("tp"), P("tp"), P("tp"), P("tp"), P("tp"),
        ),
        check_vma=False,
    )
```
